32 devices in a mesh: row: 8 (over z, y), col: 4 (over x, core).
Axes of the slice: x: 2, y: 2, z: 4, core: 2. Of those that a mesh axis runs over, the one named last changes fastest.
Arguments:
- tokens: bfloat16 [8192, 768], P(('row', 'col')), may hold values from -6 to 6
- norm1_gain: float32 [768], replicated, may hold values from 0.5 to 1.5
- norm1_bias: float32 [768], replicated, may hold values from -1.25 to 1.25
- w_query: bfloat16 [768, 768], replicated, may hold values from -0.3125 to 0.3125
- b_query: float32 [768], replicated, may hold values from -1.25 to 1.25
- w_key: bfloat16 [768, 768], replicated, may hold values from -0.3125 to 0.3125
- w_value: bfloat16 [768, 768], replicated, may hold values from -0.21875 to 0.21875
- b_value: float32 [768], replicated, may hold values from -1.25 to 1.25
- w_out: bfloat16 [768, 768], replicated, may hold values from -1.75 to 1.75
- b_out: float32 [768], replicated, may hold values from -1.25 to 1.25
- norm2_gain: float32 [768], replicated, may hold values from 0.5 to 1.5
- norm2_bias: float32 [768], replicated, may hold values from -1.25 to 1.25
- w_up: bfloat16 [768, 3072], replicated, may hold values from -0.21875 to 0.21875
- b_up: float32 [3072], replicated, may hold values from -1.25 to 1.25
- w_down: bfloat16 [3072, 768], replicated, may hold values from -0.109375 to 0.109375
- b_down: float32 [768], replicated, may hold values from -1.25 to 1.25
- slide_padded_units: int32 [8], replicated, may hold values from 1 to 21, 32 in all
- padding_shortfall: int32 [8], replicated, may hold values from 0 to 255
- cotangent: bfloat16 [8192, 768], P(('row', 'col')), may hold values from -6 to 6
Outputs:
- output: bfloat16 [8192, 768], P(('row', 'col'))
- grad_tokens: float32 [8192, 768], P(('row', 'col'))
- grad_norm1_gain: float32 [768], P('row')
- grad_norm1_bias: float32 [768], P('row')
- grad_w_query: float32 [768, 768], P('row')
- grad_b_query: float32 [768], P('row')
- grad_w_key: float32 [768, 768], P('row')
- grad_w_value: float32 [768, 768], P('row')
- grad_b_value: float32 [768], P('row')
- grad_w_out: float32 [768, 768], P('row')
- grad_b_out: float32 [768], P('row')
- grad_norm2_gain: float32 [768], P('row')
- grad_norm2_bias: float32 [768], P('row')
- grad_w_up: float32 [768, 3072], P('row')
- grad_b_up: float32 [3072], P('row')
- grad_w_down: float32 [3072, 768], P('row')
- grad_b_down: float32 [768], P('row')
The draws below stay inside these ranges and needn't reach their ends.
Inputs may be any that keep to these rules, and one draw needn't show every extreme that they name: The slides fill the sequence exactly: the slide_padded_units add up to 32, and the largest is 21. `padding_shortfall`: fewer than 256 padding tiles a slide.
All inputs are finite; a program needn't handle non-finite values.
Results may differ from the reference program's by a relative error of at most 0.017.
Values may be sent and summed in bfloat16 or wider, within the bound.
A program may use at most 256 MiB of HBM per device.

```python
import math
import jax
import jax.numpy as jnp
import numpy as np
from jax import lax

D = 768
ATTENTION_HEADS = 16
HEAD_DIM = 48
FF = 3072
DILATION_STRIDE = 16
PAD = 256
SLIDES = 8
TOKENS = 8192
SEGMENT = 1024
SPARSE_HEAD_KEYS = 512


def set_ends(drawn, key, least, top_value):
    longest = drawn.shape.index(max(drawn.shape))
    spots = []
    for shift in (0, 1):
        where = [jax.random.randint(jax.random.fold_in(key, axis), (), 0, length) for axis, length in enumerate(drawn.shape)]
        where[longest] = (where[longest] + shift) % drawn.shape[longest]
        spots.append(tuple(where))
    return drawn.at[spots[0]].set(least).at[spots[1]].set(top_value)


def steps_of(stream_key, shape, cuts, least, largest):
    def one(dim, shards_of):
        draws = jax.random.uniform(jax.random.fold_in(jax.random.fold_in(stream_key, 6), dim), (shards_of,), jnp.float32, least / len(cuts), largest / len(cuts))
        return jnp.repeat(jnp.exp(draws), shape[dim] // shards_of).reshape((-1,) + (1,) * (len(shape) - dim - 1))

    loudness = one(*cuts[0])
    for cut in cuts[1:]:
        loudness = loudness * one(*cut)
    return loudness


def split_up(amount, total, bound, slope):
    weights = [(1 << 20) // math.isqrt(rank ** slope) + 1 for rank in range(2, amount + 1)]
    surplus, holding = total - bound - (amount - 1), [1] * (amount - 1)
    while surplus > 0:
        movable = [i for i in range(amount - 1) if holding[i] < bound]
        mass, left = sum([weights[i] for i in movable]), surplus
        for i in movable:
            addition = min(bound - holding[i], max(1, left * weights[i] // mass), surplus)
            holding[i] = holding[i] + addition
            surplus = surplus - addition
    return np.array([bound] + holding)


def uneven_parts(key, number_of, total, reach, lean):
    if number_of == 2:
        one = jax.random.randint(key, (), max(1, total - reach), min(reach, total - 1) + 1)
        return jnp.stack([one, total - one])
    sizes = jnp.asarray(split_up(number_of, total, reach, lean), jnp.int32)
    pairs = (number_of - 1) // 2
    giver, taker = sizes[1:1 + 2 * pairs:2], sizes[2:2 + 2 * pairs:2]
    room = jnp.minimum(giver - 1, reach - taker)
    moved = jax.random.randint(jax.random.fold_in(key, 1), (pairs,), 0, 1 << 20) % (room + 1)
    sizes = sizes.at[1:1 + 2 * pairs:2].set(giver - moved).at[2:2 + 2 * pairs:2].set(taker + moved)
    return sizes[jax.random.permutation(jax.random.fold_in(key, 2), number_of)]


def gaussian(own_key, shape, deviation, reach, shards=(), kind=jnp.bfloat16):
    array = jax.random.normal(own_key, shape, jnp.float32) * deviation
    if len(shards) > 0:
        array = steps_of(own_key, shape, shards, -0.22, 0.18) * array
    return jnp.clip(array, min=-reach, max=reach).astype(kind)


def setup_inputs(seed: int = 0) -> dict:
    streams_of = jax.random.split(jax.random.key(seed), 20)
    return {
        "tokens": gaussian(streams_of[0], (TOKENS, D), 1.0, 6.0, ((0, 32),)),
        "norm1_gain": jnp.clip(1.0 + 0.1 * jax.random.normal(streams_of[1], (D,), jnp.float32), 0.5, 1.5),
        "norm1_bias": gaussian(streams_of[2], (D,), 0.2, 1.25, (), jnp.float32),
        "w_query": gaussian(streams_of[3], (D, D), (D // 2) ** -0.5, 0.3125),
        "b_query": gaussian(streams_of[4], (D,), 0.2, 1.25, (), jnp.float32),
        "w_key": gaussian(streams_of[5], (D, D), (D // 2) ** -0.5, 0.3125),
        "w_value": gaussian(streams_of[6], (D, D), D ** -0.5, 0.21875),
        "b_value": gaussian(streams_of[7], (D,), 0.2, 1.25, (), jnp.float32),
        "w_out": gaussian(streams_of[8], (D, D), (D // 64) ** -0.5, 1.75),
        "b_out": gaussian(streams_of[9], (D,), 0.2, 1.25, (), jnp.float32),
        "norm2_gain": jnp.clip(1.0 + 0.1 * jax.random.normal(streams_of[10], (D,), jnp.float32), 0.5, 1.5),
        "norm2_bias": gaussian(streams_of[11], (D,), 0.2, 1.25, (), jnp.float32),
        "w_up": gaussian(streams_of[12], (D, FF), D ** -0.5, 0.21875),
        "b_up": gaussian(streams_of[13], (FF,), 0.2, 1.25, (), jnp.float32),
        "w_down": gaussian(streams_of[14], (FF, D), FF ** -0.5, 0.109375),
        "b_down": gaussian(streams_of[15], (D,), 0.2, 1.25, (), jnp.float32),
        "slide_padded_units": uneven_parts(streams_of[16], SLIDES, TOKENS // PAD, 2 * (TOKENS // PAD) // 3, 2).astype(jnp.int32),
        "padding_shortfall": set_ends(jax.random.randint(streams_of[17], (SLIDES,), 0, PAD), jax.random.fold_in(streams_of[17], 1), 0, PAD - 1).astype(jnp.int32),
        "cotangent": gaussian(streams_of[18], (TOKENS, D), 1.0, 6.0, ((0, 32),)),
    }


@jax.custom_vjp
def low(v):
    return lax.optimization_barrier(v.astype(jnp.bfloat16)).astype(jnp.float32)

@jax.custom_vjp
def lower_backward(v):
    return v

def low_keep(v):
    return (low(v), None)

def low_pass(kept, grad):
    return (grad,)

def back_keep(v):
    return (v, None)

def back_low(kept, grad):
    return (low(grad),)
low.defvjp(low_keep, low_pass)
lower_backward.defvjp(back_keep, back_low)
EPS = 1e-05
NEG = -1e+30

def matmul_high(left, right):
    return jnp.dot(left, right, precision=lax.Precision.HIGHEST, preferred_element_type=jnp.float32)

def layer_norm(values, norm_gain, norm_bias):
    row_mean = lax.optimization_barrier(jnp.mean(values, axis=-1, keepdims=True))
    centred = values - row_mean
    inverse = lax.rsqrt(lax.optimization_barrier(jnp.mean(centred * centred, axis=-1, keepdims=True)) + EPS)
    return centred * inverse * norm_gain + norm_bias

def slide_lookup_tables(slide_padded_units, padding_shortfall, positions):
    slide_ends = jnp.cumsum(slide_padded_units, dtype=jnp.int32) * PAD
    slide_starts = slide_ends - slide_padded_units * PAD
    inside = (positions[:, None] >= slide_starts[None, :]) & (positions[:, None] < slide_ends[None, :])
    numbers = jnp.arange(slide_padded_units.shape[0], dtype=jnp.int32)
    labels = lax.optimization_barrier(jnp.sum(jnp.where(inside, numbers[None, :], 0), axis=1, dtype=jnp.int32))
    limits = lax.optimization_barrier(jnp.sum(jnp.where(inside, (slide_ends - padding_shortfall)[None, :], 0), axis=1, dtype=jnp.int32))
    return (labels, positions < limits)

def permitted_mask(query_positions, query_labels, key_pos, key_lab, key_valid):
    return (query_labels == key_lab) & key_valid | (query_positions == key_pos)

def log_total(scores):
    row_top = lax.optimization_barrier(jnp.max(scores, axis=-1, keepdims=True))
    return row_top[..., 0] + jnp.log(lax.optimization_barrier(jnp.sum(jnp.exp(scores - row_top), axis=-1)))

def pick_rows(softmax_statistics, selector_portion):
    sparse_extent = selector_portion.shape[0]
    reshaped_tensor = softmax_statistics.reshape(softmax_statistics.shape[0], softmax_statistics.shape[1] // sparse_extent, sparse_extent)
    return lax.optimization_barrier(jnp.sum(reshaped_tensor * selector_portion.T[:, None, :], axis=-1))

def merge_stats(first_total, total_b, selector_portion, chooser_bool):
    sparse_extent = selector_portion.shape[0]
    joint = jnp.logaddexp(pick_rows(first_total, selector_portion), total_b)
    reshaped_tensor = first_total.reshape(first_total.shape[0], first_total.shape[1] // sparse_extent, sparse_extent)
    full = jnp.where(chooser_bool.T[:, None, :], joint[:, :, None], reshaped_tensor).reshape(first_total.shape)
    return (joint, full)

def reference(tokens, norm1_gain, norm1_bias, w_query, b_query, w_key, w_value, b_value, w_out, b_out, norm2_gain, norm2_bias, w_up, b_up, w_down, b_down, slide_padded_units, padding_shortfall, cotangent):
    maximum_precision = lax.Precision.HIGHEST
    positions = jnp.arange(TOKENS, dtype=jnp.int32)
    labels, valid = slide_lookup_tables(slide_padded_units, padding_shortfall, positions)
    head_remainder = jnp.arange(ATTENTION_HEADS, dtype=jnp.int32) % DILATION_STRIDE
    head_index = np.arange(ATTENTION_HEADS) % DILATION_STRIDE
    chooser_bool = head_remainder[None, :] == jnp.arange(DILATION_STRIDE, dtype=jnp.int32)[:, None]
    selector_float = chooser_bool.astype(jnp.float32)
    sparse_positions = DILATION_STRIDE * jnp.arange(SPARSE_HEAD_KEYS, dtype=jnp.int32)[:, None] + head_remainder[None, :]
    sparse_labels, sparse_validity = slide_lookup_tables(slide_padded_units, padding_shortfall, sparse_positions.reshape(-1))
    sparse_labels = sparse_labels.reshape(SPARSE_HEAD_KEYS, ATTENTION_HEADS)
    sparse_validity = sparse_validity.reshape(SPARSE_HEAD_KEYS, ATTENTION_HEADS)
    seg_count = TOKENS // SEGMENT
    seg_sel = SEGMENT // DILATION_STRIDE
    score_scaling = HEAD_DIM ** (-0.5)

    def select_heads(row_entries):
        reshaped_tensor = row_entries.reshape(row_entries.shape[0] // DILATION_STRIDE, DILATION_STRIDE, ATTENTION_HEADS, HEAD_DIM)
        return jnp.einsum('trhd,rh->thd', reshaped_tensor, selector_float, precision=maximum_precision)

    def attention(query_rows, key_row_matrix, value_row_matrix):
        key_sparse = select_heads(key_row_matrix)
        value_sparse = select_heads(value_row_matrix)

        def segment_fn(pieces):
            query_segment, key_seg, value_seg, lab_seg, valid_seg, pos_seg = pieces
            query_three = query_segment.reshape(SEGMENT, ATTENTION_HEADS, HEAD_DIM)
            key_three = key_seg.reshape(SEGMENT, ATTENTION_HEADS, HEAD_DIM)
            value_three = value_seg.reshape(SEGMENT, ATTENTION_HEADS, HEAD_DIM)
            scores_a = lower_backward(jnp.einsum('ihd,jhd->hij', query_three, key_three, precision=maximum_precision) * score_scaling)
            allow_a = permitted_mask(pos_seg[:, None], lab_seg[:, None], pos_seg[None, :], lab_seg[None, :], valid_seg[None, :])
            scores_a = jnp.where(allow_a[None], scores_a, NEG)
            query_sparse = select_heads(query_segment)
            query_positions = pos_seg.reshape(seg_sel, DILATION_STRIDE)[:, head_index]
            query_labels = lab_seg.reshape(seg_sel, DILATION_STRIDE)[:, head_index]
            second_allow_mask = permitted_mask(query_positions.T[:, :, None], query_labels.T[:, :, None], sparse_positions.T[:, None, :], sparse_labels.T[:, None, :], sparse_validity.T[:, None, :])
            second_scores = lower_backward(jnp.einsum('sye,fye->ysf', query_sparse, key_sparse, precision=maximum_precision) * score_scaling)
            second_scores = jnp.where(second_allow_mask, second_scores, NEG)
            joint, full = merge_stats(log_total(scores_a), log_total(second_scores), selector_float, chooser_bool)
            weights_a = low(jnp.exp(scores_a - full[:, :, None]))
            second_weights = low(jnp.exp(second_scores - joint[:, :, None]))
            out_a = jnp.einsum('hij,jhd->ihd', weights_a, value_three, precision=maximum_precision)
            second_output = jnp.einsum('yxp,pyf->xyf', second_weights, value_sparse, precision=maximum_precision)
            grown_rows = (second_output[:, None] * selector_float[None, :, :, None]).reshape(SEGMENT, ATTENTION_HEADS, HEAD_DIM)
            return (out_a + grown_rows).reshape(SEGMENT, D)
        pieces = (query_rows.reshape(seg_count, SEGMENT, D), key_row_matrix.reshape(seg_count, SEGMENT, D), value_row_matrix.reshape(seg_count, SEGMENT, D), labels.reshape(seg_count, SEGMENT), valid.reshape(seg_count, SEGMENT), positions.reshape(seg_count, SEGMENT))
        return lax.map(jax.checkpoint(segment_fn), pieces).reshape(TOKENS, D)

    def forward(x_rows, gain_one, bias_one, q_weight, q_bias, k_weight, v_weight, v_bias, o_weight, o_bias, gain_two, bias_two, up_weight, up_bias, down_weight, down_bias):
        a_one = low(layer_norm(x_rows, gain_one, bias_one))
        query_rows = lower_backward(low(matmul_high(a_one, q_weight) + q_bias))
        key_row_matrix = lower_backward(low(matmul_high(a_one, k_weight)))
        value_row_matrix = lower_backward(low(matmul_high(a_one, v_weight) + v_bias))
        attended = lower_backward(low(attention(query_rows, key_row_matrix, value_row_matrix)))
        branch = lower_backward(matmul_high(attended, o_weight) + o_bias)
        y_one = x_rows + branch
        a_two = low(layer_norm(y_one, gain_two, bias_two))

        def mlp_block(row_entries):
            up_rows = lower_backward(matmul_high(row_entries, up_weight) + up_bias)
            hidden = low(jax.nn.gelu(up_rows, approximate=False))
            return matmul_high(hidden, down_weight) + down_bias
        mlp_out = lax.map(jax.checkpoint(mlp_block), a_two.reshape(seg_count, SEGMENT, D)).reshape(TOKENS, D)
        return y_one + mlp_out
    params = tuple((item.astype(jnp.float32) for item in (norm1_gain, norm1_bias, w_query, b_query, w_key, w_value, b_value, w_out, b_out, norm2_gain, norm2_bias, w_up, b_up, w_down, b_down)))
    result, backward = jax.vjp(forward, tokens.astype(jnp.float32), *params)
    grads = backward(cotangent.astype(jnp.float32))
    return (result.astype(jnp.bfloat16), grads[0], grads[1], grads[2], grads[3], grads[4], grads[5], grads[6], grads[7], grads[8], grads[9], grads[10], grads[11], grads[12], grads[13], grads[14], grads[15])
```

```python
import functools

import jax
import jax.numpy as jnp
from jax import lax
from jax.experimental import pallas as pl
from jax.experimental.pallas import tpu as pltpu
from jax.sharding import PartitionSpec as P

HEADS = 16
HEAD_DIM = 48
SLOT = 64
STRIDE = 16
PAD = 256
COLS = 4
LOCAL_HEADS = HEADS // COLS
EPS = 1e-05
NEG = -1e30
SCALE = HEAD_DIM**-0.5
SCALE2 = SCALE * 1.4426950408889634
MESH = pl.DeviceIdType.MESH
BF16 = jnp.bfloat16
F32 = jnp.float32
UNITS = (768, 768, 256, 640)
OFFSETS = (0, 768, 1536, 1792)
WIDTH = 2432


def nn(left, right):
    return jnp.dot(left, right, preferred_element_type=F32)


def nt(left, right):
    return lax.dot_general(left, right, (((1,), (1,)), ((), ())), preferred_element_type=F32)


def tn(left, right):
    return lax.dot_general(left, right, (((0,), (0,)), ((), ())), preferred_element_type=F32)


def iota(shape, dim):
    return lax.broadcasted_iota(jnp.int32, shape, dim)


def onehot(test):
    return jnp.where(test, 1.0, 0.0).astype(BF16)


def moved(values, chooser, parts=3):
    total = None
    for i in range(parts):
        low = values.astype(BF16)
        term = nn(low, chooser)
        total = term if total is None else total + term
        if i < parts - 1:
            values = values - low.astype(F32)
    return total


def normalise(x):
    centred = x - jnp.mean(x, axis=-1, keepdims=True)
    inverse = lax.rsqrt(jnp.mean(centred * centred, axis=-1, keepdims=True) + EPS)
    return centred * inverse, inverse


def norm_back(grad, unit, inverse, gain):
    scaled = grad * gain
    mean_one = jnp.mean(scaled, axis=-1, keepdims=True)
    mean_two = jnp.mean(scaled * unit, axis=-1, keepdims=True)
    return inverse * (scaled - mean_one - unit * mean_two)


def gelu_parts(u):
    z = jnp.abs(u) * 0.7071067811865476
    e = jnp.exp(-z * z)
    t = 1.0 / (1.0 + 0.3275911 * z)
    poly = t * (0.254829592 + t * (-0.284496736 + t * (1.421413741 + t * (-1.453152027 + t * 1.061405429))))
    tail = 0.5 * poly * e
    phi = jnp.where(u >= 0, 1.0 - tail, tail)
    return u * phi, phi + u * e * 0.3989422804014327


def colsum(x):
    return jnp.sum(x, axis=0, keepdims=True)


def layer(
    rows_n, slides_n, stop,
    slide_units, shortfall, par, tok_h, cot_h, wq_h, wk_h, wv_h, wo_h, wup_h, wdn_h, wdq_h,
    out_h, gt_h, gath_h, vec_h, p_h,
    wup, wdn, wqkv, wupq, wdq, wop,
    tok, gb, a1, a2, drb,
    qf, qrow, kaug, vaug, qtm, kt, vta, sdr,
    pbuf, sref, dsb, oa, att,
    y1, acc, da2, dqt, dqr,
    slab0, slab1, slab2, ra0, ra1, ra2, ra3, rb0, rb1, rb2, rb3, gath,
    kvs, qsel, wb, dqb, dkvr,
    vec, vpair, vrow, vcol, bupq, bqkv,
    lsem, gss, gsr, sps, spr, bss, bsr, u1s, u1r, u2s, u2r, ucs, ucr, ats, atr, vss, vsr, vcs, vcr, psem,
):
    row_a = rows_n // 2
    share = 768 // rows_n
    r = lax.axis_index("row")
    c = lax.axis_index("col")
    sib = c + 1 - 2 * (c % 2)
    across = (c + 2) % COLS
    diag = (sib + 2) % COLS
    ra, rbit = r // 2, r % 2
    recv_a, recv_b = (ra0, ra1, ra2, ra3), (rb0, rb1, rb2, rb3)
    slabs = (slab0, slab1, slab2, slab0.at[:, :, :, pl.ds(0, UNITS[3])])
    key_count = rows_n * 64

    def local(src, dst, i):
        return pltpu.make_async_copy(src, dst, lsem.at[i])

    in_tok = local(tok_h, tok.at[c], 0)
    in_cot = local(cot_h, gb.at[c], 1)
    in_qkv = [local(h, wup.at[:, pl.ds(768 * i, 768)], 2 + i) for i, h in enumerate((wq_h, wk_h, wv_h))]
    in_up = local(wup_h, wup, 5)
    in_dn = local(wdn_h, wdn, 6)
    in_dq = local(wdq_h, wdq, 7)
    in_wo = [
        local(wo_h.at[pl.ds(192 * s + 48 * h, 48), :], wop.at[s, pl.ds(64 * h, 48), :], 8 + 4 * s + h)
        for s in range(4)
        for h in range(4)
    ]
    in_tok.start()
    in_cot.start()
    for d in in_qkv:
        d.start()

    bar = pltpu.get_barrier_semaphore()
    for j in range(1, COLS):
        pl.semaphore_signal(bar, inc=1, device_id=(r, (c + j) % COLS), device_id_type=MESH)

    def greet(j, carry):
        pl.semaphore_signal(bar, inc=1, device_id=((r + j) % rows_n, c), device_id_type=MESH)
        return carry

    lax.fori_loop(1, rows_n, greet, 0)
    in_dq.start()
    for d in in_wo:
        d.start()
    in_dn.start()
    pl.semaphore_wait(bar, COLS - 1 + rows_n - 1)

    def remote(src, dst, send, recv, dev):
        return pltpu.make_async_remote_copy(
            src_ref=src, dst_ref=dst, send_sem=send, recv_sem=recv, device_id=dev, device_id_type=MESH
        )

    class Gather:
        def __init__(self, n, slot):
            self.near = remote(slot(c), slot(c), gss.at[n, 0], gsr.at[n, 0], (r, sib))
            self.far = remote(slot(c), slot(c), gss.at[n, 1], gsr.at[n, 1], (r, across))
            self.hand = remote(slot(across), slot(across), gss.at[n, 2], gsr.at[n, 2], (r, sib))

        def start(self):
            self.far.start()
            self.near.start()

        def forward(self):
            self.far.wait_recv()
            self.hand.start()

        def drain(self):
            self.near.wait_send()
            self.far.wait_send()
            self.hand.wait_send()

    g_tok = Gather(0, lambda i: tok.at[i])
    g_cot = Gather(1, lambda i: gb.at[i])
    g_att = [Gather(2 + p, lambda i, p=p: att.at[i, p]) for p in range(2)]
    g_dr = Gather(4, lambda i: drb.at[i])

    in_tok.wait()
    g_tok.start()
    in_cot.wait()
    g_cot.start()

    ends, lims = [], []
    total = jnp.int32(0)
    for s in range(slides_n):
        total = total + slide_units[s] * PAD
        ends.append(total)
        lims.append(total - shortfall[s])

    def label_of(pos):
        lab = jnp.zeros(pos.shape, jnp.int32)
        for s in range(slides_n - 1):
            lab = lab + jnp.where(pos >= ends[s], 1, 0)
        return lab

    def code_of(pos):
        code = label_of(pos)
        for s in range(slides_n):
            code = jnp.where((pos >= lims[s]) & (pos < ends[s]), -1, code)
        return code

    seg_first = r * 1024

    vec[...] = jnp.zeros(vec.shape, F32)
    for s in range(4):
        for h in range(4):
            wop[s, 64 * h + 48 : 64 * h + 64, :] = jnp.zeros((16, 768), BF16)
    sel_f, sel_j = iota((768, 256), 0), iota((768, 256), 1)
    head_sel = onehot((sel_f == 192 * c + 48 * (sel_j >> 6) + (sel_j & 63)) & ((sel_j & 63) < 48))
    for i, d in enumerate(in_qkv):
        d.wait()
        wqkv[:, 256 * i : 256 * i + 256] = nn(wup[:, 768 * i : 768 * i + 768], head_sel).astype(BF16)
    in_up.start()
    bqkv[...] = jnp.zeros(bqkv.shape, F32)
    biases = moved(par[0:8, :], head_sel)
    bqkv[0:1, 0:256] = biases[2:3]
    bqkv[0:1, 512:768] = biases[3:4]

    def qkv_block(b):
        x = tok[b].astype(F32)
        unit, _ = normalise(x)
        low = (unit * par[0:1, :] + par[1:2, :]).astype(BF16)
        a1[b] = low
        y = (nn(low, wqkv[...]) + bqkv[0:1, :]).astype(BF16).astype(F32)
        at = pl.ds(pl.multiple_of(256 * b, 256), 256)
        for i in range(6):
            qf[i, at, :] = y[:, 128 * i : 128 * i + 128]
        lane = iota((256, 128), 1) & 63
        key_code = code_of(seg_first + 256 * b + iota((256, 128), 0))
        key_mark = jnp.where(key_code == lane - 48, 0.0, NEG)
        marked = (lane >= 48) & (lane < 48 + slides_n)
        for p in range(2):
            qrow[p, at, :] = y[:, 128 * p : 128 * p + 128].astype(BF16)
            kaug[p, at, :] = jnp.where(marked, key_mark, y[:, 256 + 128 * p : 384 + 128 * p]).astype(BF16)
            vaug[p, at, :] = jnp.where(
                (lane == 48) | (lane == 49), 1.0, y[:, 512 + 128 * p : 640 + 128 * p]
            ).astype(BF16)
        qt, ktv, vt = y[:, :256].T, y[:, 256:512].T, y[:, 512:].T
        row = iota((128, 256), 0)
        query_label = label_of(seg_first + 256 * b + iota((128, 256), 1))
        mark = jnp.where(query_label == (row & 63) - 48, 1.0, 0.0)
        for h in range(4):
            p, half = h // 2, h % 2
            own = (row >> 6) == half
            full = jnp.where((row & 63) < 48, qt[128 * p : 128 * p + 128], mark)
            qtm[h, b] = jnp.where(own, full, 0.0).astype(BF16)
            hq, hk, hv = (m[64 * h : 64 * h + 64] for m in (qt, ktv, vt))
            kt[h, b] = hk.astype(BF16)
            vta[h, b] = jnp.where(iota((64, 256), 0) == 48, 1.0, hv).astype(BF16)
            sdr[h, b] = jnp.broadcast_to(colsum(hq * hk) * SCALE2, (8, 256))

    qkv_block(c)
    g_tok.near.wait_recv()
    qkv_block(sib)
    g_tok.forward()
    qkv_block(across)

    in_up.wait()
    for n in range(3):
        lo = (4 * share * ((256 * n) // share)) // 128 * 128
        hi = -(-(4 * share * ((256 * n + 255) // share + 1)) // 128) * 128
        o = 256 * n + iota((hi - lo, 256), 1)
        group = jnp.zeros_like(o)
        for t in range(1, rows_n):
            group = group + jnp.where(o >= share * t, 1, 0)
        unit_sel = onehot(lo + iota((hi - lo, 256), 0) == 3 * share * group + share * c + o)
        for m in range(3):
            wupq[256 * m : 256 * m + 256, 256 * n : 256 * n + 256] = nn(
                wup[256 * m : 256 * m + 256, lo:hi], unit_sel
            ).astype(BF16)
        pieces = [par[8 + t : 9 + t, :] for t in range(4)]
        line = jnp.concatenate(pieces, axis=1)[:, lo:hi]
        bupq[0:8, 256 * n : 256 * n + 256] = moved(jnp.broadcast_to(line, (8, hi - lo)), unit_sel)

    g_tok.hand.wait_recv()
    qkv_block(diag)
    g_cot.forward()

    half_lane = iota((64, 128), 1) < 64

    def picked(i, h):
        return qf[i, pl.ds(LOCAL_HEADS * c + h, 64, stride=STRIDE), :]

    for i in range(4):
        p = i % 2
        kvs[r, :, 128 * i : 128 * i + 128] = jnp.where(
            half_lane, picked(2 + i, 2 * p), picked(2 + i, 2 * p + 1)
        ).astype(BF16)
    for h in range(4):
        own = (iota((64, 128), 1) >> 6) == h % 2
        qsel[h] = jnp.where(own, picked(h // 2, h), 0.0).astype(BF16)

    def sparse_copy(j):
        return remote(kvs.at[r], kvs.at[r], sps.at[j - 1], spr.at[j - 1], ((r + j) % rows_n, c))

    def each_row(fn):
        def step(j, carry):
            fn(j)
            return carry

        lax.fori_loop(1, rows_n, step, 0)

    each_row(lambda j: sparse_copy(j).start())

    eye = iota((256, 256), 0) == iota((256, 256), 1)

    def weights_out(i):
        return pltpu.make_async_copy(pbuf.at[i % 2], p_h.at[i], psem.at[i % 2])

    def forward_tile(i):
        h, ib = i // 4, i % 4
        p, half = h // 2, h % 2
        slot = i % 2
        rhs = qtm[h, ib]
        top = jnp.full((8, 256), NEG * 10, F32)
        for jb in range(4):
            s = nn(kaug[p, 256 * jb : 256 * jb + 256, :], rhs) * SCALE2
            sref[256 * jb : 256 * jb + 256, :] = s
            top = jnp.maximum(top, jnp.max(s.reshape(32, 8, 256), axis=0))
        own = sdr[h, ib]
        top = jnp.max(jnp.maximum(top, own), axis=0, keepdims=True)
        at = pl.ds(pl.multiple_of(256 * ib, 256), 256)
        sref[at, :] = jnp.where(eye, own[0:1], sref[at, :])

        @pl.when(i >= 2)
        def _():
            weights_out(i).wait()

        for jb in range(4):
            pbuf[slot, 256 * jb : 256 * jb + 256, :] = jnp.exp2(
                sref[256 * jb : 256 * jb + 256, :] - top
            ).astype(BF16)
        weights_out(i).start()
        values = jnp.concatenate([vta[h, jb] for jb in range(4)], axis=1)
        o = nn(values, pbuf[slot])
        z = o[48:49]
        inverse = 1.0 / z
        line = iota((64, 256), 0)
        o = o * inverse
        o = jnp.where(line == 48, inverse, jnp.where(line == 49, top, jnp.where(line == 50, z, o)))
        dqt[half, ib] = o

    def branch_b(h):
        p, half = h // 2, h % 2
        lane = iota((64, 128), 1)
        k2 = kvs[:, :, 128 * p : 128 * p + 128].reshape(key_count, 128)
        v2 = kvs[:, :, 256 + 128 * p : 384 + 128 * p].reshape(key_count, 128)
        s = nt(qsel[h], k2) * SCALE2
        first = LOCAL_HEADS * c + h
        qpos = seg_first + STRIDE * iota((64, 128), 0)[:, 0:1] + first
        kpos = STRIDE * iota((8, key_count), 1)[0:1] + first
        s = jnp.where((label_of(qpos) == code_of(kpos)) | (qpos == kpos), s, NEG)
        top_b = jnp.max(s, axis=1, keepdims=True)
        e = jnp.exp2(s - top_b)
        z_b = jnp.sum(e, axis=1, keepdims=True)
        o_b = nn(e.astype(BF16), v2)
        at = pl.ds(first, 64, stride=STRIDE)
        old = oa[p, at, :]
        top_a = old[:, 64 * half + 49 : 64 * half + 50]
        z_a = old[:, 64 * half + 50 : 64 * half + 51]
        top = jnp.maximum(top_a, top_b)
        in_a, in_b = jnp.exp2(top_a - top), jnp.exp2(top_b - top)
        inverse = 1.0 / (in_a * z_a + in_b * z_b)
        o = (in_a * z_a * old + in_b * o_b) * inverse
        own = (lane >> 6) == half
        new = jnp.where(own & ((lane & 63) < 48), o, jnp.where(lane == 64 * half + 48, in_a * inverse, old))
        oa[p, at, :] = new
        wb[h] = (e * (in_b * inverse)).astype(wb.dtype)

    lane256 = iota((256, 128), 1)
    for p in range(2):
        def fwd(t, carry, p=p):
            forward_tile(8 * p + t)
            return carry

        lax.fori_loop(0, 8, fwd, 0)
        for ib in range(4):
            oa[p, 256 * ib : 256 * ib + 256, :] = jnp.concatenate([dqt[0, ib], dqt[1, ib]], axis=0).T
        if p == 0:
            each_row(lambda j: sparse_copy(j).wait_recv())
        branch_b(2 * p)
        branch_b(2 * p + 1)
        for ib in range(4):
            att[c, p, ib] = jnp.where(
                (lane256 & 63) < 48, oa[p, 256 * ib : 256 * ib + 256, :], 0.0
            ).astype(BF16)
        g_att[p].start()
    weights_out(14).wait()
    weights_out(15).wait()
    g_cot.near.wait_recv()
    g_cot.hand.wait_recv()
    vec[5:6, :] = colsum(gb[...].reshape(1024, 768).astype(F32))
    for d in in_wo:
        d.wait()
    for p in range(2):
        g_att[p].forward()
    for p in range(2):
        g_att[p].near.wait_recv()
        g_att[p].hand.wait_recv()

    def project(b):
        out = tok[b].astype(F32) + par[4:5, :]
        for s in range(4):
            out = out + nn(jnp.concatenate([att[s, 0, b], att[s, 1, b]], axis=1), wop[s])
        return out

    def second_norm(b, values):
        unit, inverse = normalise(values)
        a2[b] = (unit * par[5:6, :] + par[6:7, :]).astype(BF16)
        return unit, inverse

    y1[...] = project(c)
    second_norm(c, y1[...])

    in_dn.wait()
    acc[...] = y1[...] + par[7:8, :]
    da2[...] = jnp.zeros(da2.shape, F32)

    def mlp(i, carry):
        low = a2[c]
        g = gb[c]
        at = pl.ds(pl.multiple_of(768 * i, 768), 768)
        u = nn(low, wup[:, at]) + par[pl.ds(8 + i, 1), :]
        hidden, slope = gelu_parts(u)
        acc[...] += nn(hidden.astype(BF16), wdn[at, :])
        du = (nt(g, wdn[at, :]) * slope).astype(BF16)
        da2[...] += nt(du, wup[:, at])
        return carry

    lax.fori_loop(0, 4, mlp, 0)
    wqkv[0:256, :] = acc[...].astype(BF16)
    out_copy = local(wqkv.at[pl.ds(0, 256), :], out_h, 0)
    out_copy.start()
    unit, inverse = normalise(y1[...])
    vec[3:4, :] = colsum(da2[...] * unit)
    vec[4:5, :] = colsum(da2[...])
    dy1 = gb[c].astype(F32) + norm_back(da2[...], unit, inverse, par[5:6, :])
    y1[...] = dy1
    drb[c] = dy1.astype(BF16)
    g_dr.start()

    for j in range(1, 4):
        b = (c + j) % 4
        second_norm(b, project(b))
    in_dq.wait()

    def quarter(b, carry):
        u = nn(a2[b], wupq[...]) + bupq[0:1, :]
        hidden, slope = gelu_parts(u)
        at = pl.ds(pl.multiple_of(256 * b, 256), 256)
        wdn[at, :] = hidden.astype(BF16)
        du = (nt(gb[b], wdq[...]) * slope).astype(BF16)
        wdn[pl.ds(pl.multiple_of(1024 + 256 * b, 256), 256), :] = du
        vec[6:7, :] += colsum(du.astype(F32))
        return carry

    lax.fori_loop(0, 4, quarter, 0)

    def put(n, block, first):
        buf = slabs[n]
        width = block.shape[1]
        at = first
        while at < first + block.shape[0]:
            which, off = at // share, at % share
            size = min(share - off, first + block.shape[0] - at)
            buf[which % 2, which // 2, off : off + size, 0:width] = block[at - first : at - first + size].astype(BF16)
            at += size

    def phase_one(n):
        return remote(slabs[n].at[1 - rbit], recv_a[n], u1s.at[n], u1r.at[n], (2 * ra + 1 - rbit, c))

    def phase_two(n, j):
        to = (ra + j) % row_a
        return remote(slabs[n].at[rbit, to], recv_b[n].at[j - 1], u2s.at[n, j - 1], u2r.at[n, j - 1], (2 * to + rbit, c))

    def start_two(n):
        phase_one(n).wait_recv()

        def add(i, carry):
            slabs[n][rbit, i] = (slabs[n][rbit, i].astype(F32) + recv_a[n][i].astype(F32)).astype(BF16)
            return carry

        lax.fori_loop(0, row_a, add, 0)

        def send(j, carry):
            phase_two(n, j).start()
            return carry

        lax.fori_loop(1, row_a, send, 0)

    def slab_sent(n):
        phase_one(n).wait_send()

        def sent(j, carry):
            phase_two(n, j).wait_send()
            return carry

        lax.fori_loop(1, row_a, sent, 0)

    def col_copy(n, j):
        at = pl.ds(OFFSETS[n], UNITS[n])
        return remote(gath.at[c, :, at], gath.at[c, :, at], ucs.at[n, j - 1], ucr.at[n, j - 1], (r, (c + j) % COLS))

    def finish(n):
        def wait(j, carry):
            phase_two(n, j).wait_recv()
            return carry

        lax.fori_loop(1, row_a, wait, 0)
        gath[c, :, OFFSETS[n] : OFFSETS[n] + UNITS[n]] = (
            lax.fori_loop(
                0, row_a - 1, lambda j, t: t + recv_b[n][j].astype(F32), slabs[n][rbit, ra].astype(F32)
            )
        ).astype(BF16)
        for j in range(1, COLS):
            col_copy(n, j).start()

    for m in range(2):
        put(0, tn(wdn[0:1024, 384 * m : 384 * m + 384], gb[...].reshape(1024, 768)), 384 * m)
    phase_one(0).start()
    g_dr.forward()
    for m in range(2):
        lanes = jnp.concatenate([a2[b, :, 384 * m : 384 * m + 384] for b in range(4)], axis=0)
        put(1, tn(lanes, wdn[1024:2048, :]), 384 * m)
    phase_one(1).start()

    g_dr.near.wait_recv()
    g_dr.hand.wait_recv()
    vec[2:3, :] = colsum(drb[...].reshape(1024, 768).astype(F32))
    bones = onehot((iota((256, 256), 0) >> 6) == (iota((256, 256), 1) >> 6))

    def out_grad(b, carry):
        lane = iota((256, 256), 1) & 63
        at = pl.ds(pl.multiple_of(256 * b, 256), 256)
        d_att = nt(drb[b], wop[c]).astype(BF16).astype(F32)
        attended = jnp.concatenate([att[c, 0, b], att[c, 1, b]], axis=1).astype(F32)
        rowsum = moved(d_att * attended, bones, 2)
        factor = moved(
            jnp.where(lane == 48, jnp.concatenate([oa[0, at, :], oa[1, at, :]], axis=1), 0.0), bones
        )
        minus = -rowsum * factor
        high = minus.astype(BF16).astype(F32)
        marked = jnp.where(lane == 48, high, jnp.where(lane == 49, minus - high, d_att * factor))
        flipped = marked.T
        line = iota((128, 256), 0)
        for p in range(2):
            kaug[p, at, :] = marked[:, 128 * p : 128 * p + 128].astype(BF16)
            qf[p, at, :] = d_att[:, 128 * p : 128 * p + 128]
            qf[2 + p, at, :] = rowsum[:, 128 * p : 128 * p + 128]
        for h in range(4):
            p = h // 2
            qtm[h, b] = jnp.where(
                (line >> 6) == h % 2, flipped[128 * p : 128 * p + 128], 0.0
            ).astype(BF16)
        return carry

    lax.fori_loop(0, 4, out_grad, 0)

    own_cols = onehot(
        (iota((256, 768), 1) == 192 * c + iota((256, 768), 0)) & (iota((256, 768), 0) < 192)
    )
    dr_own = jnp.concatenate([nt(own_cols, drb[b]).astype(BF16) for b in range(4)], axis=1)
    for s in range(4):
        both = jnp.concatenate(
            [att[s, 0].reshape(1024, 128), att[s, 1].reshape(1024, 128)], axis=1
        )
        block = nn(dr_own, both).T
        for h in range(4):
            put(2, block[64 * h : 64 * h + 48], 192 * s + 48 * h)
    phase_one(2).start()

    step_rows = min(rows_n, 8)
    step_keys = 64 * step_rows

    def dilated_block(t):
        tall, wide = pl.multiple_of(64 * (t // 6), 64), pl.multiple_of(512 * (t % 6), 512)
        return wup.at[pl.ds(tall, 64), pl.ds(wide, 512)]

    for p in range(2):
        sides = []
        for half in range(2):
            h = 2 * p + half
            own = (iota((64, 128), 1) >> 6) == half
            d_sel = jnp.where(own, picked(p, h), 0.0).astype(BF16)
            sides.append((h, d_sel, picked(2 + p, h)[:, 64 * half : 64 * half + 1]))
            dqb[h] = jnp.zeros((64, 128), F32)

        def some_keys(n, carry, p=p, sides=sides):
            some = pl.ds(pl.multiple_of(step_rows * n, step_rows), step_rows)
            k2 = kvs[some, :, 128 * p : 128 * p + 128].reshape(step_keys, 128)
            v2 = kvs[some, :, 256 + 128 * p : 384 + 128 * p].reshape(step_keys, 128)
            dk, dv = 0.0, 0.0
            for h, d_sel, rs in sides:
                own = (iota((64, 128), 1) >> 6) == h % 2
                w = wb[h, :, pl.ds(pl.multiple_of(step_keys * n, step_keys), step_keys)]
                ds = (w.astype(F32) * (nt(d_sel, v2) - rs)).astype(BF16)
                dqb[h] += jnp.where(own, nn(ds, k2), 0.0)
                dk = dk + tn(ds, qsel[h])
                dv = dv + tn(w, d_sel)
            for t in range(step_rows):
                block = dilated_block(step_rows * n + t)
                block[:, 128 * p : 128 * p + 128] = dk[64 * t : 64 * t + 64].astype(BF16)
                block[:, 256 + 128 * p : 384 + 128 * p] = dv[64 * t : 64 * t + 64].astype(BF16)
            return carry

        lax.fori_loop(0, rows_n // step_rows, some_keys, 0)

    def dilated_copy(j):
        to = (r + j) % rows_n
        return remote(dilated_block(to), dkvr.at[j - 1], bss.at[j - 1], bsr.at[j - 1], (to, c))

    each_row(lambda j: dilated_copy(j).start())

    qf[...] = jnp.zeros(qf.shape, F32)

    def weights_in(i):
        return pltpu.make_async_copy(p_h.at[i], pbuf.at[i % 2], psem.at[i % 2])

    def backward_tile(i):
        h, ib = i // 4, i % 4
        p, half = h // 2, h % 2
        slot = i % 2
        weights_in(i).wait()

        @pl.when(i + 1 < 16)
        def _():
            weights_in(i + 1).start()

        rhs = qtm[h, ib]
        for jb in range(4):
            at = slice(256 * jb, 256 * jb + 256)
            dsb[at, :] = (pbuf[slot, at, :].astype(F32) * nn(vaug[p, at, :], rhs)).astype(BF16)
        keys = jnp.concatenate([kt[h, jb] for jb in range(4)], axis=1)
        dqt[h, ib] = nn(keys, dsb[...])
        at = pl.ds(pl.multiple_of(256 * ib, 256), 256)
        own = (iota((256, 128), 1) >> 6) == half
        d_rows, q_rows = kaug[p, at, :], qrow[p, at, :]
        for jb in range(4):
            js = slice(256 * jb, 256 * jb + 256)
            qf[2 + p, js, :] += jnp.where(own, nn(dsb[js, :], q_rows), 0.0)
            qf[4 + p, js, :] += jnp.where(own, nn(pbuf[slot, js, :], d_rows), 0.0)

    weights_in(0).start()
    for part in range(4):
        def bwd(t, carry, part=part):
            backward_tile(4 * part + t)
            return carry

        lax.fori_loop(0, 4, bwd, 0)
        if part == 0:
            start_two(0)
        if part == 1:
            start_two(1)
        if part == 2:
            start_two(2)

    each_row(lambda j: dilated_copy(j).wait_recv())
    spread = lax.fori_loop(
        0, rows_n - 1, lambda j, t: t + dkvr[j].astype(F32), dilated_block(r)[...].astype(F32)
    )
    each_row(lambda j: dilated_copy(j).wait_send())
    back_qkv = [local(h, wup.at[:, pl.ds(768 * i, 768)], 2 + i) for i, h in enumerate((wq_h, wk_h, wv_h))]
    for d in back_qkv:
        d.start()
    for h in range(4):
        p = h // 2
        own = (iota((64, 128), 1) >> 6) == h % 2
        at = pl.ds(LOCAL_HEADS * c + h, 64, stride=STRIDE)
        qf[p, at, :] += dqb[h]
        qf[2 + p, at, :] += jnp.where(own, spread[:, 128 * p : 128 * p + 128], 0.0)
        qf[4 + p, at, :] += jnp.where(own, spread[:, 256 + 128 * p : 384 + 128 * p], 0.0)

    def turned(i, b):
        at = pl.ds(pl.multiple_of(256 * b, 256), 256)
        return jnp.concatenate([qf[2 * i, at, :], qf[2 * i + 1, at, :]], axis=1).T

    def compact(b, carry):
        dq = (jnp.concatenate([dqt[h, b] for h in range(4)], axis=0) + turned(0, b)) * SCALE
        for i, m in enumerate((dq, turned(1, b) * SCALE, turned(2, b))):
            for h in range(4):
                a2[b, 48 * h : 48 * h + 48, 256 * i : 256 * i + 256] = m[64 * h : 64 * h + 48].astype(BF16)
        return carry

    lax.fori_loop(0, 4, compact, 0)

    def exchange(j):
        to = (c + j) % COLS
        at = pl.ds(pl.multiple_of(192 * c, 64), 192)
        return remote(a2.at[to, pl.ds(0, 192), :], dqr.at[at, :], ats.at[j - 1], atr.at[j - 1], (r, to))

    for j in range(1, COLS):
        exchange(j).start()
    dqr[pl.ds(pl.multiple_of(192 * c, 64), 192), :] = a2[c, 0:192, :]
    finish(0)
    finish(1)

    rows576 = [
        jnp.concatenate(
            [a2[b, 0:192, 256 * i : 256 * i + 256] for i in range(3)] + [jnp.zeros((64, 256), BF16)], axis=0
        )
        for b in range(4)
    ]
    lhs = jnp.concatenate(rows576, axis=1)
    slab_sent(0)
    for m in range(2):
        lanes = jnp.concatenate([a1[b, :, 384 * m : 384 * m + 384] for b in range(4)], axis=0)
        put(3, nn(lhs, lanes).T, 384 * m)
    phase_one(3).start()
    ones = jnp.ones((16, 1024), BF16)
    vec[7:8, 0:640] = nt(ones, lhs)[0:1]
    finish(2)

    for d in back_qkv:
        d.wait()
    for j in range(1, COLS):
        exchange(j).wait_recv()
    da1 = nn(wup[:, 0:768], dqr[:, 0:256])
    for i in range(1, 3):
        da1 = da1 + nn(wup[:, 768 * i : 768 * i + 768], dqr[:, 256 * i : 256 * i + 256])
    da1 = da1.T
    unit, inverse = normalise(tok[c].astype(F32))
    vec[0:1, :] = colsum(da1 * unit)
    vec[1:2, :] = colsum(da1)
    vec_pair = remote(vec, vpair, vss.at[0], vsr.at[0], (2 * ra + 1 - rbit, c))
    vec_pair.start()
    start_two(3)
    da2[...] = y1[...] + norm_back(da1, unit, inverse, par[0:1, :])
    gt_copy = local(da2, gt_h, 1)
    gt_copy.start()

    vec_pair.wait_recv()
    vrow[ra] = vec[...] + vpair[...]

    def vec_copy(j):
        to = (ra + j) % row_a
        return remote(vrow.at[ra], vrow.at[ra], vss.at[j], vsr.at[j], (2 * to + rbit, c))

    def each_pair(fn):
        def step(j, carry):
            fn(j)
            return carry

        lax.fori_loop(1, row_a, step, 0)

    each_pair(lambda j: vec_copy(j).start())
    finish(3)
    each_pair(lambda j: vec_copy(j).wait_recv())
    vcol[c] = lax.fori_loop(0, row_a, lambda j, t: t + vrow[j], jnp.zeros((16, 768), F32))

    def vec_col(j):
        return remote(vcol.at[c], vcol.at[c], vcs.at[j - 1], vcr.at[j - 1], (r, (c + j) % COLS))

    for j in range(1, COLS):
        vec_col(j).start()
    for j in range(1, COLS):
        vec_col(j).wait_recv()
        for n in range(4):
            col_copy(n, j).wait_recv()
    out_gath = local(gath, gath_h, 2)
    out_vec = local(vcol, vec_h, 3)
    out_gath.start()
    out_vec.start()

    for g in (g_tok, g_cot, *g_att, g_dr):
        g.drain()
    each_row(lambda j: sparse_copy(j).wait_send())
    vec_pair.wait_send()
    each_pair(lambda j: vec_copy(j).wait_send())
    for n in range(4):
        if n:
            slab_sent(n)
        for j in range(1, COLS):
            col_copy(n, j).wait_send()
    for j in range(1, COLS):
        exchange(j).wait_send()
        vec_col(j).wait_send()
    out_copy.wait()
    gt_copy.wait()
    out_gath.wait()
    out_vec.wait()


def finale(rows_n, gath, vec, out_in, gt_in, out, gt, g1, b1, gq, bq, gk, gv, bv, go, bo, g2, b2, gu, bu, gd, bd):
    share = 768 // rows_n
    r = lax.axis_index("row")
    out[...] = out_in[...]
    gt[...] = gt_in[...]
    part = [gath[s].astype(F32)[:share] for s in range(COLS)]

    def across(off, width):
        return jnp.concatenate([part[s][:, off : off + width] for s in range(COLS)], axis=1)

    gq[...] = across(1792, 192)
    gk[...] = across(1792 + 192, 192)
    gv[...] = across(1792 + 384, 192)
    go[...] = across(1536, 192)
    gu[...] = jnp.concatenate(
        [part[s][:, 768 + share * t : 768 + share * t + share] for t in range(rows_n) for s in range(COLS)], axis=1
    )
    for s in range(COLS):
        gd[share * s : share * s + share, :] = part[s][:, 0:768]
    summed = vec[0] + vec[1] + vec[2] + vec[3]
    wide = max(128, -(-share // 128) * 128)
    f, j = iota((768, wide), 0), iota((768, wide), 1)
    pick = onehot((f == share * r + j) & (j < share))
    mine = vec[0]
    total = moved(jnp.concatenate([summed[0:8], mine[0:8]], axis=0), pick)
    hidden = [moved(vec[s][0:8], pick) for s in range(COLS)]
    qv = [None, None]
    for n, off in enumerate((0, 384)):
        for s in range(COLS):
            place = onehot((f + 192 * s - off == share * r + j) & (j < share) & (f >= off) & (f < off + 192))
            term = moved(vec[s][0:8], place)
            qv[n] = term if qv[n] is None else qv[n] + term
    g1[...] = total[0, :share]
    b1[...] = total[1, :share]
    bo[...] = total[8 + 2, :share]
    g2[...] = total[3, :share]
    b2[...] = total[4, :share]
    bd[...] = total[8 + 5, :share]
    bq[...] = qv[0][7, :share]
    bv[...] = qv[1][7, :share]
    bu[...] = jnp.concatenate([hidden[s][6:7, :share] for s in range(COLS)], axis=1)[0]


def body(rows_n, tokens, norm1_gain, norm1_bias, w_query, b_query, w_key, w_value, b_value, w_out, b_out,
         norm2_gain, norm2_bias, w_up, b_up, w_down, b_down, slide_padded_units, padding_shortfall, cotangent):
    row_a, share = rows_n // 2, 768 // rows_n
    padded = -(-share // 16) * 16
    c = lax.axis_index("col")
    par = jnp.concatenate(
        [
            jnp.stack([norm1_gain, norm1_bias, b_query, b_value, b_out, norm2_gain, norm2_bias, b_down]),
            b_up.reshape(4, 768),
            jnp.zeros((4, 768), F32),
        ]
    )
    down_q = lax.dynamic_index_in_dim(w_down.reshape(rows_n, COLS, share, 768), c, 1, False).reshape(768, 768)
    vmem = pltpu.VMEM
    dma = pltpu.SemaphoreType.DMA
    between = max(row_a - 1, 1)
    scratch = [
        vmem((768, 3072), BF16), vmem((3072, 768), BF16), vmem((768, 768), BF16), vmem((768, 768), BF16),
        vmem((768, 768), BF16), vmem((4, 256, 768), BF16),
        *[vmem((4, 256, 768), BF16) for _ in range(5)],
        vmem((6, 1040, 128), F32), vmem((2, 1024, 128), BF16), vmem((2, 1024, 128), BF16),
        vmem((2, 1024, 128), BF16), vmem((4, 4, 128, 256), BF16), vmem((4, 4, 64, 256), BF16),
        vmem((4, 4, 64, 256), BF16), vmem((4, 4, 8, 256), F32),
        vmem((2, 1024, 256), BF16), vmem((1024, 256), F32), vmem((1024, 256), BF16),
        vmem((2, 1040, 128), F32), vmem((4, 2, 4, 256, 128), BF16),
        vmem((256, 768), F32), vmem((256, 768), F32), vmem((256, 768), F32),
        vmem((4, 4, 64, 256), F32), vmem((768, 768), BF16),
        *[vmem((2, row_a, padded, w), BF16) for w in UNITS[:3]],
        *[vmem((row_a, padded, w), BF16) for w in UNITS],
        *[vmem((between, padded, w), BF16) for w in UNITS],
        vmem((4, padded, WIDTH), BF16),
        vmem((rows_n, 64, 512), BF16), vmem((4, 64, 128), BF16), vmem((4, 64, rows_n * 64), BF16),
        vmem((4, 64, 128), F32), vmem((rows_n - 1, 64, 512), BF16),
        vmem((16, 768), F32), vmem((16, 768), F32), vmem((row_a, 16, 768), F32), vmem((4, 16, 768), F32), vmem((8, 768), F32),
        vmem((8, 768), F32),
        dma((24,)), dma((5, 3)), dma((5, 3)), dma((rows_n - 1,)), dma((rows_n - 1,)), dma((rows_n - 1,)),
        dma((rows_n - 1,)), dma((4,)), dma((4,)), dma((4, between)), dma((4, between)), dma((4, 3)), dma((4, 3)),
        dma((3,)), dma((3,)), dma((row_a,)), dma((row_a,)), dma((3,)), dma((3,)), dma((2,)),
    ]
    hbm = pl.BlockSpec(memory_space=pl.ANY)
    smem = pl.BlockSpec(memory_space=pltpu.SMEM)
    whole = pl.BlockSpec(memory_space=pltpu.VMEM)
    sds = jax.ShapeDtypeStruct
    out, gt, gath, vec, _ = pl.pallas_call(
        functools.partial(layer, rows_n, slide_padded_units.shape[0], None),
        out_shape=(
            sds((256, 768), BF16), sds((256, 768), F32), sds((4, padded, WIDTH), BF16), sds((4, 16, 768), F32),
            sds((16, 1024, 256), BF16),
        ),
        in_specs=[smem, smem, whole] + [hbm] * 9,
        out_specs=(hbm,) * 5,
        scratch_shapes=scratch,
        compiler_params=pltpu.CompilerParams(
            collective_id=0, has_side_effects=True, vmem_limit_bytes=(992 if rows_n <= 8 else 1021) * 64 * 1024
        ),
        name="layer",
    )(slide_padded_units, padding_shortfall, par, tokens, cotangent, w_query, w_key, w_value, w_out, w_up, w_down,
      down_q)
    vec1 = sds((share,), F32)
    mat = sds((share, 768), F32)
    return pl.pallas_call(
        functools.partial(finale, rows_n),
        out_shape=(
            sds((256, 768), BF16), sds((256, 768), F32), vec1, vec1, mat, vec1, mat, mat, vec1, mat, vec1, vec1, vec1,
            sds((share, 3072), F32), sds((4 * share,), F32), sds((4 * share, 768), F32), vec1,
        ),
        in_specs=[whole] * 4,
        out_specs=(whole,) * 17,
        compiler_params=pltpu.CompilerParams(vmem_limit_bytes=48 * 1024 * 1024),
        name="finale",
    )(gath, vec, out, gt)


def solution(mesh):
    tiles = P(("row", "col"), None)
    one, two = P("row"), P("row", None)
    return jax.shard_map(
        functools.partial(body, mesh.shape["row"]),
        mesh=mesh,
        in_specs=(tiles,) + (P(),) * 17 + (tiles,),
        out_specs=(tiles, tiles, one, one, two, one, two, two, one, two, one, one, one, two, one, two, one),
        check_vma=False,
    )
```

```python
import functools

import jax
import jax.numpy as jnp
from jax import lax
from jax.experimental import pallas as pl
from jax.experimental.pallas import tpu as pltpu
from jax.sharding import PartitionSpec as P

HEADS = 16
HEAD_DIM = 48
SLOT = 64
STRIDE = 16
PAD = 256
COLS = 4
LOCAL_HEADS = HEADS // COLS
EPS = 1e-05
NEG = -1e30
SCALE = HEAD_DIM**-0.5
SCALE2 = SCALE * 1.4426950408889634
MESH = pl.DeviceIdType.MESH
BF16 = jnp.bfloat16
F32 = jnp.float32
UNITS = (768, 768, 256, 640)
OFFSETS = (0, 768, 1536, 1792)
WIDTH = 2432


def nn(left, right):
    return jnp.dot(left, right, preferred_element_type=F32)


def nt(left, right):
    return lax.dot_general(left, right, (((1,), (1,)), ((), ())), preferred_element_type=F32)


def tn(left, right):
    return lax.dot_general(left, right, (((0,), (0,)), ((), ())), preferred_element_type=F32)


def iota(shape, dim):
    return lax.broadcasted_iota(jnp.int32, shape, dim)


def onehot(test):
    return jnp.where(test, 1.0, 0.0).astype(BF16)


def moved(values, chooser, parts=3):
    total = None
    for i in range(parts):
        low = values.astype(BF16)
        term = nn(low, chooser)
        total = term if total is None else total + term
        if i < parts - 1:
            values = values - low.astype(F32)
    return total


def normalise(x):
    centred = x - jnp.mean(x, axis=-1, keepdims=True)
    inverse = lax.rsqrt(jnp.mean(centred * centred, axis=-1, keepdims=True) + EPS)
    return centred * inverse, inverse


def norm_back(grad, unit, inverse, gain):
    scaled = grad * gain
    mean_one = jnp.mean(scaled, axis=-1, keepdims=True)
    mean_two = jnp.mean(scaled * unit, axis=-1, keepdims=True)
    return inverse * (scaled - mean_one - unit * mean_two)


def gelu_parts(u):
    z = jnp.abs(u) * 0.7071067811865476
    e = jnp.exp(-z * z)
    t = 1.0 / (1.0 + 0.3275911 * z)
    poly = t * (0.254829592 + t * (-0.284496736 + t * (1.421413741 + t * (-1.453152027 + t * 1.061405429))))
    tail = 0.5 * poly * e
    phi = jnp.where(u >= 0, 1.0 - tail, tail)
    return u * phi, phi + u * e * 0.3989422804014327


def colsum(x):
    return jnp.sum(x, axis=0, keepdims=True)


def layer(
    rows_n, slides_n, keep,
    slide_units, shortfall, v0, v1, v2, v3, v4, v5, v6, v7, v8, tok_h, cot_h, wq_h, wk_h, wv_h, wo_h, wup_h, wdn_h, wdq_h,
    out_h, gt_h, gath_h, vec_h, p_h,
    wup, wdn, wqkv, wupq, wdq, wop,
    tok, gb, a1, a2, drb,
    qf, qrow, kaug, vaug, qtm, kt, vta, sdr,
    pbuf, sref, dsb, oa, att,
    y1, acc, da2, dqt, dqr,
    slab0, slab1, slab2, ra0, ra1, ra2, ra3, rb0, rb1, rb2, rb3, rc0, rc1, rc2, rc3, gath,
    kvo, kvc, qsel, wb, dqb, dkvr,
    par, vec, vin, vrow, vcol, bupq, bqkv,
    lsem, gss, gsr, afs, afr, kos, kor, sps, spr, bss, bsr, u1s, u1r, u2s, u2r, u3s, u3r, ucs, ucr, ats, atr,
    vss, vsr, vcs, vcr, psem,
):
    his = rows_n // 4
    share = 768 // rows_n
    r = lax.axis_index("row")
    c = lax.axis_index("col")
    sib = c + 1 - 2 * (c % 2)
    across = (c + 2) % COLS
    diag = (sib + 2) % COLS
    hi, lo, bit = r // 4, (r // 2) % 2, r % 2
    recv_a, recv_b, recv_c = (ra0, ra1, ra2, ra3), (rb0, rb1, rb2, rb3), (rc0, rc1, rc2, rc3)
    slabs = (slab0, slab1, slab2, wdn.at[pl.ds(0, slab0.shape[0]), pl.ds(0, UNITS[3])])
    tall = slab0.shape[0] // rows_n
    key_count = rows_n * 64

    def local(src, dst, i):
        return pltpu.make_async_copy(src, dst, lsem.at[i])

    in_tok = local(tok_h, tok.at[c], 0)
    in_cot = local(cot_h, gb.at[c], 1)
    in_qkv = [local(h, wup.at[:, pl.ds(768 * i, 768)], 2 + i) for i, h in enumerate((wq_h, wk_h, wv_h))]
    in_up = local(wup_h, wup, 5)
    in_dn = local(wdn_h, wdn, 6)
    if share % 16 == 0:
        in_dq = [
            local(wdq_h.at[pl.ds(4 * share * t + share * c, share), :], wdq.at[pl.ds(share * t, share), :], 24 + t)
            for t in range(rows_n)
        ]
    else:
        in_dq = [local(wdq_h, wdq, 24)]
    in_wo = [
        local(wo_h.at[pl.ds(192 * s + 48 * h, 48), :], wop.at[s, pl.ds(64 * h, 48), :], 8 + 4 * s + h)
        for s in range(4)
        for h in range(4)
    ]
    in_tok.start()
    in_cot.start()
    for d in in_qkv:
        d.start()

    bar = pltpu.get_barrier_semaphore()
    for j in range(1, COLS):
        pl.semaphore_signal(bar, inc=1, device_id=(r, (c + j) % COLS), device_id_type=MESH)

    def greet(j, carry):
        pl.semaphore_signal(bar, inc=1, device_id=((r + j) % rows_n, c), device_id_type=MESH)
        return carry

    lax.fori_loop(1, rows_n, greet, 0)
    for d in in_dq:
        d.start()
    for d in in_wo:
        d.start()
    in_dn.start()
    pl.semaphore_wait(bar, COLS - 1 + rows_n - 1)

    def remote(src, dst, send, recv, dev):
        return pltpu.make_async_remote_copy(
            src_ref=src, dst_ref=dst, send_sem=send, recv_sem=recv, device_id=dev, device_id_type=MESH
        )

    class Gather:
        def __init__(self, n, slot):
            self.near = remote(slot(c), slot(c), gss.at[n, 0], gsr.at[n, 0], (r, sib))
            self.far = remote(slot(c), slot(c), gss.at[n, 1], gsr.at[n, 1], (r, across))
            self.hand = remote(slot(across), slot(across), gss.at[n, 2], gsr.at[n, 2], (r, sib))

        def start(self):
            self.far.start()
            self.near.start()

        def forward(self):
            self.far.wait_recv()
            self.hand.start()

        def drain(self):
            self.near.wait_send()
            self.far.wait_send()
            self.hand.wait_send()

    g_tok = Gather(0, lambda i: tok.at[i])
    g_cot = Gather(1, lambda i: gb.at[i])
    g_dr = Gather(2, lambda i: drb.at[i])

    class Attended:
        def __init__(self, p):
            def copy(n, owner, block, dev):
                ref = att.at[owner, p] if block is None else att.at[owner, p, block]
                return remote(ref, ref, afs.at[p, n], afr.at[p, n], (r, dev))

            self.first = [copy(0, c, None, sib), copy(1, c, across, across), copy(2, c, diag, diag)]
            self.rest = [copy(3, c, diag, across), copy(4, c, c, across), copy(5, c, sib, across)]
            self.hand = [copy(6, across, c, sib), copy(7, across, across, sib), copy(8, across, diag, sib)]

    attended = [Attended(p) for p in range(2)]

    in_tok.wait()
    g_tok.start()
    in_cot.wait()
    g_cot.start()
    for i, v in enumerate((v0, v1, v2, v3, v4, v5, v6, v7)):
        par[i : i + 1, :] = v[...].reshape(1, 768)
    for i in range(4):
        par[8 + i : 9 + i, :] = v8[768 * i : 768 * i + 768].reshape(1, 768)

    ends, lims = [], []
    total = jnp.int32(0)
    for s in range(slides_n):
        total = total + slide_units[s] * PAD
        ends.append(total)
        lims.append(total - shortfall[s])

    def label_of(pos):
        lab = jnp.zeros(pos.shape, jnp.int32)
        for s in range(slides_n - 1):
            lab = lab + jnp.where(pos >= ends[s], 1, 0)
        return lab

    def code_of(pos):
        code = label_of(pos)
        for s in range(slides_n):
            code = jnp.where((pos >= lims[s]) & (pos < ends[s]), -1, code)
        return code

    seg_first = r * 1024

    vec[...] = jnp.zeros(vec.shape, F32)
    for s in range(4):
        for h in range(4):
            wop[s, 64 * h + 48 : 64 * h + 64, :] = jnp.zeros((16, 768), BF16)
    sel_f, sel_j = iota((768, 256), 0), iota((768, 256), 1)
    head_sel = onehot((sel_f == 192 * c + 48 * (sel_j >> 6) + (sel_j & 63)) & ((sel_j & 63) < 48))
    for i, d in enumerate(in_qkv):
        d.wait()
        wqkv[:, 256 * i : 256 * i + 256] = nn(wup[:, 768 * i : 768 * i + 768], head_sel).astype(BF16)
    bqkv[...] = jnp.zeros(bqkv.shape, F32)
    biases = moved(par[0:8, :], head_sel)
    bqkv[0:1, 0:256] = biases[2:3]
    bqkv[0:1, 512:768] = biases[3:4]

    def first_norm(b):
        unit, _ = normalise(tok[b].astype(F32))
        a1[b] = (unit * par[0:1, :] + par[1:2, :]).astype(BF16)

    first_norm(c)
    on_head = (iota((256, 768), 0) & (STRIDE - 1)) == ((iota((256, 768), 1) * 1366) >> 16)

    def dilated(values):
        return jnp.sum(jnp.where(on_head, values.astype(BF16).astype(F32), 0.0).reshape(16, 16, 768), axis=1)

    k_sel = dilated(nn(a1[c], wup[:, 768:1536]))
    v_sel = dilated(nn(a1[c], wup[:, 1536:2304]) + par[3:4, :])
    for s in range(COLS):
        kvo[s] = jnp.concatenate(
            [k_sel[:, 192 * s : 192 * s + 192], v_sel[:, 192 * s : 192 * s + 192]], axis=1
        ).astype(BF16)
    own16 = pl.ds(pl.multiple_of(16 * c, 16), 16)

    def own_dilated(j):
        to = (c + j) % COLS
        return remote(kvo.at[to], kvc.at[r, own16, :], kos.at[j - 1], kor.at[j - 1], (r, to))

    for j in range(1, COLS):
        own_dilated(j).start()
    kvc[r, own16, :] = kvo[c]
    in_up.start()

    def qkv_block(b):
        low = a1[b]
        y = (nn(low, wqkv[...]) + bqkv[0:1, :]).astype(BF16).astype(F32)
        at = pl.ds(pl.multiple_of(256 * b, 256), 256)
        for i in range(6):
            qf[i, at, :] = y[:, 128 * i : 128 * i + 128]
        lane = iota((256, 128), 1) & 63
        key_code = code_of(seg_first + 256 * b + iota((256, 128), 0))
        key_mark = jnp.where(key_code == lane - 48, 0.0, NEG)
        marked = (lane >= 48) & (lane < 48 + slides_n)
        for p in range(2):
            qrow[p, at, :] = y[:, 128 * p : 128 * p + 128].astype(BF16)
            kaug[p, at, :] = jnp.where(marked, key_mark, y[:, 256 + 128 * p : 384 + 128 * p]).astype(BF16)
            vaug[p, at, :] = jnp.where(
                (lane == 48) | (lane == 49), 1.0, y[:, 512 + 128 * p : 640 + 128 * p]
            ).astype(BF16)
        qt, ktv, vt = y[:, :256].T, y[:, 256:512].T, y[:, 512:].T
        row = iota((128, 256), 0)
        query_label = label_of(seg_first + 256 * b + iota((128, 256), 1))
        mark = jnp.where(query_label == (row & 63) - 48, 1.0, 0.0)
        for h in range(4):
            p, half = h // 2, h % 2
            own = (row >> 6) == half
            full = jnp.where((row & 63) < 48, qt[128 * p : 128 * p + 128], mark)
            qtm[h, b] = jnp.where(own, full, 0.0).astype(BF16)
            hq, hk, hv = (m[64 * h : 64 * h + 64] for m in (qt, ktv, vt))
            kt[h, b] = hk.astype(BF16)
            vta[h, b] = jnp.where(iota((64, 256), 0) == 48, 1.0, hv).astype(BF16)
            sdr[h, b] = jnp.broadcast_to(colsum(hq * hk) * SCALE2, (8, 256))

    def sparse_copy(j):
        return remote(kvc.at[r], kvc.at[r], sps.at[j - 1], spr.at[j - 1], ((r + j) % rows_n, c))

    def each_row(fn):
        def step(j, carry):
            fn(j)
            return carry

        lax.fori_loop(1, rows_n, step, 0)

    qkv_block(c)
    g_tok.near.wait_recv()
    first_norm(sib)
    qkv_block(sib)
    for j in range(1, COLS):
        own_dilated(j).wait_recv()
    each_row(lambda j: sparse_copy(j).start())

    in_up.wait()
    for n in range(3):
        start = (4 * share * ((256 * n) // share)) // 128 * 128
        stop = -(-(4 * share * ((256 * n + 255) // share + 1)) // 128) * 128
        o = 256 * n + iota((stop - start, 256), 1)
        group = jnp.zeros_like(o)
        for t in range(1, rows_n):
            group = group + jnp.where(o >= share * t, 1, 0)
        unit_sel = onehot(start + iota((stop - start, 256), 0) == 3 * share * group + share * c + o)
        for m in range(3):
            wupq[256 * m : 256 * m + 256, 256 * n : 256 * n + 256] = nn(
                wup[256 * m : 256 * m + 256, start:stop], unit_sel
            ).astype(BF16)
        pieces = [par[8 + t : 9 + t, :] for t in range(4)]
        line = jnp.concatenate(pieces, axis=1)[:, start:stop]
        bupq[0:8, 256 * n : 256 * n + 256] = moved(jnp.broadcast_to(line, (8, stop - start)), unit_sel)

    g_tok.forward()
    first_norm(across)
    qkv_block(across)
    g_tok.hand.wait_recv()
    first_norm(diag)
    qkv_block(diag)

    def picked(i, h):
        return qf[i, pl.ds(LOCAL_HEADS * c + h, 64, stride=STRIDE), :]

    def both_picked(i, p):
        lane = iota((64, 128), 1)
        return jnp.concatenate(
            [jnp.where((lane >> 6) == half, picked(i, 2 * p + half), 0.0) for half in range(2)], axis=0
        ).astype(BF16)

    def placing(p, first, transposed=False):
        shape = (256, 128) if transposed else (128, 256)
        wide, narrow = iota(shape, 0 if transposed else 1), iota(shape, 1 if transposed else 0)
        return onehot(((narrow & 63) < 48) & (wide == first + 48 * (2 * p + (narrow >> 6)) + (narrow & 63)))

    for p in range(2):
        qsel[p] = nn(both_picked(p, p), placing(p, 0)).astype(BF16)

    eye = iota((256, 256), 0) == iota((256, 256), 1)

    def weights_out(i):
        return pltpu.make_async_copy(pbuf.at[i % 2], p_h.at[i], psem.at[i % 2])

    def forward_tile(i):
        h, ib = i // 4, i % 4
        p, half = h // 2, h % 2
        slot = i if keep else i % 2
        rhs = qtm[h, ib]
        top = jnp.full((8, 256), NEG * 10, F32)
        for jb in range(4):
            s = nn(kaug[p, 256 * jb : 256 * jb + 256, :], rhs) * SCALE2
            sref[256 * jb : 256 * jb + 256, :] = s
            top = jnp.maximum(top, jnp.max(s.reshape(32, 8, 256), axis=0))
        own = sdr[h, ib]
        top = jnp.max(jnp.maximum(top, own), axis=0, keepdims=True)
        at = pl.ds(pl.multiple_of(256 * ib, 256), 256)
        sref[at, :] = jnp.where(eye, own[0:1], sref[at, :])

        if not keep:

            @pl.when(i >= 2)
            def _():
                weights_out(i).wait()

        for jb in range(4):
            pbuf[slot, 256 * jb : 256 * jb + 256, :] = jnp.exp2(
                sref[256 * jb : 256 * jb + 256, :] - top
            ).astype(BF16)
        if not keep:
            weights_out(i).start()
        values = jnp.concatenate([vta[h, jb] for jb in range(4)], axis=1)
        o = nn(values, pbuf[slot])
        z = o[48:49]
        inverse = 1.0 / z
        line = iota((64, 256), 0)
        o = o * inverse
        o = jnp.where(line == 48, inverse, jnp.where(line == 49, top, jnp.where(line == 50, z, o)))
        dqt[half, ib] = o

    def branch_b(p):
        lane = iota((64, 128), 1)
        s = nt(qsel[p], kvc[:, :, 0:256].reshape(key_count, 256)) * SCALE2
        masked = []
        for half in range(2):
            first = LOCAL_HEADS * c + 2 * p + half
            qpos = seg_first + STRIDE * iota((64, 128), 0)[:, 0:1] + first
            kpos = STRIDE * iota((8, key_count), 1)[0:1] + first
            allowed = (label_of(qpos) == code_of(kpos)) | (qpos == kpos)
            masked.append(jnp.where(allowed, s[64 * half : 64 * half + 64], NEG))
        s = jnp.concatenate(masked, axis=0)
        tops = jnp.max(s, axis=1, keepdims=True)
        e = jnp.exp2(s - tops)
        sums = jnp.sum(e, axis=1, keepdims=True)
        outs = moved(nn(e.astype(BF16), kvc[:, :, 128:384].reshape(key_count, 256)), placing(p, 64, True))
        factors = []
        for half in range(2):
            rows = slice(64 * half, 64 * half + 64)
            top_b, z_b, o_b = tops[rows], sums[rows], outs[rows]
            at = pl.ds(LOCAL_HEADS * c + 2 * p + half, 64, stride=STRIDE)
            old = oa[p, at, :]
            top_a = old[:, 64 * half + 49 : 64 * half + 50]
            z_a = old[:, 64 * half + 50 : 64 * half + 51]
            top = jnp.maximum(top_a, top_b)
            in_a, in_b = jnp.exp2(top_a - top), jnp.exp2(top_b - top)
            inverse = 1.0 / (in_a * z_a + in_b * z_b)
            o = (in_a * z_a * old + in_b * o_b) * inverse
            own = (lane >> 6) == half
            oa[p, at, :] = jnp.where(
                own & ((lane & 63) < 48), o, jnp.where(lane == 64 * half + 48, in_a * inverse, old)
            )
            factors.append(in_b * inverse)
        wb[p] = (e * jnp.concatenate(factors, axis=0)).astype(BF16)

    lane256 = iota((256, 128), 1)
    for p in range(2):
        def fwd(t, carry, p=p):
            forward_tile(8 * p + t)
            return carry

        lax.fori_loop(0, 8, fwd, 0)
        for ib in range(4):
            oa[p, 256 * ib : 256 * ib + 256, :] = jnp.concatenate([dqt[0, ib], dqt[1, ib]], axis=0).T
        if p == 0:
            each_row(lambda j: sparse_copy(j).wait_recv())
        else:
            g_cot.forward()
        branch_b(p)
        for ib in range(4):
            att[c, p, ib] = jnp.where(
                (lane256 & 63) < 48, oa[p, 256 * ib : 256 * ib + 256, :], 0.0
            ).astype(BF16)
        for d in attended[p].first:
            d.start()
    if not keep:
        weights_out(14).wait()
        weights_out(15).wait()
    for a in attended:
        for d in a.rest:
            d.start()
    g_cot.near.wait_recv()
    g_cot.hand.wait_recv()
    vec[5:6, :] = colsum(gb[...].reshape(1024, 768).astype(F32))
    for d in in_wo:
        d.wait()
    for a in attended:
        for d in a.first:
            d.wait_recv()

    def project(b):
        out = tok[b].astype(F32) + par[4:5, :]
        for s in range(4):
            out = out + nn(jnp.concatenate([att[s, 0, b], att[s, 1, b]], axis=1), wop[s])
        return out

    def second_norm(b, values):
        unit, inverse = normalise(values)
        a2[b] = (unit * par[5:6, :] + par[6:7, :]).astype(BF16)
        return unit, inverse

    y1[...] = project(c)
    second_norm(c, y1[...])

    in_dn.wait()
    acc[...] = y1[...] + par[7:8, :]
    da2[...] = jnp.zeros(da2.shape, F32)

    def mlp(i, carry):
        low = a2[c]
        g = gb[c]
        at = pl.ds(pl.multiple_of(768 * i, 768), 768)
        u = nn(low, wup[:, at]) + par[pl.ds(8 + i, 1), :]
        hidden, slope = gelu_parts(u)
        acc[...] += nn(hidden.astype(BF16), wdn[at, :])
        du = (nt(g, wdn[at, :]) * slope).astype(BF16)
        da2[...] += nt(du, wup[:, at])
        return carry

    lax.fori_loop(0, 4, mlp, 0)
    for a in attended:
        for d in a.rest:
            d.wait_recv()
        for d in a.hand:
            d.start()
    wqkv[0:256, :] = acc[...].astype(BF16)
    out_copy = local(wqkv.at[pl.ds(0, 256), :], out_h, 0)
    out_copy.start()
    unit, inverse = normalise(y1[...])
    vec[3:4, :] = colsum(da2[...] * unit)
    vec[4:5, :] = colsum(da2[...])
    dy1 = gb[c].astype(F32) + norm_back(da2[...], unit, inverse, par[5:6, :])
    y1[...] = dy1
    drb[c] = dy1.astype(BF16)
    g_dr.start()

    for a in attended:
        for d in a.hand:
            d.wait_recv()
    for j in range(1, 4):
        b = (c + j) % 4
        second_norm(b, project(b))
    for d in in_dq:
        d.wait()

    def quarter(b, carry):
        u = nn(a2[b], wupq[...]) + bupq[0:1, :]
        hidden, slope = gelu_parts(u)
        at = pl.ds(pl.multiple_of(256 * b, 256), 256)
        wdn[at, :] = hidden.astype(BF16)
        du = (nt(gb[b], wdq[...]) * slope).astype(BF16)
        wdn[pl.ds(pl.multiple_of(1024 + 256 * b, 256), 256), :] = du
        vec[6:7, :] += colsum(du.astype(F32))
        return carry

    lax.fori_loop(0, 4, quarter, 0)

    def slab_at(b, l, h):
        return ((2 * b + l) * his + h) * tall

    def put(n, block, first):
        buf = slabs[n]
        width = block.shape[1]
        at = first
        while at < first + block.shape[0]:
            which, off = at // share, at % share
            size = min(share - off, first + block.shape[0] - at)
            row = slab_at(which % 2, (which // 2) % 2, which // 4) + off
            buf[row : row + size, 0:width] = block[at - first : at - first + size].astype(BF16)
            at += size

    def one(n):
        half = 2 * his * tall
        at = pl.ds(pl.multiple_of((1 - bit) * half, half), half)
        return remote(slabs[n].at[at, :], recv_a[n], u1s.at[n], u1r.at[n], (r + 1 - 2 * bit, c))

    def two(n):
        at = pl.ds(pl.multiple_of(slab_at(bit, 1 - lo, 0), his * tall), his * tall)
        return remote(slabs[n].at[at, :], recv_b[n], u2s.at[n], u2r.at[n], (r + 2 - 4 * lo, c))

    def slab(l, h):
        return pl.ds(pl.multiple_of(slab_at(bit, l, h), tall), tall)

    def three(n, j):
        to = (hi + j) % his
        return remote(
            slabs[n].at[slab(lo, to), :], recv_c[n].at[j - 1], u3s.at[n, j - 1], u3r.at[n, j - 1],
            (4 * to + 2 * lo + bit, c),
        )

    def each_hi(fn):
        def step(j, carry):
            fn(j)
            return carry

        lax.fori_loop(1, his, step, 0)

    def start_two(n):
        one(n).wait_recv()

        def add(i, carry):
            for l in range(2):
                at = pl.ds(pl.multiple_of((l * his + i) * tall, tall), tall)
                slabs[n][slab(l, i), :] = (slabs[n][slab(l, i), :].astype(F32) + recv_a[n][at, :].astype(F32)).astype(BF16)
            return carry

        lax.fori_loop(0, his, add, 0)
        two(n).start()

    def start_three(n):
        two(n).wait_recv()

        def add(i, carry):
            at = pl.ds(pl.multiple_of(i * tall, tall), tall)
            slabs[n][slab(lo, i), :] = (slabs[n][slab(lo, i), :].astype(F32) + recv_b[n][at, :].astype(F32)).astype(BF16)
            return carry

        lax.fori_loop(0, his, add, 0)
        each_hi(lambda j: three(n, j).start())

    def slab_sent(n):
        one(n).wait_send()
        two(n).wait_send()
        each_hi(lambda j: three(n, j).wait_send())

    def col_copy(n, j):
        at = pl.ds(OFFSETS[n], UNITS[n])
        return remote(gath.at[c, :, at], gath.at[c, :, at], ucs.at[n, j - 1], ucr.at[n, j - 1], (r, (c + j) % COLS))

    def finish(n):
        each_hi(lambda j: three(n, j).wait_recv())
        gath[c, :, OFFSETS[n] : OFFSETS[n] + UNITS[n]] = (
            lax.fori_loop(
                0, his - 1, lambda j, t: t + recv_c[n][j].astype(F32), slabs[n][slab(lo, hi), :].astype(F32)
            )
        ).astype(BF16)
        for j in range(1, COLS):
            col_copy(n, j).start()

    for m in range(2):
        put(0, tn(wdn[0:1024, 384 * m : 384 * m + 384], gb[...].reshape(1024, 768)), 384 * m)
    one(0).start()
    g_dr.forward()
    for m in range(2):
        lanes = jnp.concatenate([a2[b, :, 384 * m : 384 * m + 384] for b in range(4)], axis=0)
        put(1, tn(lanes, wdn[1024:2048, :]), 384 * m)

    g_dr.near.wait_recv()
    g_dr.hand.wait_recv()
    vec[2:3, :] = colsum(drb[...].reshape(1024, 768).astype(F32))
    bones = onehot((iota((256, 256), 0) >> 6) == (iota((256, 256), 1) >> 6))

    def out_grad(b, carry):
        lane = iota((256, 256), 1) & 63
        at = pl.ds(pl.multiple_of(256 * b, 256), 256)
        d_att = nt(drb[b], wop[c]).astype(BF16).astype(F32)
        mine = jnp.concatenate([att[c, 0, b], att[c, 1, b]], axis=1).astype(F32)
        rowsum = moved(d_att * mine, bones, 2)
        factor = moved(
            jnp.where(lane == 48, jnp.concatenate([oa[0, at, :], oa[1, at, :]], axis=1), 0.0), bones
        )
        minus = -rowsum * factor
        high = minus.astype(BF16).astype(F32)
        marked = jnp.where(lane == 48, high, jnp.where(lane == 49, minus - high, d_att * factor))
        flipped = marked.T
        line = iota((128, 256), 0)
        for p in range(2):
            kaug[p, at, :] = marked[:, 128 * p : 128 * p + 128].astype(BF16)
            qf[p, at, :] = d_att[:, 128 * p : 128 * p + 128]
            qf[2 + p, at, :] = rowsum[:, 128 * p : 128 * p + 128]
        for h in range(4):
            p = h // 2
            qtm[h, b] = jnp.where(
                (line >> 6) == h % 2, flipped[128 * p : 128 * p + 128], 0.0
            ).astype(BF16)
        return carry

    lax.fori_loop(0, 4, out_grad, 0)

    own_cols = onehot(
        (iota((256, 768), 1) == 192 * c + iota((256, 768), 0)) & (iota((256, 768), 0) < 192)
    )
    dr_own = jnp.concatenate([nt(own_cols, drb[b]).astype(BF16) for b in range(4)], axis=1)
    for s in range(4):
        both = jnp.concatenate(
            [att[s, 0].reshape(1024, 128), att[s, 1].reshape(1024, 128)], axis=1
        )
        block = nn(dr_own, both).T
        for h in range(4):
            put(2, block[64 * h : 64 * h + 48], 192 * s + 48 * h)

    step_rows = min(rows_n, 8)
    step_keys = 64 * step_rows

    def dilated_block(t):
        tall, wide = pl.multiple_of(64 * (t // 8), 64), pl.multiple_of(384 * (t % 8), 384)
        return wup.at[pl.ds(tall, 64), pl.ds(wide, 384)]

    d_sel, sums = [], []
    for p in range(2):
        d_sel.append(nn(both_picked(p, p), placing(p, 64)).astype(BF16))
        sums.append(
            jnp.concatenate([picked(2 + p, 2 * p + i)[:, 64 * i : 64 * i + 1] for i in range(2)], axis=0)
        )
    dqb[...] = jnp.zeros(dqb.shape, F32)

    def some_keys(n, carry):
        some = pl.ds(pl.multiple_of(step_rows * n, step_rows), step_rows)
        k2 = kvc[some, :, 0:256].reshape(step_keys, 256)
        v2 = kvc[some, :, 128:384].reshape(step_keys, 256)
        dk, dv = 0.0, 0.0
        for p in range(2):
            w = wb[p, :, pl.ds(pl.multiple_of(step_keys * n, step_keys), step_keys)]
            ds = (w.astype(F32) * (nt(d_sel[p], v2) - sums[p])).astype(BF16)
            dqb[p] += nn(ds, k2)
            dk = dk + tn(ds, qsel[p])
            dv = dv + tn(w, d_sel[p])
        for t in range(step_rows):
            block = dilated_block(step_rows * n + t)
            rows = slice(64 * t, 64 * t + 64)
            block[:, 0:128] = dk[rows, 0:128].astype(BF16)
            block[:, 128:256] = (dk[rows, 128:256] + dv[rows, 0:128]).astype(BF16)
            block[:, 256:384] = dv[rows, 128:256].astype(BF16)
        return carry

    lax.fori_loop(0, rows_n // step_rows, some_keys, 0)

    def dilated_copy(j):
        to = (r + j) % rows_n
        return remote(dilated_block(to), dkvr.at[j - 1], bss.at[j - 1], bsr.at[j - 1], (to, c))

    each_row(lambda j: dilated_copy(j).start())
    one(1).start()
    one(2).start()

    qf[...] = jnp.zeros(qf.shape, F32)

    def weights_in(i):
        return pltpu.make_async_copy(p_h.at[i], pbuf.at[i % 2], psem.at[i % 2])

    def backward_tile(i):
        h, ib = i // 4, i % 4
        p, half = h // 2, h % 2
        slot = i if keep else i % 2
        if not keep:
            weights_in(i).wait()

            @pl.when(i + 1 < 16)
            def _():
                weights_in(i + 1).start()

        rhs = qtm[h, ib]
        for jb in range(4):
            at = slice(256 * jb, 256 * jb + 256)
            dsb[at, :] = (pbuf[slot, at, :].astype(F32) * nn(vaug[p, at, :], rhs)).astype(BF16)
        keys = jnp.concatenate([kt[h, jb] for jb in range(4)], axis=1)
        dqt[h, ib] = nn(keys, dsb[...])
        at = pl.ds(pl.multiple_of(256 * ib, 256), 256)
        own = (iota((256, 128), 1) >> 6) == half
        d_rows, q_rows = kaug[p, at, :], qrow[p, at, :]
        for jb in range(4):
            js = slice(256 * jb, 256 * jb + 256)
            qf[2 + p, js, :] += jnp.where(own, nn(dsb[js, :], q_rows), 0.0)
            qf[4 + p, js, :] += jnp.where(own, nn(pbuf[slot, js, :], d_rows), 0.0)

    if not keep:
        weights_in(0).start()
    for first, last in ((0, 11), (11, 16)):
        def bwd(t, carry):
            backward_tile(t)
            return carry

        lax.fori_loop(first, last, bwd, 0)
        if first == 0:
            start_two(0)

    each_row(lambda j: dilated_copy(j).wait_recv())
    spread = lax.fori_loop(
        0, rows_n - 1, lambda j, t: t + dkvr[j].astype(F32), dilated_block(r)[...].astype(F32)
    )
    each_row(lambda j: dilated_copy(j).wait_send())
    back_qkv = [local(h, wup.at[:, pl.ds(768 * i, 768)], 2 + i) for i, h in enumerate((wq_h, wk_h, wv_h))]
    for d in back_qkv:
        d.start()
    source, slot = iota((384, 512), 0), iota((384, 512), 1)
    spread = moved(
        spread,
        onehot(((slot & 63) < 48) & (source == 192 * (slot >> 8) + 48 * ((slot & 255) >> 6) + (slot & 63))),
        2,
    )
    dq_b = [moved(dqb[p], placing(p, 0, True), 2) for p in range(2)]
    for h in range(4):
        p, rows = h // 2, slice(64 * (h % 2), 64 * (h % 2) + 64)
        own = (iota((64, 128), 1) >> 6) == h % 2
        at = pl.ds(LOCAL_HEADS * c + h, 64, stride=STRIDE)
        qf[p, at, :] += jnp.where(own, dq_b[p][rows], 0.0)
        qf[2 + p, at, :] += jnp.where(own, spread[:, 128 * p : 128 * p + 128], 0.0)
        qf[4 + p, at, :] += jnp.where(own, spread[:, 256 + 128 * p : 384 + 128 * p], 0.0)

    def turned(i, b):
        at = pl.ds(pl.multiple_of(256 * b, 256), 256)
        return jnp.concatenate([qf[2 * i, at, :], qf[2 * i + 1, at, :]], axis=1).T

    def compact(b, carry):
        dq = (jnp.concatenate([dqt[h, b] for h in range(4)], axis=0) + turned(0, b)) * SCALE
        for i, m in enumerate((dq, turned(1, b) * SCALE, turned(2, b))):
            for h in range(4):
                a2[b, 48 * h : 48 * h + 48, 256 * i : 256 * i + 256] = m[64 * h : 64 * h + 48].astype(BF16)
        return carry

    lax.fori_loop(0, 4, compact, 0)

    def exchange(j):
        to = (c + j) % COLS
        at = pl.ds(pl.multiple_of(192 * c, 64), 192)
        return remote(a2.at[to, pl.ds(0, 192), :], dqr.at[at, :], ats.at[j - 1], atr.at[j - 1], (r, to))

    for j in range(1, COLS):
        exchange(j).start()
    dqr[pl.ds(pl.multiple_of(192 * c, 64), 192), :] = a2[c, 0:192, :]
    rows576 = [
        jnp.concatenate(
            [a2[b, 0:192, 256 * i : 256 * i + 256] for i in range(3)] + [jnp.zeros((64, 256), BF16)], axis=0
        )
        for b in range(4)
    ]
    lhs = jnp.concatenate(rows576, axis=1)
    for m in range(2):
        lanes = jnp.concatenate([a1[b, :, 384 * m : 384 * m + 384] for b in range(4)], axis=0)
        put(3, nn(lhs, lanes).T, 384 * m)
    one(3).start()
    start_three(0)
    ones = jnp.ones((16, 1024), BF16)
    vec[7:8, 0:640] = nt(ones, lhs)[0:1]
    start_two(1)
    finish(0)

    for d in back_qkv:
        d.wait()
    for j in range(1, COLS):
        exchange(j).wait_recv()
    da1 = nn(wup[:, 0:768], dqr[:, 0:256])
    for i in range(1, 3):
        da1 = da1 + nn(wup[:, 768 * i : 768 * i + 768], dqr[:, 256 * i : 256 * i + 256])
    da1 = da1.T
    unit, inverse = normalise(tok[c].astype(F32))
    vec[0:1, :] = colsum(da1 * unit)
    vec[1:2, :] = colsum(da1)
    vec_one = remote(vec, vin.at[0], vss.at[0], vsr.at[0], (r + 1 - 2 * bit, c))
    vec_one.start()
    da2[...] = y1[...] + norm_back(da1, unit, inverse, par[0:1, :])
    gt_copy = local(da2, gt_h, 1)
    gt_copy.start()
    start_two(2)
    vec_one.wait_recv()
    vcol[c] = vec[...] + vin[0]
    vec_two = remote(vcol.at[c], vin.at[1], vss.at[1], vsr.at[1], (r + 2 - 4 * lo, c))
    vec_two.start()
    start_three(1)
    start_three(2)
    vec_two.wait_recv()
    vrow[hi] = vcol[c] + vin[1]

    def vec_three(j):
        to = (hi + j) % his
        return remote(vrow.at[hi], vrow.at[hi], vss.at[1 + j], vsr.at[1 + j], (4 * to + 2 * lo + bit, c))

    each_hi(lambda j: vec_three(j).start())
    start_two(3)
    finish(1)
    finish(2)
    each_hi(lambda j: vec_three(j).wait_recv())
    vec_two.wait_send()
    vcol[c] = lax.fori_loop(0, his, lambda j, t: t + vrow[j], jnp.zeros((16, 768), F32))

    def vec_col(j):
        return remote(vcol.at[c], vcol.at[c], vcs.at[j - 1], vcr.at[j - 1], (r, (c + j) % COLS))

    for j in range(1, COLS):
        vec_col(j).start()
    start_three(3)
    finish(3)
    for j in range(1, COLS):
        vec_col(j).wait_recv()
        for n in range(4):
            col_copy(n, j).wait_recv()
    out_gath = local(gath, gath_h, 2)
    out_vec = local(vcol, vec_h, 3)
    out_gath.start()
    out_vec.start()

    for g in (g_tok, g_cot, g_dr):
        g.drain()
    for a in attended:
        for d in (*a.first, *a.rest, *a.hand):
            d.wait_send()
    each_row(lambda j: sparse_copy(j).wait_send())
    vec_one.wait_send()
    each_hi(lambda j: vec_three(j).wait_send())
    for n in range(4):
        slab_sent(n)
        for j in range(1, COLS):
            col_copy(n, j).wait_send()
    for j in range(1, COLS):
        exchange(j).wait_send()
        own_dilated(j).wait_send()
        vec_col(j).wait_send()
    out_copy.wait()
    gt_copy.wait()
    out_gath.wait()
    out_vec.wait()


def finale(
    rows_n, gath_h, vec_h, out_h, gt_h, out, gt, g1, b1, gq, bq, gk, gv, bv, go, bo, g2, b2, gu, bu, gd, bd,
    gath, vec, sems,
):
    copies = [
        pltpu.make_async_copy(src, dst, sems.at[i])
        for i, (src, dst) in enumerate(((gath_h, gath), (vec_h, vec), (out_h, out), (gt_h, gt)))
    ]
    for d in copies:
        d.start()
    share = 768 // rows_n
    r = lax.axis_index("row")
    copies[0].wait()
    part = [gath[s].astype(F32)[:share] for s in range(COLS)]

    def across(off, width):
        return jnp.concatenate([part[s][:, off : off + width] for s in range(COLS)], axis=1)

    gq[...] = across(1792, 192)
    gk[...] = across(1792 + 192, 192)
    gv[...] = across(1792 + 384, 192)
    go[...] = across(1536, 192)
    gu[...] = jnp.concatenate(
        [part[s][:, 768 + share * t : 768 + share * t + share] for t in range(rows_n) for s in range(COLS)], axis=1
    )
    for s in range(COLS):
        gd[share * s : share * s + share, :] = part[s][:, 0:768]
    copies[1].wait()
    summed = vec[0] + vec[1] + vec[2] + vec[3]
    wide = max(128, -(-share // 128) * 128)
    f, j = iota((768, wide), 0), iota((768, wide), 1)
    pick = onehot((f == share * r + j) & (j < share))
    mine = vec[0]
    total = moved(jnp.concatenate([summed[0:8], mine[0:8]], axis=0), pick)
    hidden = [moved(vec[s][0:8], pick) for s in range(COLS)]
    qv = [None, None]
    for n, off in enumerate((0, 384)):
        for s in range(COLS):
            place = onehot((f + 192 * s - off == share * r + j) & (j < share) & (f >= off) & (f < off + 192))
            term = moved(vec[s][0:8], place)
            qv[n] = term if qv[n] is None else qv[n] + term
    g1[...] = total[0, :share]
    b1[...] = total[1, :share]
    bo[...] = total[8 + 2, :share]
    g2[...] = total[3, :share]
    b2[...] = total[4, :share]
    bd[...] = total[8 + 5, :share]
    bq[...] = qv[0][7, :share]
    bv[...] = qv[1][7, :share]
    bu[...] = jnp.concatenate([hidden[s][6:7, :share] for s in range(COLS)], axis=1)[0]
    copies[2].wait()
    copies[3].wait()


def body(rows_n, tokens, norm1_gain, norm1_bias, w_query, b_query, w_key, w_value, b_value, w_out, b_out,
         norm2_gain, norm2_bias, w_up, b_up, w_down, b_down, slide_padded_units, padding_shortfall, cotangent):
    his, share = rows_n // 4, 768 // rows_n
    padded = -(-share // 16) * 16
    c = lax.axis_index("col")
    down_q = w_down
    if share % 16:
        down_q = lax.dynamic_index_in_dim(w_down.reshape(rows_n, COLS, share, 768), c, 1, False).reshape(768, 768)
    vmem = pltpu.VMEM
    dma = pltpu.SemaphoreType.DMA
    between = max(his - 1, 1)
    keep = rows_n <= 8
    scratch = [
        vmem((768, 3072), BF16), vmem((3072, 768), BF16), vmem((768, 768), BF16), vmem((768, 768), BF16),
        vmem((768, 768), BF16), vmem((4, 256, 768), BF16),
        *[vmem((4, 256, 768), BF16) for _ in range(5)],
        vmem((6, 1040, 128), F32), vmem((2, 1024, 128), BF16), vmem((2, 1024, 128), BF16),
        vmem((2, 1024, 128), BF16), vmem((4, 4, 128, 256), BF16), vmem((4, 4, 64, 256), BF16),
        vmem((4, 4, 64, 256), BF16), vmem((4, 4, 8, 256), F32),
        vmem((16 if keep else 2, 1024, 256), BF16), vmem((1024, 256), F32), vmem((1024, 256), BF16),
        vmem((2, 1040, 128), F32), vmem((4, 2, 4, 256, 128), BF16),
        vmem((256, 768), F32), vmem((256, 768), F32), vmem((256, 768), F32),
        vmem((4, 4, 64, 256), F32), vmem((768, 768), BF16),
        *[vmem((rows_n * padded, w), BF16) for w in UNITS[:3]],
        *[vmem((2 * his * padded, w), BF16) for w in UNITS],
        *[vmem((his * padded, w), BF16) for w in UNITS],
        *[vmem((between, padded, w), BF16) for w in UNITS],
        vmem((4, padded, WIDTH), BF16),
        vmem((4, 16, 384), BF16), vmem((rows_n, 64, 384), BF16), vmem((2, 128, 256), BF16),
        vmem((2, 128, rows_n * 64), BF16), vmem((2, 128, 256), F32), vmem((rows_n - 1, 64, 384), BF16),
        vmem((16, 768), F32), vmem((16, 768), F32), vmem((2, 16, 768), F32), vmem((his, 16, 768), F32),
        vmem((4, 16, 768), F32), vmem((8, 768), F32), vmem((8, 768), F32),
        dma((24 + rows_n,)), dma((3, 3)), dma((3, 3)), dma((2, 9)), dma((2, 9)), dma((3,)), dma((3,)),
        dma((rows_n - 1,)), dma((rows_n - 1,)), dma((rows_n - 1,)), dma((rows_n - 1,)),
        dma((4,)), dma((4,)), dma((4,)), dma((4,)), dma((4, between)), dma((4, between)), dma((4, 3)), dma((4, 3)),
        dma((3,)), dma((3,)), dma((his + 1,)), dma((his + 1,)), dma((3,)), dma((3,)), dma((2,)),
    ]
    hbm = pl.BlockSpec(memory_space=pl.ANY)
    smem = pl.BlockSpec(memory_space=pltpu.SMEM)
    whole = pl.BlockSpec(memory_space=pltpu.VMEM)
    sds = jax.ShapeDtypeStruct
    out, gt, gath, vec, _ = pl.pallas_call(
        functools.partial(layer, rows_n, slide_padded_units.shape[0], keep),
        out_shape=(
            sds((256, 768), BF16), sds((256, 768), F32), sds((4, padded, WIDTH), BF16), sds((4, 16, 768), F32),
            sds((8, 128) if keep else (16, 1024, 256), BF16),
        ),
        in_specs=[smem, smem] + [whole] * 9 + [hbm] * 9,
        out_specs=(hbm,) * 5,
        scratch_shapes=scratch,
        compiler_params=pltpu.CompilerParams(
            collective_id=0, has_side_effects=True, vmem_limit_bytes=(992 if rows_n <= 8 else 1021) * 64 * 1024
        ),
        name="layer",
    )(slide_padded_units, padding_shortfall, norm1_gain, norm1_bias, b_query, b_value, b_out, norm2_gain, norm2_bias,
      b_down, b_up, tokens, cotangent, w_query, w_key, w_value, w_out, w_up, w_down,
      down_q)
    vec1 = sds((share,), F32)
    mat = sds((share, 768), F32)
    return pl.pallas_call(
        functools.partial(finale, rows_n),
        out_shape=(
            sds((256, 768), BF16), sds((256, 768), F32), vec1, vec1, mat, vec1, mat, mat, vec1, mat, vec1, vec1, vec1,
            sds((share, 3072), F32), sds((4 * share,), F32), sds((4 * share, 768), F32), vec1,
        ),
        in_specs=[hbm] * 4,
        out_specs=(whole,) * 17,
        scratch_shapes=[vmem((4, padded, WIDTH), BF16), vmem((4, 16, 768), F32), dma((4,))],
        compiler_params=pltpu.CompilerParams(vmem_limit_bytes=48 * 1024 * 1024),
        name="finale",
    )(gath, vec, out, gt)


def solution(mesh):
    tiles = P(("row", "col"), None)
    one, two = P("row"), P("row", None)
    return jax.shard_map(
        functools.partial(body, mesh.shape["row"]),
        mesh=mesh,
        in_specs=(tiles,) + (P(),) * 17 + (tiles,),
        out_specs=(tiles, tiles, one, one, two, one, two, two, one, two, one, one, one, two, one, two, one),
        check_vma=False,
    )
```

```python
import functools

import jax
import jax.numpy as jnp
from jax import lax
from jax.experimental import pallas as pl
from jax.experimental.pallas import tpu as pltpu
from jax.sharding import PartitionSpec as P

HEADS = 16
HEAD_DIM = 48
SLOT = 64
STRIDE = 16
PAD = 256
COLS = 4
LOCAL_HEADS = HEADS // COLS
EPS = 1e-05
NEG = -1e30
SCALE = HEAD_DIM**-0.5
SCALE2 = SCALE * 1.4426950408889634
MESH = pl.DeviceIdType.MESH
BF16 = jnp.bfloat16
F32 = jnp.float32
UNITS = (768, 512, 256, 256, 640)
OFFSETS = (0, 768, 1280, 1536, 1792)
DOWN, UP, UP_LAST, OUT, QKV = range(5)
WIDTH = 2432


def nn(left, right):
    return jnp.dot(left, right, preferred_element_type=F32)


def nt(left, right):
    return lax.dot_general(left, right, (((1,), (1,)), ((), ())), preferred_element_type=F32)


def tn(left, right):
    return lax.dot_general(left, right, (((0,), (0,)), ((), ())), preferred_element_type=F32)


def iota(shape, dim):
    return lax.broadcasted_iota(jnp.int32, shape, dim)


def onehot(test):
    return jnp.where(test, 1.0, 0.0).astype(BF16)


def moved(values, chooser, parts=3):
    total = None
    for i in range(parts):
        low = values.astype(BF16)
        term = nn(low, chooser)
        total = term if total is None else total + term
        if i < parts - 1:
            values = values - low.astype(F32)
    return total


def normalise(x):
    centred = x - jnp.mean(x, axis=-1, keepdims=True)
    inverse = lax.rsqrt(jnp.mean(centred * centred, axis=-1, keepdims=True) + EPS)
    return centred * inverse, inverse


def norm_back(grad, unit, inverse, gain):
    scaled = grad * gain
    mean_one = jnp.mean(scaled, axis=-1, keepdims=True)
    mean_two = jnp.mean(scaled * unit, axis=-1, keepdims=True)
    return inverse * (scaled - mean_one - unit * mean_two)


def gelu_parts(u):
    z = jnp.abs(u) * 0.7071067811865476
    e = jnp.exp(-z * z)
    t = 1.0 / (1.0 + 0.3275911 * z)
    poly = t * (0.254829592 + t * (-0.284496736 + t * (1.421413741 + t * (-1.453152027 + t * 1.061405429))))
    tail = 0.5 * poly * e
    phi = jnp.where(u >= 0, 1.0 - tail, tail)
    return u * phi, phi + u * e * 0.3989422804014327


def colsum(x):
    return jnp.sum(x, axis=0, keepdims=True)


def layer(
    rows_n, slides_n, keep,
    slide_units, shortfall, v0, v1, v2, v3, v4, v5, v6, v7, v8, tok_h, cot_h, wq_h, wk_h, wv_h, wo_h, wup_h, wdn_h, wdq_h,
    out_h, gt_h, gath_h, vec_h, p_h,
    wup, wdn, wqkv, wupq, wdq, wop,
    tok, gb, a1, a2, drb,
    qf, qrow, kaug, vaug, qtm, kt, vta, sdr,
    pbuf, sref, dsb, oa, att,
    y1, acc, da2, dqt, dqr,
    slab0, slab1, slab2, slab3, ra0, ra1, ra2, ra3, ra4, rb0, rb1, rb2, rb3, rb4, rc0, rc1, rc2, rc3, rc4, gath,
    kvo, kvc, qsel, wb, dqb, dkvr,
    par, vec, vin, vrow, vcol, bupq, bqkv,
    lsem, gss, gsr, afs, afr, kos, kor, sps, spr, bss, bsr, u1s, u1r, u2s, u2r, u3s, u3r, ucs, ucr, ats, atr,
    vss, vsr, vcs, vcr, psem,
):
    his = rows_n // 4
    share = 768 // rows_n
    r = lax.axis_index("row")
    c = lax.axis_index("col")
    sib = c + 1 - 2 * (c % 2)
    across = (c + 2) % COLS
    diag = (sib + 2) % COLS
    hi, lo, bit = r // 4, (r // 2) % 2, r % 2
    recv_a, recv_b, recv_c = (ra0, ra1, ra2, ra3, ra4), (rb0, rb1, rb2, rb3, rb4), (rc0, rc1, rc2, rc3, rc4)
    slabs = (slab0, slab1, slab2, slab3, wdn.at[pl.ds(0, slab0.shape[0]), pl.ds(0, UNITS[QKV])])
    tall = slab0.shape[0] // rows_n
    key_count = rows_n * 64

    def local(src, dst, i):
        return pltpu.make_async_copy(src, dst, lsem.at[i])

    in_tok = local(tok_h, tok.at[c], 0)
    in_cot = local(cot_h, gb.at[c], 1)
    in_qkv = [local(h, wdn.at[pl.ds(768 * i, 768), :], 2 + i) for i, h in enumerate((wq_h, wk_h, wv_h))]
    in_up = local(wup_h, wup, 5)
    in_dn = local(wdn_h, wdn, 6)
    if share % 16 == 0:
        in_dq = [
            local(wdq_h.at[pl.ds(4 * share * t + share * c, share), :], wdq.at[pl.ds(share * t, share), :], 24 + t)
            for t in range(rows_n)
        ]
    else:
        in_dq = [local(wdq_h, wdq, 24)]
    in_wo = [
        local(wo_h.at[pl.ds(192 * s + 48 * h, 48), :], wop.at[s, pl.ds(64 * h, 48), :], 8 + 4 * s + h)
        for s in range(4)
        for h in range(4)
    ]
    in_tok.start()
    in_cot.start()
    for d in in_qkv:
        d.start()

    bar = pltpu.get_barrier_semaphore()
    for j in range(1, COLS):
        pl.semaphore_signal(bar, inc=1, device_id=(r, (c + j) % COLS), device_id_type=MESH)

    def greet(j, carry):
        pl.semaphore_signal(bar, inc=1, device_id=((r + j) % rows_n, c), device_id_type=MESH)
        return carry

    lax.fori_loop(1, rows_n, greet, 0)
    pl.semaphore_wait(bar, COLS - 1 + rows_n - 1)

    def remote(src, dst, send, recv, dev):
        return pltpu.make_async_remote_copy(
            src_ref=src, dst_ref=dst, send_sem=send, recv_sem=recv, device_id=dev, device_id_type=MESH
        )

    class Gather:
        def __init__(self, n, slot):
            self.near = remote(slot(c), slot(c), gss.at[n, 0], gsr.at[n, 0], (r, sib))
            self.far = remote(slot(c), slot(c), gss.at[n, 1], gsr.at[n, 1], (r, across))
            self.hand = remote(slot(across), slot(across), gss.at[n, 2], gsr.at[n, 2], (r, sib))

        def start(self):
            self.far.start()
            self.near.start()

        def forward(self):
            self.far.wait_recv()
            self.hand.start()

        def drain(self):
            self.near.wait_send()
            self.far.wait_send()
            self.hand.wait_send()

    g_tok = Gather(0, lambda i: tok.at[i])
    g_cot = Gather(1, lambda i: gb.at[i])
    g_dr = Gather(2, lambda i: drb.at[i])

    class Attended:
        def __init__(self, p):
            def copy(n, owner, block, dev):
                ref = att.at[owner, p] if block is None else att.at[owner, p, block]
                return remote(ref, ref, afs.at[p, n], afr.at[p, n], (r, dev))

            self.first = [copy(0, c, None, sib), copy(1, c, across, across), copy(2, c, diag, diag)]
            self.rest = [copy(3, c, diag, across), copy(4, c, c, across), copy(5, c, sib, across)]
            self.hand = [copy(6, across, c, sib), copy(7, across, across, sib), copy(8, across, diag, sib)]

    attended = [Attended(p) for p in range(2)]

    in_tok.wait()
    g_tok.start()
    for i, v in enumerate((v0, v1, v2, v3, v4, v5, v6, v7)):
        par[i : i + 1, :] = v[...].reshape(1, 768)
    for i in range(4):
        par[8 + i : 9 + i, :] = v8[768 * i : 768 * i + 768].reshape(1, 768)

    ends, lims = [], []
    total = jnp.int32(0)
    for s in range(slides_n):
        total = total + slide_units[s] * PAD
        ends.append(total)
        lims.append(total - shortfall[s])

    def label_of(pos):
        lab = jnp.zeros(pos.shape, jnp.int32)
        for s in range(slides_n - 1):
            lab = lab + jnp.where(pos >= ends[s], 1, 0)
        return lab

    def code_of(pos):
        code = label_of(pos)
        for s in range(slides_n):
            code = jnp.where((pos >= lims[s]) & (pos < ends[s]), -1, code)
        return code

    seg_first = r * 1024

    vec[...] = jnp.zeros(vec.shape, F32)
    for s in range(4):
        for h in range(4):
            wop[s, 64 * h + 48 : 64 * h + 64, :] = jnp.zeros((16, 768), BF16)
    sel_f, sel_j = iota((768, 256), 0), iota((768, 256), 1)
    head_sel = onehot((sel_f == 192 * c + 48 * (sel_j >> 6) + (sel_j & 63)) & ((sel_j & 63) < 48))
    for i, d in enumerate(in_qkv):
        d.wait()
        wqkv[:, 256 * i : 256 * i + 256] = nn(wdn[768 * i : 768 * i + 768, :], head_sel).astype(BF16)
    in_up.start()
    for d in in_wo:
        d.start()
    bqkv[...] = jnp.zeros(bqkv.shape, F32)
    biases = moved(par[0:8, :], head_sel)
    bqkv[0:1, 0:256] = biases[2:3]
    bqkv[0:1, 512:768] = biases[3:4]

    def first_norm(b):
        unit, _ = normalise(tok[b].astype(F32))
        a1[b] = (unit * par[0:1, :] + par[1:2, :]).astype(BF16)

    first_norm(c)
    on_head = (iota((256, 768), 0) & (STRIDE - 1)) == ((iota((256, 768), 1) * 1366) >> 16)

    def dilated(values):
        return jnp.sum(jnp.where(on_head, values.astype(BF16).astype(F32), 0.0).reshape(16, 16, 768), axis=1)

    k_sel = dilated(nn(a1[c], wdn[768:1536, :]))
    v_sel = dilated(nn(a1[c], wdn[1536:2304, :]) + par[3:4, :])
    for s in range(COLS):
        kvo[s] = jnp.concatenate(
            [k_sel[:, 192 * s : 192 * s + 192], v_sel[:, 192 * s : 192 * s + 192]], axis=1
        ).astype(BF16)
    own16 = pl.ds(pl.multiple_of(16 * c, 16), 16)

    def own_dilated(j):
        to = (c + j) % COLS
        return remote(kvo.at[to], kvc.at[r, own16, :], kos.at[j - 1], kor.at[j - 1], (r, to))

    for j in range(1, COLS):
        own_dilated(j).start()
    kvc[r, own16, :] = kvo[c]
    in_cot.wait()
    g_cot.start()
    in_dn.start()
    for d in in_dq:
        d.start()

    def qkv_block(b):
        low = a1[b]
        y = (nn(low, wqkv[...]) + bqkv[0:1, :]).astype(BF16).astype(F32)
        at = pl.ds(pl.multiple_of(256 * b, 256), 256)
        for i in range(6):
            qf[i, at, :] = y[:, 128 * i : 128 * i + 128]
        lane = iota((256, 128), 1) & 63
        key_code = code_of(seg_first + 256 * b + iota((256, 128), 0))
        key_mark = jnp.where(key_code == lane - 48, 0.0, NEG)
        marked = (lane >= 48) & (lane < 48 + slides_n)
        for p in range(2):
            qrow[p, at, :] = y[:, 128 * p : 128 * p + 128].astype(BF16)
            kaug[p, at, :] = jnp.where(marked, key_mark, y[:, 256 + 128 * p : 384 + 128 * p]).astype(BF16)
            vaug[p, at, :] = jnp.where(
                (lane == 48) | (lane == 49), 1.0, y[:, 512 + 128 * p : 640 + 128 * p]
            ).astype(BF16)
        qt, ktv, vt = y[:, :256].T, y[:, 256:512].T, y[:, 512:].T
        row = iota((128, 256), 0)
        query_label = label_of(seg_first + 256 * b + iota((128, 256), 1))
        mark = jnp.where(query_label == (row & 63) - 48, 1.0, 0.0)
        for h in range(4):
            p, half = h // 2, h % 2
            own = (row >> 6) == half
            full = jnp.where((row & 63) < 48, qt[128 * p : 128 * p + 128], mark)
            qtm[h, b] = jnp.where(own, full, 0.0).astype(BF16)
            hq, hk, hv = (m[64 * h : 64 * h + 64] for m in (qt, ktv, vt))
            kt[h, b] = hk.astype(BF16)
            vta[h, b] = jnp.where(iota((64, 256), 0) == 48, 1.0, hv).astype(BF16)
            sdr[h, b] = jnp.broadcast_to(colsum(hq * hk) * SCALE2, (8, 256))

    def sparse_copy(j):
        return remote(kvc.at[r], kvc.at[r], sps.at[j - 1], spr.at[j - 1], ((r + j) % rows_n, c))

    def each_row(fn):
        def step(j, carry):
            fn(j)
            return carry

        lax.fori_loop(1, rows_n, step, 0)

    qkv_block(c)
    g_tok.near.wait_recv()
    first_norm(sib)
    qkv_block(sib)
    for j in range(1, COLS):
        own_dilated(j).wait_recv()
    each_row(lambda j: sparse_copy(j).start())

    g_tok.forward()
    first_norm(across)
    qkv_block(across)
    g_tok.hand.wait_recv()
    first_norm(diag)
    qkv_block(diag)

    def picked(i, h):
        return qf[i, pl.ds(LOCAL_HEADS * c + h, 64, stride=STRIDE), :]

    def both_picked(i, p):
        lane = iota((64, 128), 1)
        return jnp.concatenate(
            [jnp.where((lane >> 6) == half, picked(i, 2 * p + half), 0.0) for half in range(2)], axis=0
        ).astype(BF16)

    def placing(p, first, transposed=False):
        shape = (256, 128) if transposed else (128, 256)
        wide, narrow = iota(shape, 0 if transposed else 1), iota(shape, 1 if transposed else 0)
        return onehot(((narrow & 63) < 48) & (wide == first + 48 * (2 * p + (narrow >> 6)) + (narrow & 63)))

    for p in range(2):
        qsel[p] = nn(both_picked(p, p), placing(p, 0)).astype(BF16)

    eye = iota((256, 256), 0) == iota((256, 256), 1)

    def weights_out(i):
        return pltpu.make_async_copy(pbuf.at[i % 2], p_h.at[i], psem.at[i % 2])

    def forward_tile(i):
        h, ib = i // 4, i % 4
        p, half = h // 2, h % 2
        slot = i if keep else i % 2
        rhs = qtm[h, ib]
        top = jnp.full((8, 256), NEG * 10, F32)
        for jb in range(4):
            s = nn(kaug[p, 256 * jb : 256 * jb + 256, :], rhs) * SCALE2
            sref[256 * jb : 256 * jb + 256, :] = s
            top = jnp.maximum(top, jnp.max(s.reshape(32, 8, 256), axis=0))
        own = sdr[h, ib]
        top = jnp.max(jnp.maximum(top, own), axis=0, keepdims=True)
        at = pl.ds(pl.multiple_of(256 * ib, 256), 256)
        sref[at, :] = jnp.where(eye, own[0:1], sref[at, :])

        if not keep:

            @pl.when(i >= 2)
            def _():
                weights_out(i).wait()

        for jb in range(4):
            pbuf[slot, 256 * jb : 256 * jb + 256, :] = jnp.exp2(
                sref[256 * jb : 256 * jb + 256, :] - top
            ).astype(BF16)
        if not keep:
            weights_out(i).start()
        values = jnp.concatenate([vta[h, jb] for jb in range(4)], axis=1)
        o = nn(values, pbuf[slot])
        z = o[48:49]
        inverse = 1.0 / z
        line = iota((64, 256), 0)
        o = o * inverse
        o = jnp.where(line == 48, inverse, jnp.where(line == 49, top, jnp.where(line == 50, z, o)))
        dqt[half, ib] = o

    def branch_b(p):
        lane = iota((64, 128), 1)
        s = nt(qsel[p], kvc[:, :, 0:256].reshape(key_count, 256)) * SCALE2
        masked = []
        for half in range(2):
            first = LOCAL_HEADS * c + 2 * p + half
            qpos = seg_first + STRIDE * iota((64, 128), 0)[:, 0:1] + first
            kpos = STRIDE * iota((8, key_count), 1)[0:1] + first
            allowed = (label_of(qpos) == code_of(kpos)) | (qpos == kpos)
            masked.append(jnp.where(allowed, s[64 * half : 64 * half + 64], NEG))
        s = jnp.concatenate(masked, axis=0)
        tops = jnp.max(s, axis=1, keepdims=True)
        e = jnp.exp2(s - tops)
        sums = jnp.sum(e, axis=1, keepdims=True)
        outs = moved(nn(e.astype(BF16), kvc[:, :, 128:384].reshape(key_count, 256)), placing(p, 64, True))
        factors = []
        for half in range(2):
            rows = slice(64 * half, 64 * half + 64)
            top_b, z_b, o_b = tops[rows], sums[rows], outs[rows]
            at = pl.ds(LOCAL_HEADS * c + 2 * p + half, 64, stride=STRIDE)
            old = oa[p, at, :]
            top_a = old[:, 64 * half + 49 : 64 * half + 50]
            z_a = old[:, 64 * half + 50 : 64 * half + 51]
            top = jnp.maximum(top_a, top_b)
            in_a, in_b = jnp.exp2(top_a - top), jnp.exp2(top_b - top)
            inverse = 1.0 / (in_a * z_a + in_b * z_b)
            o = (in_a * z_a * old + in_b * o_b) * inverse
            own = (lane >> 6) == half
            oa[p, at, :] = jnp.where(
                own & ((lane & 63) < 48), o, jnp.where(lane == 64 * half + 48, in_a * inverse, old)
            )
            factors.append(in_b * inverse)
        wb[p] = (e * jnp.concatenate(factors, axis=0)).astype(BF16)

    lane256 = iota((256, 128), 1)
    for p in range(2):
        def fwd(t, carry, p=p):
            forward_tile(8 * p + t)
            return carry

        lax.fori_loop(0, 8, fwd, 0)
        for ib in range(4):
            oa[p, 256 * ib : 256 * ib + 256, :] = jnp.concatenate([dqt[0, ib], dqt[1, ib]], axis=0).T
        if p == 0:
            each_row(lambda j: sparse_copy(j).wait_recv())
        else:
            g_cot.forward()
        branch_b(p)
        for ib in range(4):
            att[c, p, ib] = jnp.where(
                (lane256 & 63) < 48, oa[p, 256 * ib : 256 * ib + 256, :], 0.0
            ).astype(BF16)
        for d in attended[p].first:
            d.start()
    if not keep:
        weights_out(14).wait()
        weights_out(15).wait()
    for a in attended:
        for d in a.rest:
            d.start()

    in_up.wait()
    for n in range(3):
        start = (4 * share * ((256 * n) // share)) // 128 * 128
        stop = -(-(4 * share * ((256 * n + 255) // share + 1)) // 128) * 128
        o = 256 * n + iota((stop - start, 256), 1)
        group = jnp.zeros_like(o)
        for t in range(1, rows_n):
            group = group + jnp.where(o >= share * t, 1, 0)
        unit_sel = onehot(start + iota((stop - start, 256), 0) == 3 * share * group + share * c + o)
        for m in range(3):
            wupq[256 * m : 256 * m + 256, 256 * n : 256 * n + 256] = nn(
                wup[256 * m : 256 * m + 256, start:stop], unit_sel
            ).astype(BF16)
        pieces = [par[8 + t : 9 + t, :] for t in range(4)]
        line = jnp.concatenate(pieces, axis=1)[:, start:stop]
        bupq[0:8, 256 * n : 256 * n + 256] = moved(jnp.broadcast_to(line, (8, stop - start)), unit_sel)

    g_cot.near.wait_recv()
    g_cot.hand.wait_recv()
    vec[5:6, :] = colsum(gb[...].reshape(1024, 768).astype(F32))
    for d in in_wo:
        d.wait()
    for a in attended:
        for d in a.first:
            d.wait_recv()

    def project(b):
        out = tok[b].astype(F32) + par[4:5, :]
        for s in range(4):
            out = out + nn(jnp.concatenate([att[s, 0, b], att[s, 1, b]], axis=1), wop[s])
        return out

    def second_norm(b, values):
        unit, inverse = normalise(values)
        a2[b] = (unit * par[5:6, :] + par[6:7, :]).astype(BF16)
        return unit, inverse

    y1[...] = project(c)
    second_norm(c, y1[...])

    in_dn.wait()
    acc[...] = y1[...] + par[7:8, :]
    da2[...] = jnp.zeros(da2.shape, F32)

    def mlp(i, carry):
        low = a2[c]
        g = gb[c]
        at = pl.ds(pl.multiple_of(768 * i, 768), 768)
        u = nn(low, wup[:, at]) + par[pl.ds(8 + i, 1), :]
        hidden, slope = gelu_parts(u)
        acc[...] += nn(hidden.astype(BF16), wdn[at, :])
        du = (nt(g, wdn[at, :]) * slope).astype(BF16)
        da2[...] += nt(du, wup[:, at])
        return carry

    lax.fori_loop(0, 4, mlp, 0)
    for a in attended:
        for d in a.rest:
            d.wait_recv()
        for d in a.hand:
            d.start()
    wqkv[0:256, :] = acc[...].astype(BF16)
    out_copy = local(wqkv.at[pl.ds(0, 256), :], out_h, 0)
    out_copy.start()
    unit, inverse = normalise(y1[...])
    vec[3:4, :] = colsum(da2[...] * unit)
    vec[4:5, :] = colsum(da2[...])
    dy1 = gb[c].astype(F32) + norm_back(da2[...], unit, inverse, par[5:6, :])
    y1[...] = dy1
    drb[c] = dy1.astype(BF16)
    g_dr.start()

    for a in attended:
        for d in a.hand:
            d.wait_recv()
    for j in range(1, 4):
        b = (c + j) % 4
        second_norm(b, project(b))
    for d in in_dq:
        d.wait()

    def quarter(b, carry):
        u = nn(a2[b], wupq[...]) + bupq[0:1, :]
        hidden, slope = gelu_parts(u)
        at = pl.ds(pl.multiple_of(256 * b, 256), 256)
        wdn[at, :] = hidden.astype(BF16)
        du = (nt(gb[b], wdq[...]) * slope).astype(BF16)
        wdn[pl.ds(pl.multiple_of(1024 + 256 * b, 256), 256), :] = du
        vec[6:7, :] += colsum(du.astype(F32))
        return carry

    lax.fori_loop(0, 4, quarter, 0)

    def slab_at(b, l, h):
        return ((2 * b + l) * his + h) * tall

    def put(n, block, first):
        buf = slabs[n]
        width = block.shape[1]
        at = first
        while at < first + block.shape[0]:
            which, off = at // share, at % share
            size = min(share - off, first + block.shape[0] - at)
            row = slab_at(which % 2, (which // 2) % 2, which // 4) + off
            buf[row : row + size, 0:width] = block[at - first : at - first + size].astype(BF16)
            at += size

    def one(n):
        half = 2 * his * tall
        at = pl.ds(pl.multiple_of((1 - bit) * half, half), half)
        return remote(slabs[n].at[at, :], recv_a[n], u1s.at[n], u1r.at[n], (r + 1 - 2 * bit, c))

    def two(n):
        at = pl.ds(pl.multiple_of(slab_at(bit, 1 - lo, 0), his * tall), his * tall)
        return remote(slabs[n].at[at, :], recv_b[n], u2s.at[n], u2r.at[n], (r + 2 - 4 * lo, c))

    def slab(l, h):
        return pl.ds(pl.multiple_of(slab_at(bit, l, h), tall), tall)

    def three(n, j):
        to = (hi + j) % his
        return remote(
            slabs[n].at[slab(lo, to), :], recv_c[n].at[j - 1], u3s.at[n, j - 1], u3r.at[n, j - 1],
            (4 * to + 2 * lo + bit, c),
        )

    def each_hi(fn):
        def step(j, carry):
            fn(j)
            return carry

        lax.fori_loop(1, his, step, 0)

    def start_two(n):
        one(n).wait_recv()

        def add(i, carry):
            for l in range(2):
                at = pl.ds(pl.multiple_of((l * his + i) * tall, tall), tall)
                slabs[n][slab(l, i), :] = (slabs[n][slab(l, i), :].astype(F32) + recv_a[n][at, :].astype(F32)).astype(BF16)
            return carry

        lax.fori_loop(0, his, add, 0)
        two(n).start()

    def start_three(n):
        two(n).wait_recv()

        def add(i, carry):
            at = pl.ds(pl.multiple_of(i * tall, tall), tall)
            slabs[n][slab(lo, i), :] = (slabs[n][slab(lo, i), :].astype(F32) + recv_b[n][at, :].astype(F32)).astype(BF16)
            return carry

        lax.fori_loop(0, his, add, 0)
        each_hi(lambda j: three(n, j).start())

    def slab_sent(n):
        one(n).wait_send()
        two(n).wait_send()
        each_hi(lambda j: three(n, j).wait_send())

    def col_copy(n, j):
        at = pl.ds(OFFSETS[n], UNITS[n])
        return remote(gath.at[c, :, at], gath.at[c, :, at], ucs.at[n, j - 1], ucr.at[n, j - 1], (r, (c + j) % COLS))

    def finish(n):
        each_hi(lambda j: three(n, j).wait_recv())
        gath[c, :, OFFSETS[n] : OFFSETS[n] + UNITS[n]] = (
            lax.fori_loop(
                0, his - 1, lambda j, t: t + recv_c[n][j].astype(F32), slabs[n][slab(lo, hi), :].astype(F32)
            )
        ).astype(BF16)
        for j in range(1, COLS):
            col_copy(n, j).start()

    for m in range(2):
        put(DOWN, tn(wdn[0:1024, 384 * m : 384 * m + 384], gb[...].reshape(1024, 768)), 384 * m)
    one(DOWN).start()
    g_dr.forward()
    for m in range(2):
        lanes = jnp.concatenate([a2[b, :, 384 * m : 384 * m + 384] for b in range(4)], axis=0)
        block = tn(lanes, wdn[1024:2048, :])
        put(UP, block[:, 0:512], 384 * m)
        put(UP_LAST, block[:, 512:768], 384 * m)

    g_dr.near.wait_recv()
    g_dr.hand.wait_recv()
    vec[2:3, :] = colsum(drb[...].reshape(1024, 768).astype(F32))
    bones = onehot((iota((256, 256), 0) >> 6) == (iota((256, 256), 1) >> 6))

    def out_grad(b, carry):
        lane = iota((256, 256), 1) & 63
        at = pl.ds(pl.multiple_of(256 * b, 256), 256)
        d_att = nt(drb[b], wop[c]).astype(BF16).astype(F32)
        mine = jnp.concatenate([att[c, 0, b], att[c, 1, b]], axis=1).astype(F32)
        rowsum = moved(d_att * mine, bones, 2)
        factor = moved(
            jnp.where(lane == 48, jnp.concatenate([oa[0, at, :], oa[1, at, :]], axis=1), 0.0), bones
        )
        minus = -rowsum * factor
        high = minus.astype(BF16).astype(F32)
        marked = jnp.where(lane == 48, high, jnp.where(lane == 49, minus - high, d_att * factor))
        flipped = marked.T
        line = iota((128, 256), 0)
        for p in range(2):
            kaug[p, at, :] = marked[:, 128 * p : 128 * p + 128].astype(BF16)
            qf[p, at, :] = d_att[:, 128 * p : 128 * p + 128]
            qf[2 + p, at, :] = rowsum[:, 128 * p : 128 * p + 128]
        for h in range(4):
            p = h // 2
            qtm[h, b] = jnp.where(
                (line >> 6) == h % 2, flipped[128 * p : 128 * p + 128], 0.0
            ).astype(BF16)
        return carry

    lax.fori_loop(0, 4, out_grad, 0)

    own_cols = onehot(
        (iota((256, 768), 1) == 192 * c + iota((256, 768), 0)) & (iota((256, 768), 0) < 192)
    )
    dr_own = jnp.concatenate([nt(own_cols, drb[b]).astype(BF16) for b in range(4)], axis=1)
    for s in range(4):
        both = jnp.concatenate(
            [att[s, 0].reshape(1024, 128), att[s, 1].reshape(1024, 128)], axis=1
        )
        block = nn(dr_own, both).T
        for h in range(4):
            put(OUT, block[64 * h : 64 * h + 48], 192 * s + 48 * h)

    step_rows = min(rows_n, 8)
    step_keys = 64 * step_rows

    def dilated_block(t):
        tall, wide = pl.multiple_of(64 * (t // 8), 64), pl.multiple_of(384 * (t % 8), 384)
        return wup.at[pl.ds(tall, 64), pl.ds(wide, 384)]

    d_sel, sums = [], []
    for p in range(2):
        d_sel.append(nn(both_picked(p, p), placing(p, 64)).astype(BF16))
        sums.append(
            jnp.concatenate([picked(2 + p, 2 * p + i)[:, 64 * i : 64 * i + 1] for i in range(2)], axis=0)
        )
    dqb[...] = jnp.zeros(dqb.shape, F32)

    def some_keys(n, carry):
        some = pl.ds(pl.multiple_of(step_rows * n, step_rows), step_rows)
        k2 = kvc[some, :, 0:256].reshape(step_keys, 256)
        v2 = kvc[some, :, 128:384].reshape(step_keys, 256)
        dk, dv = 0.0, 0.0
        for p in range(2):
            w = wb[p, :, pl.ds(pl.multiple_of(step_keys * n, step_keys), step_keys)]
            ds = (w.astype(F32) * (nt(d_sel[p], v2) - sums[p])).astype(BF16)
            dqb[p] += nn(ds, k2)
            dk = dk + tn(ds, qsel[p])
            dv = dv + tn(w, d_sel[p])
        for t in range(step_rows):
            block = dilated_block(step_rows * n + t)
            rows = slice(64 * t, 64 * t + 64)
            block[:, 0:128] = dk[rows, 0:128].astype(BF16)
            block[:, 128:256] = (dk[rows, 128:256] + dv[rows, 0:128]).astype(BF16)
            block[:, 256:384] = dv[rows, 128:256].astype(BF16)
        return carry

    lax.fori_loop(0, rows_n // step_rows, some_keys, 0)

    def dilated_copy(j):
        to = (r + j) % rows_n
        return remote(dilated_block(to), dkvr.at[j - 1], bss.at[j - 1], bsr.at[j - 1], (to, c))

    each_row(lambda j: dilated_copy(j).start())

    qf[...] = jnp.zeros(qf.shape, F32)

    def weights_in(i):
        return pltpu.make_async_copy(p_h.at[i], pbuf.at[i % 2], psem.at[i % 2])

    def backward_tile(i):
        h, ib = i // 4, i % 4
        p, half = h // 2, h % 2
        slot = i if keep else i % 2
        if not keep:
            weights_in(i).wait()

            @pl.when(i + 1 < 16)
            def _():
                weights_in(i + 1).start()

        rhs = qtm[h, ib]
        for jb in range(4):
            at = slice(256 * jb, 256 * jb + 256)
            dsb[at, :] = (pbuf[slot, at, :].astype(F32) * nn(vaug[p, at, :], rhs)).astype(BF16)
        keys = jnp.concatenate([kt[h, jb] for jb in range(4)], axis=1)
        dqt[h, ib] = nn(keys, dsb[...])
        at = pl.ds(pl.multiple_of(256 * ib, 256), 256)
        own = (iota((256, 128), 1) >> 6) == half
        d_rows, q_rows = kaug[p, at, :], qrow[p, at, :]
        for jb in range(4):
            js = slice(256 * jb, 256 * jb + 256)
            qf[2 + p, js, :] += jnp.where(own, nn(dsb[js, :], q_rows), 0.0)
            qf[4 + p, js, :] += jnp.where(own, nn(pbuf[slot, js, :], d_rows), 0.0)

    if not keep:
        weights_in(0).start()
    for first, last in ((0, 11), (11, 16)):
        def bwd(t, carry):
            backward_tile(t)
            return carry

        lax.fori_loop(first, last, bwd, 0)
        if first == 0:
            start_two(DOWN)
            one(UP).start()
            one(OUT).start()

    each_row(lambda j: dilated_copy(j).wait_recv())
    spread = lax.fori_loop(
        0, rows_n - 1, lambda j, t: t + dkvr[j].astype(F32), dilated_block(r)[...].astype(F32)
    )
    each_row(lambda j: dilated_copy(j).wait_send())
    back_qkv = [local(h, wup.at[:, pl.ds(768 * i, 768)], 2 + i) for i, h in enumerate((wq_h, wk_h, wv_h))]
    for d in back_qkv:
        d.start()
    source, slot = iota((384, 512), 0), iota((384, 512), 1)
    spread = moved(
        spread,
        onehot(((slot & 63) < 48) & (source == 192 * (slot >> 8) + 48 * ((slot & 255) >> 6) + (slot & 63))),
        2,
    )
    dq_b = [moved(dqb[p], placing(p, 0, True), 2) for p in range(2)]
    for h in range(4):
        p, rows = h // 2, slice(64 * (h % 2), 64 * (h % 2) + 64)
        own = (iota((64, 128), 1) >> 6) == h % 2
        at = pl.ds(LOCAL_HEADS * c + h, 64, stride=STRIDE)
        qf[p, at, :] += jnp.where(own, dq_b[p][rows], 0.0)
        qf[2 + p, at, :] += jnp.where(own, spread[:, 128 * p : 128 * p + 128], 0.0)
        qf[4 + p, at, :] += jnp.where(own, spread[:, 256 + 128 * p : 384 + 128 * p], 0.0)

    def turned(i, b):
        at = pl.ds(pl.multiple_of(256 * b, 256), 256)
        return jnp.concatenate([qf[2 * i, at, :], qf[2 * i + 1, at, :]], axis=1).T

    def compact(b, carry):
        dq = (jnp.concatenate([dqt[h, b] for h in range(4)], axis=0) + turned(0, b)) * SCALE
        for i, m in enumerate((dq, turned(1, b) * SCALE, turned(2, b))):
            for h in range(4):
                a2[b, 48 * h : 48 * h + 48, 256 * i : 256 * i + 256] = m[64 * h : 64 * h + 48].astype(BF16)
        return carry

    lax.fori_loop(0, 4, compact, 0)

    def exchange(j):
        to = (c + j) % COLS
        at = pl.ds(pl.multiple_of(192 * c, 64), 192)
        return remote(a2.at[to, pl.ds(0, 192), :], dqr.at[at, :], ats.at[j - 1], atr.at[j - 1], (r, to))

    for j in range(1, COLS):
        exchange(j).start()
    dqr[pl.ds(pl.multiple_of(192 * c, 64), 192), :] = a2[c, 0:192, :]
    rows576 = [
        jnp.concatenate(
            [a2[b, 0:192, 256 * i : 256 * i + 256] for i in range(3)] + [jnp.zeros((64, 256), BF16)], axis=0
        )
        for b in range(4)
    ]
    lhs = jnp.concatenate(rows576, axis=1)
    for m in range(2):
        lanes = jnp.concatenate([a1[b, :, 384 * m : 384 * m + 384] for b in range(4)], axis=0)
        put(QKV, nn(lhs, lanes).T, 384 * m)
    one(QKV).start()
    start_three(DOWN)
    ones = jnp.ones((16, 1024), BF16)
    vec[7:8, 0:640] = nt(ones, lhs)[0:1]
    start_two(UP)
    start_two(OUT)
    finish(DOWN)
    start_three(UP)

    for d in back_qkv:
        d.wait()
    for j in range(1, COLS):
        exchange(j).wait_recv()
    da1 = nn(wup[:, 0:768], dqr[:, 0:256])
    for i in range(1, 3):
        da1 = da1 + nn(wup[:, 768 * i : 768 * i + 768], dqr[:, 256 * i : 256 * i + 256])
    da1 = da1.T
    unit, inverse = normalise(tok[c].astype(F32))
    vec[0:1, :] = colsum(da1 * unit)
    vec[1:2, :] = colsum(da1)
    vec_one = remote(vec, vin.at[0], vss.at[0], vsr.at[0], (r + 1 - 2 * bit, c))
    vec_one.start()
    da2[...] = y1[...] + norm_back(da1, unit, inverse, par[0:1, :])
    gt_copy = local(da2, gt_h, 1)
    gt_copy.start()
    start_two(QKV)
    one(UP_LAST).start()
    start_three(OUT)
    vec_one.wait_recv()
    vcol[c] = vec[...] + vin[0]
    vec_two = remote(vcol.at[c], vin.at[1], vss.at[1], vsr.at[1], (r + 2 - 4 * lo, c))
    vec_two.start()
    finish(UP)
    start_two(UP_LAST)
    vec_two.wait_recv()
    vrow[hi] = vcol[c] + vin[1]

    def vec_three(j):
        to = (hi + j) % his
        return remote(vrow.at[hi], vrow.at[hi], vss.at[1 + j], vsr.at[1 + j], (4 * to + 2 * lo + bit, c))

    each_hi(lambda j: vec_three(j).start())
    finish(OUT)
    start_three(QKV)
    start_three(UP_LAST)
    each_hi(lambda j: vec_three(j).wait_recv())
    vec_two.wait_send()
    vcol[c] = lax.fori_loop(0, his, lambda j, t: t + vrow[j], jnp.zeros((16, 768), F32))

    def vec_col(j):
        return remote(vcol.at[c], vcol.at[c], vcs.at[j - 1], vcr.at[j - 1], (r, (c + j) % COLS))

    for j in range(1, COLS):
        vec_col(j).start()
    finish(QKV)
    finish(UP_LAST)
    for j in range(1, COLS):
        vec_col(j).wait_recv()
        for n in range(5):
            col_copy(n, j).wait_recv()
    out_gath = local(gath, gath_h, 2)
    out_vec = local(vcol, vec_h, 3)
    out_gath.start()
    out_vec.start()

    for g in (g_tok, g_cot, g_dr):
        g.drain()
    for a in attended:
        for d in (*a.first, *a.rest, *a.hand):
            d.wait_send()
    each_row(lambda j: sparse_copy(j).wait_send())
    vec_one.wait_send()
    each_hi(lambda j: vec_three(j).wait_send())
    for n in range(5):
        slab_sent(n)
        for j in range(1, COLS):
            col_copy(n, j).wait_send()
    for j in range(1, COLS):
        exchange(j).wait_send()
        own_dilated(j).wait_send()
        vec_col(j).wait_send()
    out_copy.wait()
    gt_copy.wait()
    out_gath.wait()
    out_vec.wait()


def finale(
    rows_n, gath_h, vec_h, out_h, gt_h, out, gt, g1, b1, gq, bq, gk, gv, bv, go, bo, g2, b2, gu, bu, gd, bd,
    gath, vec, sems,
):
    copies = [
        pltpu.make_async_copy(src, dst, sems.at[i])
        for i, (src, dst) in enumerate(((gath_h, gath), (vec_h, vec), (out_h, out), (gt_h, gt)))
    ]
    for d in copies:
        d.start()
    share = 768 // rows_n
    r = lax.axis_index("row")
    copies[0].wait()
    part = [gath[s].astype(F32)[:share] for s in range(COLS)]

    def across(off, width):
        return jnp.concatenate([part[s][:, off : off + width] for s in range(COLS)], axis=1)

    gq[...] = across(1792, 192)
    gk[...] = across(1792 + 192, 192)
    gv[...] = across(1792 + 384, 192)
    go[...] = across(1536, 192)
    gu[...] = jnp.concatenate(
        [part[s][:, 768 + share * t : 768 + share * t + share] for t in range(rows_n) for s in range(COLS)], axis=1
    )
    for s in range(COLS):
        gd[share * s : share * s + share, :] = part[s][:, 0:768]
    copies[1].wait()
    summed = vec[0] + vec[1] + vec[2] + vec[3]
    wide = max(128, -(-share // 128) * 128)
    f, j = iota((768, wide), 0), iota((768, wide), 1)
    pick = onehot((f == share * r + j) & (j < share))
    mine = vec[0]
    total = moved(jnp.concatenate([summed[0:8], mine[0:8]], axis=0), pick)
    hidden = [moved(vec[s][0:8], pick) for s in range(COLS)]
    qv = [None, None]
    for n, off in enumerate((0, 384)):
        for s in range(COLS):
            place = onehot((f + 192 * s - off == share * r + j) & (j < share) & (f >= off) & (f < off + 192))
            term = moved(vec[s][0:8], place)
            qv[n] = term if qv[n] is None else qv[n] + term
    g1[...] = total[0, :share]
    b1[...] = total[1, :share]
    bo[...] = total[8 + 2, :share]
    g2[...] = total[3, :share]
    b2[...] = total[4, :share]
    bd[...] = total[8 + 5, :share]
    bq[...] = qv[0][7, :share]
    bv[...] = qv[1][7, :share]
    bu[...] = jnp.concatenate([hidden[s][6:7, :share] for s in range(COLS)], axis=1)[0]
    copies[2].wait()
    copies[3].wait()


def body(rows_n, tokens, norm1_gain, norm1_bias, w_query, b_query, w_key, w_value, b_value, w_out, b_out,
         norm2_gain, norm2_bias, w_up, b_up, w_down, b_down, slide_padded_units, padding_shortfall, cotangent):
    his, share = rows_n // 4, 768 // rows_n
    padded = -(-share // 16) * 16
    c = lax.axis_index("col")
    down_q = w_down
    if share % 16:
        down_q = lax.dynamic_index_in_dim(w_down.reshape(rows_n, COLS, share, 768), c, 1, False).reshape(768, 768)
    vmem = pltpu.VMEM
    dma = pltpu.SemaphoreType.DMA
    between = max(his - 1, 1)
    keep = rows_n <= 8
    scratch = [
        vmem((768, 3072), BF16), vmem((3072, 768), BF16), vmem((768, 768), BF16), vmem((768, 768), BF16),
        vmem((768, 768), BF16), vmem((4, 256, 768), BF16),
        *[vmem((4, 256, 768), BF16) for _ in range(5)],
        vmem((6, 1040, 128), F32), vmem((2, 1024, 128), BF16), vmem((2, 1024, 128), BF16),
        vmem((2, 1024, 128), BF16), vmem((4, 4, 128, 256), BF16), vmem((4, 4, 64, 256), BF16),
        vmem((4, 4, 64, 256), BF16), vmem((4, 4, 8, 256), F32),
        vmem((16 if keep else 2, 1024, 256), BF16), vmem((1024, 256), F32), vmem((1024, 256), BF16),
        vmem((2, 1040, 128), F32), vmem((4, 2, 4, 256, 128), BF16),
        vmem((256, 768), F32), vmem((256, 768), F32), vmem((256, 768), F32),
        vmem((4, 4, 64, 256), F32), vmem((768, 768), BF16),
        *[vmem((rows_n * padded, w), BF16) for w in UNITS[:QKV]],
        *[vmem((2 * his * padded, w), BF16) for w in UNITS],
        *[vmem((his * padded, w), BF16) for w in UNITS],
        *[vmem((between, padded, w), BF16) for w in UNITS],
        vmem((4, padded, WIDTH), BF16),
        vmem((4, 16, 384), BF16), vmem((rows_n, 64, 384), BF16), vmem((2, 128, 256), BF16),
        vmem((2, 128, rows_n * 64), BF16), vmem((2, 128, 256), F32), vmem((rows_n - 1, 64, 384), BF16),
        vmem((16, 768), F32), vmem((16, 768), F32), vmem((2, 16, 768), F32), vmem((his, 16, 768), F32),
        vmem((4, 16, 768), F32), vmem((8, 768), F32), vmem((8, 768), F32),
        dma((24 + rows_n,)), dma((3, 3)), dma((3, 3)), dma((2, 9)), dma((2, 9)), dma((3,)), dma((3,)),
        dma((rows_n - 1,)), dma((rows_n - 1,)), dma((rows_n - 1,)), dma((rows_n - 1,)),
        dma((5,)), dma((5,)), dma((5,)), dma((5,)), dma((5, between)), dma((5, between)), dma((5, 3)), dma((5, 3)),
        dma((3,)), dma((3,)), dma((his + 1,)), dma((his + 1,)), dma((3,)), dma((3,)), dma((2,)),
    ]
    hbm = pl.BlockSpec(memory_space=pl.ANY)
    smem = pl.BlockSpec(memory_space=pltpu.SMEM)
    whole = pl.BlockSpec(memory_space=pltpu.VMEM)
    sds = jax.ShapeDtypeStruct
    out, gt, gath, vec, _ = pl.pallas_call(
        functools.partial(layer, rows_n, slide_padded_units.shape[0], keep),
        out_shape=(
            sds((256, 768), BF16), sds((256, 768), F32), sds((4, padded, WIDTH), BF16), sds((4, 16, 768), F32),
            sds((8, 128) if keep else (16, 1024, 256), BF16),
        ),
        in_specs=[smem, smem] + [whole] * 9 + [hbm] * 9,
        out_specs=(hbm,) * 5,
        scratch_shapes=scratch,
        compiler_params=pltpu.CompilerParams(
            collective_id=0, has_side_effects=True, vmem_limit_bytes=(992 if rows_n <= 8 else 1021) * 64 * 1024
        ),
        name="layer",
    )(slide_padded_units, padding_shortfall, norm1_gain, norm1_bias, b_query, b_value, b_out, norm2_gain, norm2_bias,
      b_down, b_up, tokens, cotangent, w_query, w_key, w_value, w_out, w_up, w_down,
      down_q)
    vec1 = sds((share,), F32)
    mat = sds((share, 768), F32)
    return pl.pallas_call(
        functools.partial(finale, rows_n),
        out_shape=(
            sds((256, 768), BF16), sds((256, 768), F32), vec1, vec1, mat, vec1, mat, mat, vec1, mat, vec1, vec1, vec1,
            sds((share, 3072), F32), sds((4 * share,), F32), sds((4 * share, 768), F32), vec1,
        ),
        in_specs=[pl.BlockSpec(memory_space=pltpu.HBM)] * 4,
        out_specs=(whole,) * 17,
        scratch_shapes=[vmem((4, padded, WIDTH), BF16), vmem((4, 16, 768), F32), dma((4,))],
        compiler_params=pltpu.CompilerParams(vmem_limit_bytes=1016 * 64 * 1024),
        name="finale",
    )(gath, vec, out, gt)


def solution(mesh):
    tiles = P(("row", "col"), None)
    one, two = P("row"), P("row", None)
    return jax.shard_map(
        functools.partial(body, mesh.shape["row"]),
        mesh=mesh,
        in_specs=(tiles,) + (P(),) * 17 + (tiles,),
        out_specs=(tiles, tiles, one, one, two, one, two, two, one, two, one, one, one, two, one, two, one),
        check_vma=False,
    )
```

```python
import functools

import jax
import jax.numpy as jnp
from jax import lax
from jax.experimental import pallas as pl
from jax.experimental.pallas import tpu as pltpu
from jax.sharding import PartitionSpec as P

HEADS = 16
HEAD_DIM = 48
SLOT = 64
STRIDE = 16
PAD = 256
COLS = 4
LOCAL_HEADS = HEADS // COLS
EPS = 1e-05
NEG = -1e30
SCALE = HEAD_DIM**-0.5
SCALE2 = SCALE * 1.4426950408889634
MESH = pl.DeviceIdType.MESH
BF16 = jnp.bfloat16
F32 = jnp.float32
UNITS = (768, 512, 256, 256, 384, 256)
OFFSETS = (0, 768, 1280, 1536, 1792, 2176)
DOWN, UP, UP_LAST, OUT, QK, VAL = range(6)
WIDTH = 2432


def nn(left, right):
    return jnp.dot(left, right, preferred_element_type=F32)


def nt(left, right):
    return lax.dot_general(left, right, (((1,), (1,)), ((), ())), preferred_element_type=F32)


def tn(left, right):
    return lax.dot_general(left, right, (((0,), (0,)), ((), ())), preferred_element_type=F32)


def iota(shape, dim):
    return lax.broadcasted_iota(jnp.int32, shape, dim)


def onehot(test):
    return jnp.where(test, 1.0, 0.0).astype(BF16)


def moved(values, chooser, parts=3):
    total = None
    for i in range(parts):
        low = values.astype(BF16)
        term = nn(low, chooser)
        total = term if total is None else total + term
        if i < parts - 1:
            values = values - low.astype(F32)
    return total


def normalise(x):
    centred = x - jnp.mean(x, axis=-1, keepdims=True)
    inverse = lax.rsqrt(jnp.mean(centred * centred, axis=-1, keepdims=True) + EPS)
    return centred * inverse, inverse


def norm_back(grad, unit, inverse, gain):
    scaled = grad * gain
    mean_one = jnp.mean(scaled, axis=-1, keepdims=True)
    mean_two = jnp.mean(scaled * unit, axis=-1, keepdims=True)
    return inverse * (scaled - mean_one - unit * mean_two)


def gelu_parts(u):
    z = jnp.abs(u) * 0.7071067811865476
    e = jnp.exp(-z * z)
    t = 1.0 / (1.0 + 0.3275911 * z)
    poly = t * (0.254829592 + t * (-0.284496736 + t * (1.421413741 + t * (-1.453152027 + t * 1.061405429))))
    tail = 0.5 * poly * e
    phi = jnp.where(u >= 0, 1.0 - tail, tail)
    return u * phi, phi + u * e * 0.3989422804014327


def colsum(x):
    return jnp.sum(x, axis=0, keepdims=True)


def layer(
    rows_n, slides_n, keep,
    slide_units, shortfall, v0, v1, v2, v3, v4, v5, v6, v7, v8, tok_h, cot_h, wq_h, wk_h, wv_h, wo_h, wup_h, wdn_h, wdq_h,
    out_h, gt_h, gath_h, vec_h, p_h,
    wup, wdn, wqkv, wupq, wdq, wop,
    tok, gb, a1, a2, drb,
    qf, qrow, kaug, vaug, qtm, kt, vta, sdr,
    pbuf, sref, dsb, oa, att,
    y1, acc, da2, dqt, dqr,
    slab0, slab1, slab2, slab3, ra0, ra1, ra2, ra3, ra4, ra5, rb0, rb1, rb2, rb3, rb4, rb5, rc0, rc1, rc2, rc3, rc4, rc5, gath,
    kvo, kvc, qsel, wb, dqb, dkvr,
    par, vec, vin, vrow, vcol, bupq, bqkv,
    lsem, gss, gsr, afs, afr, kos, kor, sps, spr, bss, bsr, u1s, u1r, u2s, u2r, u3s, u3r, ucs, ucr, ats, atr,
    vss, vsr, vcs, vcr, psem,
):
    his = rows_n // 4
    share = 768 // rows_n
    r = lax.axis_index("row")
    c = lax.axis_index("col")
    sib = c + 1 - 2 * (c % 2)
    across = (c + 2) % COLS
    diag = (sib + 2) % COLS
    hi, lo, bit = r // 4, (r // 2) % 2, r % 2
    recv_a, recv_b, recv_c = (ra0, ra1, ra2, ra3, ra4, ra5), (rb0, rb1, rb2, rb3, rb4, rb5), (rc0, rc1, rc2, rc3, rc4, rc5)
    slabs = (
        slab0, slab1, slab2, slab3,
        wdn.at[pl.ds(0, slab0.shape[0]), pl.ds(0, UNITS[QK])],
        wdn.at[pl.ds(0, slab0.shape[0]), pl.ds(UNITS[QK], UNITS[VAL])],
    )
    tall = slab0.shape[0] // rows_n
    key_count = rows_n * 64

    def local(src, dst, i):
        return pltpu.make_async_copy(src, dst, lsem.at[i])

    in_tok = local(tok_h, tok.at[c], 0)
    in_cot = local(cot_h, gb.at[c], 1)
    in_qkv = [local(h, wdn.at[pl.ds(768 * i, 768), :], 2 + i) for i, h in enumerate((wq_h, wk_h, wv_h))]
    in_up = local(wup_h, wup, 5)
    in_dn = local(wdn_h, wdn, 6)
    if share % 16 == 0:
        in_dq = [
            local(wdq_h.at[pl.ds(4 * share * t + share * c, share), :], wdq.at[pl.ds(share * t, share), :], 24 + t)
            for t in range(rows_n)
        ]
    else:
        in_dq = [local(wdq_h, wdq, 24)]
    in_wo = [
        local(wo_h.at[pl.ds(192 * s + 48 * h, 48), :], wop.at[s, pl.ds(64 * h, 48), :], 8 + 4 * s + h)
        for s in range(4)
        for h in range(4)
    ]
    in_tok.start()
    in_cot.start()
    for d in in_qkv:
        d.start()

    bar = pltpu.get_barrier_semaphore()
    for j in range(1, COLS):
        pl.semaphore_signal(bar, inc=1, device_id=(r, (c + j) % COLS), device_id_type=MESH)

    def greet(j, carry):
        pl.semaphore_signal(bar, inc=1, device_id=((r + j) % rows_n, c), device_id_type=MESH)
        return carry

    lax.fori_loop(1, rows_n, greet, 0)
    pl.semaphore_wait(bar, COLS - 1 + rows_n - 1)

    def remote(src, dst, send, recv, dev):
        return pltpu.make_async_remote_copy(
            src_ref=src, dst_ref=dst, send_sem=send, recv_sem=recv, device_id=dev, device_id_type=MESH
        )

    class Gather:
        def __init__(self, n, slot):
            self.near = remote(slot(c), slot(c), gss.at[n, 0], gsr.at[n, 0], (r, sib))
            self.far = remote(slot(c), slot(c), gss.at[n, 1], gsr.at[n, 1], (r, across))
            self.hand = remote(slot(across), slot(across), gss.at[n, 2], gsr.at[n, 2], (r, sib))

        def start(self):
            self.far.start()
            self.near.start()

        def forward(self):
            self.far.wait_recv()
            self.hand.start()

        def drain(self):
            self.near.wait_send()
            self.far.wait_send()
            self.hand.wait_send()

    g_tok = Gather(0, lambda i: tok.at[i])
    g_cot = Gather(1, lambda i: gb.at[i])
    g_dr = Gather(2, lambda i: drb.at[i])

    class Attended:
        def __init__(self, p):
            def copy(n, owner, block, dev):
                ref = att.at[owner, p] if block is None else att.at[owner, p, block]
                return remote(ref, ref, afs.at[p, n], afr.at[p, n], (r, dev))

            self.first = [copy(0, c, None, sib), copy(1, c, across, across), copy(2, c, diag, diag)]
            self.rest = [copy(3, c, diag, across), copy(4, c, c, across), copy(5, c, sib, across)]
            self.hand = [copy(6, across, c, sib), copy(7, across, across, sib), copy(8, across, diag, sib)]

    attended = [Attended(p) for p in range(2)]

    in_tok.wait()
    g_tok.start()
    for i, v in enumerate((v0, v1, v2, v3, v4, v5, v6, v7)):
        par[i : i + 1, :] = v[...].reshape(1, 768)
    for i in range(4):
        par[8 + i : 9 + i, :] = v8[768 * i : 768 * i + 768].reshape(1, 768)

    ends, lims = [], []
    total = jnp.int32(0)
    for s in range(slides_n):
        total = total + slide_units[s] * PAD
        ends.append(total)
        lims.append(total - shortfall[s])

    def label_of(pos):
        lab = jnp.zeros(pos.shape, jnp.int32)
        for s in range(slides_n - 1):
            lab = lab + jnp.where(pos >= ends[s], 1, 0)
        return lab

    def code_of(pos):
        code = label_of(pos)
        for s in range(slides_n):
            code = jnp.where((pos >= lims[s]) & (pos < ends[s]), -1, code)
        return code

    seg_first = r * 1024

    vec[...] = jnp.zeros(vec.shape, F32)
    for s in range(4):
        for h in range(4):
            wop[s, 64 * h + 48 : 64 * h + 64, :] = jnp.zeros((16, 768), BF16)
    sel_f, sel_j = iota((768, 256), 0), iota((768, 256), 1)
    head_sel = onehot((sel_f == 192 * c + 48 * (sel_j >> 6) + (sel_j & 63)) & ((sel_j & 63) < 48))
    for i, d in enumerate(in_qkv):
        d.wait()
        wqkv[:, 256 * i : 256 * i + 256] = nn(wdn[768 * i : 768 * i + 768, :], head_sel).astype(BF16)
    in_up.start()
    for d in in_wo:
        d.start()
    bqkv[...] = jnp.zeros(bqkv.shape, F32)
    biases = moved(par[0:8, :], head_sel)
    bqkv[0:1, 0:256] = biases[2:3]
    bqkv[0:1, 512:768] = biases[3:4]

    def first_norm(b):
        unit, _ = normalise(tok[b].astype(F32))
        a1[b] = (unit * par[0:1, :] + par[1:2, :]).astype(BF16)

    first_norm(c)
    on_head = (iota((256, 768), 0) & (STRIDE - 1)) == ((iota((256, 768), 1) * 1366) >> 16)

    def dilated(values):
        return jnp.sum(jnp.where(on_head, values.astype(BF16).astype(F32), 0.0).reshape(16, 16, 768), axis=1)

    k_sel = dilated(nn(a1[c], wdn[768:1536, :]))
    v_sel = dilated(nn(a1[c], wdn[1536:2304, :]) + par[3:4, :])
    for s in range(COLS):
        kvo[s] = jnp.concatenate(
            [k_sel[:, 192 * s : 192 * s + 192], v_sel[:, 192 * s : 192 * s + 192]], axis=1
        ).astype(BF16)
    own16 = pl.ds(pl.multiple_of(16 * c, 16), 16)

    def own_dilated(j):
        to = (c + j) % COLS
        return remote(kvo.at[to], kvc.at[r, own16, :], kos.at[j - 1], kor.at[j - 1], (r, to))

    for j in range(1, COLS):
        own_dilated(j).start()
    kvc[r, own16, :] = kvo[c]
    in_cot.wait()
    g_cot.start()
    in_dn.start()
    for d in in_dq:
        d.start()

    def qkv_block(b):
        low = a1[b]
        y = (nn(low, wqkv[...]) + bqkv[0:1, :]).astype(BF16).astype(F32)
        at = pl.ds(pl.multiple_of(256 * b, 256), 256)
        for i in range(6):
            qf[i, at, :] = y[:, 128 * i : 128 * i + 128]
        lane = iota((256, 128), 1) & 63
        key_code = code_of(seg_first + 256 * b + iota((256, 128), 0))
        key_mark = jnp.where(key_code == lane - 48, 0.0, NEG)
        marked = (lane >= 48) & (lane < 48 + slides_n)
        for p in range(2):
            qrow[p, at, :] = y[:, 128 * p : 128 * p + 128].astype(BF16)
            kaug[p, at, :] = jnp.where(marked, key_mark, y[:, 256 + 128 * p : 384 + 128 * p]).astype(BF16)
            vaug[p, at, :] = jnp.where(
                (lane == 48) | (lane == 49), 1.0, y[:, 512 + 128 * p : 640 + 128 * p]
            ).astype(BF16)
        qt, ktv, vt = y[:, :256].T, y[:, 256:512].T, y[:, 512:].T
        row = iota((128, 256), 0)
        query_label = label_of(seg_first + 256 * b + iota((128, 256), 1))
        mark = jnp.where(query_label == (row & 63) - 48, 1.0, 0.0)
        for h in range(4):
            p, half = h // 2, h % 2
            own = (row >> 6) == half
            full = jnp.where((row & 63) < 48, qt[128 * p : 128 * p + 128], mark)
            qtm[h, b] = jnp.where(own, full, 0.0).astype(BF16)
            hq, hk, hv = (m[64 * h : 64 * h + 64] for m in (qt, ktv, vt))
            kt[h, b] = hk.astype(BF16)
            vta[h, b] = jnp.where(iota((64, 256), 0) == 48, 1.0, hv).astype(BF16)
            sdr[h, b] = jnp.broadcast_to(colsum(hq * hk) * SCALE2, (8, 256))

    def sparse_copy(j):
        return remote(kvc.at[r], kvc.at[r], sps.at[j - 1], spr.at[j - 1], ((r + j) % rows_n, c))

    def each_row(fn):
        def step(j, carry):
            fn(j)
            return carry

        lax.fori_loop(1, rows_n, step, 0)

    qkv_block(c)
    g_tok.near.wait_recv()
    first_norm(sib)
    qkv_block(sib)
    for j in range(1, COLS):
        own_dilated(j).wait_recv()
    each_row(lambda j: sparse_copy(j).start())

    g_tok.forward()
    first_norm(across)
    qkv_block(across)
    g_tok.hand.wait_recv()
    first_norm(diag)
    qkv_block(diag)

    def picked(i, h):
        return qf[i, pl.ds(LOCAL_HEADS * c + h, 64, stride=STRIDE), :]

    def both_picked(i, p):
        lane = iota((64, 128), 1)
        return jnp.concatenate(
            [jnp.where((lane >> 6) == half, picked(i, 2 * p + half), 0.0) for half in range(2)], axis=0
        ).astype(BF16)

    def placing(p, first, transposed=False):
        shape = (256, 128) if transposed else (128, 256)
        wide, narrow = iota(shape, 0 if transposed else 1), iota(shape, 1 if transposed else 0)
        return onehot(((narrow & 63) < 48) & (wide == first + 48 * (2 * p + (narrow >> 6)) + (narrow & 63)))

    for p in range(2):
        qsel[p] = nn(both_picked(p, p), placing(p, 0)).astype(BF16)

    eye = iota((256, 256), 0) == iota((256, 256), 1)

    def weights_out(i):
        return pltpu.make_async_copy(pbuf.at[i % 2], p_h.at[i], psem.at[i % 2])

    def forward_tile(i):
        h, ib = i // 4, i % 4
        p, half = h // 2, h % 2
        slot = i if keep else i % 2
        rhs = qtm[h, ib]
        top = jnp.full((8, 256), NEG * 10, F32)
        for jb in range(4):
            s = nn(kaug[p, 256 * jb : 256 * jb + 256, :], rhs) * SCALE2
            sref[256 * jb : 256 * jb + 256, :] = s
            top = jnp.maximum(top, jnp.max(s.reshape(32, 8, 256), axis=0))
        own = sdr[h, ib]
        top = jnp.max(jnp.maximum(top, own), axis=0, keepdims=True)
        at = pl.ds(pl.multiple_of(256 * ib, 256), 256)
        sref[at, :] = jnp.where(eye, own[0:1], sref[at, :])

        if not keep:

            @pl.when(i >= 2)
            def _():
                weights_out(i).wait()

        for jb in range(4):
            pbuf[slot, 256 * jb : 256 * jb + 256, :] = jnp.exp2(
                sref[256 * jb : 256 * jb + 256, :] - top
            ).astype(BF16)
        if not keep:
            weights_out(i).start()
        values = jnp.concatenate([vta[h, jb] for jb in range(4)], axis=1)
        o = nn(values, pbuf[slot])
        z = o[48:49]
        inverse = 1.0 / z
        line = iota((64, 256), 0)
        o = o * inverse
        o = jnp.where(line == 48, inverse, jnp.where(line == 49, top, jnp.where(line == 50, z, o)))
        dqt[half, ib] = o

    def branch_b(p):
        lane = iota((64, 128), 1)
        s = nt(qsel[p], kvc[:, :, 0:256].reshape(key_count, 256)) * SCALE2
        masked = []
        for half in range(2):
            first = LOCAL_HEADS * c + 2 * p + half
            qpos = seg_first + STRIDE * iota((64, 128), 0)[:, 0:1] + first
            kpos = STRIDE * iota((8, key_count), 1)[0:1] + first
            allowed = (label_of(qpos) == code_of(kpos)) | (qpos == kpos)
            masked.append(jnp.where(allowed, s[64 * half : 64 * half + 64], NEG))
        s = jnp.concatenate(masked, axis=0)
        tops = jnp.max(s, axis=1, keepdims=True)
        e = jnp.exp2(s - tops)
        sums = jnp.sum(e, axis=1, keepdims=True)
        outs = moved(nn(e.astype(BF16), kvc[:, :, 128:384].reshape(key_count, 256)), placing(p, 64, True))
        factors = []
        for half in range(2):
            rows = slice(64 * half, 64 * half + 64)
            top_b, z_b, o_b = tops[rows], sums[rows], outs[rows]
            at = pl.ds(LOCAL_HEADS * c + 2 * p + half, 64, stride=STRIDE)
            old = oa[p, at, :]
            top_a = old[:, 64 * half + 49 : 64 * half + 50]
            z_a = old[:, 64 * half + 50 : 64 * half + 51]
            top = jnp.maximum(top_a, top_b)
            in_a, in_b = jnp.exp2(top_a - top), jnp.exp2(top_b - top)
            inverse = 1.0 / (in_a * z_a + in_b * z_b)
            o = (in_a * z_a * old + in_b * o_b) * inverse
            own = (lane >> 6) == half
            oa[p, at, :] = jnp.where(
                own & ((lane & 63) < 48), o, jnp.where(lane == 64 * half + 48, in_a * inverse, old)
            )
            factors.append(in_b * inverse)
        wb[p] = (e * jnp.concatenate(factors, axis=0)).astype(BF16)

    lane256 = iota((256, 128), 1)
    for p in range(2):
        def fwd(t, carry, p=p):
            forward_tile(8 * p + t)
            return carry

        lax.fori_loop(0, 8, fwd, 0)
        for ib in range(4):
            oa[p, 256 * ib : 256 * ib + 256, :] = jnp.concatenate([dqt[0, ib], dqt[1, ib]], axis=0).T
        if p == 0:
            each_row(lambda j: sparse_copy(j).wait_recv())
        else:
            g_cot.forward()
        branch_b(p)
        for ib in range(4):
            att[c, p, ib] = jnp.where(
                (lane256 & 63) < 48, oa[p, 256 * ib : 256 * ib + 256, :], 0.0
            ).astype(BF16)
        for d in attended[p].first:
            d.start()
    if not keep:
        weights_out(14).wait()
        weights_out(15).wait()
    for a in attended:
        for d in a.rest:
            d.start()

    in_up.wait()
    for n in range(3):
        start = (4 * share * ((256 * n) // share)) // 128 * 128
        stop = -(-(4 * share * ((256 * n + 255) // share + 1)) // 128) * 128
        o = 256 * n + iota((stop - start, 256), 1)
        group = jnp.zeros_like(o)
        for t in range(1, rows_n):
            group = group + jnp.where(o >= share * t, 1, 0)
        unit_sel = onehot(start + iota((stop - start, 256), 0) == 3 * share * group + share * c + o)
        for m in range(3):
            wupq[256 * m : 256 * m + 256, 256 * n : 256 * n + 256] = nn(
                wup[256 * m : 256 * m + 256, start:stop], unit_sel
            ).astype(BF16)
        pieces = [par[8 + t : 9 + t, :] for t in range(4)]
        line = jnp.concatenate(pieces, axis=1)[:, start:stop]
        bupq[0:8, 256 * n : 256 * n + 256] = moved(jnp.broadcast_to(line, (8, stop - start)), unit_sel)

    g_cot.near.wait_recv()
    g_cot.hand.wait_recv()
    vec[5:6, :] = colsum(gb[...].reshape(1024, 768).astype(F32))
    for d in in_wo:
        d.wait()
    for a in attended:
        for d in a.first:
            d.wait_recv()

    def project(b):
        out = tok[b].astype(F32) + par[4:5, :]
        for s in range(4):
            out = out + nn(jnp.concatenate([att[s, 0, b], att[s, 1, b]], axis=1), wop[s])
        return out

    def second_norm(b, values):
        unit, inverse = normalise(values)
        a2[b] = (unit * par[5:6, :] + par[6:7, :]).astype(BF16)
        return unit, inverse

    y1[...] = project(c)
    second_norm(c, y1[...])

    in_dn.wait()
    acc[...] = y1[...] + par[7:8, :]
    da2[...] = jnp.zeros(da2.shape, F32)

    def mlp(i, carry):
        low = a2[c]
        g = gb[c]
        at = pl.ds(pl.multiple_of(768 * i, 768), 768)
        u = nn(low, wup[:, at]) + par[pl.ds(8 + i, 1), :]
        hidden, slope = gelu_parts(u)
        acc[...] += nn(hidden.astype(BF16), wdn[at, :])
        du = (nt(g, wdn[at, :]) * slope).astype(BF16)
        da2[...] += nt(du, wup[:, at])
        return carry

    lax.fori_loop(0, 4, mlp, 0)
    for a in attended:
        for d in a.rest:
            d.wait_recv()
        for d in a.hand:
            d.start()
    wqkv[0:256, :] = acc[...].astype(BF16)
    out_copy = local(wqkv.at[pl.ds(0, 256), :], out_h, 0)
    out_copy.start()
    unit, inverse = normalise(y1[...])
    vec[3:4, :] = colsum(da2[...] * unit)
    vec[4:5, :] = colsum(da2[...])
    dy1 = gb[c].astype(F32) + norm_back(da2[...], unit, inverse, par[5:6, :])
    y1[...] = dy1
    drb[c] = dy1.astype(BF16)
    g_dr.start()

    for a in attended:
        for d in a.hand:
            d.wait_recv()
    for j in range(1, 4):
        b = (c + j) % 4
        second_norm(b, project(b))
    for d in in_dq:
        d.wait()

    def quarter(b, carry):
        u = nn(a2[b], wupq[...]) + bupq[0:1, :]
        hidden, slope = gelu_parts(u)
        at = pl.ds(pl.multiple_of(256 * b, 256), 256)
        wdn[at, :] = hidden.astype(BF16)
        du = (nt(gb[b], wdq[...]) * slope).astype(BF16)
        wdn[pl.ds(pl.multiple_of(1024 + 256 * b, 256), 256), :] = du
        vec[6:7, :] += colsum(du.astype(F32))
        return carry

    lax.fori_loop(0, 4, quarter, 0)

    def slab_at(b, l, h):
        return ((2 * b + l) * his + h) * tall

    def put(n, block, first):
        buf = slabs[n]
        width = block.shape[1]
        at = first
        while at < first + block.shape[0]:
            which, off = at // share, at % share
            size = min(share - off, first + block.shape[0] - at)
            row = slab_at(which % 2, (which // 2) % 2, which // 4) + off
            buf[row : row + size, 0:width] = block[at - first : at - first + size].astype(BF16)
            at += size

    def one(n):
        half = 2 * his * tall
        at = pl.ds(pl.multiple_of((1 - bit) * half, half), half)
        return remote(slabs[n].at[at, :], recv_a[n], u1s.at[n], u1r.at[n], (r + 1 - 2 * bit, c))

    def two(n):
        at = pl.ds(pl.multiple_of(slab_at(bit, 1 - lo, 0), his * tall), his * tall)
        return remote(slabs[n].at[at, :], recv_b[n], u2s.at[n], u2r.at[n], (r + 2 - 4 * lo, c))

    def slab(l, h):
        return pl.ds(pl.multiple_of(slab_at(bit, l, h), tall), tall)

    def three(n, j):
        to = (hi + j) % his
        return remote(
            slabs[n].at[slab(lo, to), :], recv_c[n].at[j - 1], u3s.at[n, j - 1], u3r.at[n, j - 1],
            (4 * to + 2 * lo + bit, c),
        )

    def each_hi(fn):
        def step(j, carry):
            fn(j)
            return carry

        lax.fori_loop(1, his, step, 0)

    def start_two(n):
        one(n).wait_recv()

        def add(i, carry):
            for l in range(2):
                at = pl.ds(pl.multiple_of((l * his + i) * tall, tall), tall)
                slabs[n][slab(l, i), :] = (slabs[n][slab(l, i), :].astype(F32) + recv_a[n][at, :].astype(F32)).astype(BF16)
            return carry

        lax.fori_loop(0, his, add, 0)
        two(n).start()

    def start_three(n):
        two(n).wait_recv()

        def add(i, carry):
            at = pl.ds(pl.multiple_of(i * tall, tall), tall)
            slabs[n][slab(lo, i), :] = (slabs[n][slab(lo, i), :].astype(F32) + recv_b[n][at, :].astype(F32)).astype(BF16)
            return carry

        lax.fori_loop(0, his, add, 0)
        each_hi(lambda j: three(n, j).start())

    def slab_sent(n):
        one(n).wait_send()
        two(n).wait_send()
        each_hi(lambda j: three(n, j).wait_send())

    def col_copy(n, j):
        at = pl.ds(OFFSETS[n], UNITS[n])
        return remote(gath.at[c, :, at], gath.at[c, :, at], ucs.at[n, j - 1], ucr.at[n, j - 1], (r, (c + j) % COLS))

    def finish(n):
        each_hi(lambda j: three(n, j).wait_recv())
        gath[c, :, OFFSETS[n] : OFFSETS[n] + UNITS[n]] = (
            lax.fori_loop(
                0, his - 1, lambda j, t: t + recv_c[n][j].astype(F32), slabs[n][slab(lo, hi), :].astype(F32)
            )
        ).astype(BF16)
        for j in range(1, COLS):
            col_copy(n, j).start()

    for m in range(2):
        put(DOWN, tn(wdn[0:1024, 384 * m : 384 * m + 384], gb[...].reshape(1024, 768)), 384 * m)
    one(DOWN).start()
    g_dr.forward()
    for m in range(2):
        lanes = jnp.concatenate([a2[b, :, 384 * m : 384 * m + 384] for b in range(4)], axis=0)
        block = tn(lanes, wdn[1024:2048, :])
        put(UP, block[:, 0:512], 384 * m)
        put(UP_LAST, block[:, 512:768], 384 * m)

    g_dr.near.wait_recv()
    g_dr.hand.wait_recv()
    vec[2:3, :] = colsum(drb[...].reshape(1024, 768).astype(F32))
    bones = onehot((iota((256, 256), 0) >> 6) == (iota((256, 256), 1) >> 6))

    def out_grad(b, carry):
        lane = iota((256, 256), 1) & 63
        at = pl.ds(pl.multiple_of(256 * b, 256), 256)
        d_att = nt(drb[b], wop[c]).astype(BF16).astype(F32)
        mine = jnp.concatenate([att[c, 0, b], att[c, 1, b]], axis=1).astype(F32)
        rowsum = moved(d_att * mine, bones, 2)
        factor = moved(
            jnp.where(lane == 48, jnp.concatenate([oa[0, at, :], oa[1, at, :]], axis=1), 0.0), bones
        )
        minus = -rowsum * factor
        high = minus.astype(BF16).astype(F32)
        marked = jnp.where(lane == 48, high, jnp.where(lane == 49, minus - high, d_att * factor))
        flipped = marked.T
        line = iota((128, 256), 0)
        for p in range(2):
            kaug[p, at, :] = marked[:, 128 * p : 128 * p + 128].astype(BF16)
            qf[p, at, :] = d_att[:, 128 * p : 128 * p + 128]
            qf[2 + p, at, :] = rowsum[:, 128 * p : 128 * p + 128]
        for h in range(4):
            p = h // 2
            qtm[h, b] = jnp.where(
                (line >> 6) == h % 2, flipped[128 * p : 128 * p + 128], 0.0
            ).astype(BF16)
        return carry

    lax.fori_loop(0, 4, out_grad, 0)

    own_cols = onehot(
        (iota((256, 768), 1) == 192 * c + iota((256, 768), 0)) & (iota((256, 768), 0) < 192)
    )
    dr_own = jnp.concatenate([nt(own_cols, drb[b]).astype(BF16) for b in range(4)], axis=1)
    for s in range(4):
        both = jnp.concatenate(
            [att[s, 0].reshape(1024, 128), att[s, 1].reshape(1024, 128)], axis=1
        )
        block = nn(dr_own, both).T
        for h in range(4):
            put(OUT, block[64 * h : 64 * h + 48], 192 * s + 48 * h)

    step_rows = min(rows_n, 8)
    step_keys = 64 * step_rows

    def dilated_block(t):
        tall, wide = pl.multiple_of(64 * (t // 8), 64), pl.multiple_of(384 * (t % 8), 384)
        return wup.at[pl.ds(tall, 64), pl.ds(wide, 384)]

    d_sel, sums = [], []
    for p in range(2):
        d_sel.append(nn(both_picked(p, p), placing(p, 64)).astype(BF16))
        sums.append(
            jnp.concatenate([picked(2 + p, 2 * p + i)[:, 64 * i : 64 * i + 1] for i in range(2)], axis=0)
        )
    dqb[...] = jnp.zeros(dqb.shape, F32)

    def some_keys(n, carry):
        some = pl.ds(pl.multiple_of(step_rows * n, step_rows), step_rows)
        k2 = kvc[some, :, 0:256].reshape(step_keys, 256)
        v2 = kvc[some, :, 128:384].reshape(step_keys, 256)
        dk, dv = 0.0, 0.0
        for p in range(2):
            w = wb[p, :, pl.ds(pl.multiple_of(step_keys * n, step_keys), step_keys)]
            ds = (w.astype(F32) * (nt(d_sel[p], v2) - sums[p])).astype(BF16)
            dqb[p] += nn(ds, k2)
            dk = dk + tn(ds, qsel[p])
            dv = dv + tn(w, d_sel[p])
        for t in range(step_rows):
            block = dilated_block(step_rows * n + t)
            rows = slice(64 * t, 64 * t + 64)
            block[:, 0:128] = dk[rows, 0:128].astype(BF16)
            block[:, 128:256] = (dk[rows, 128:256] + dv[rows, 0:128]).astype(BF16)
            block[:, 256:384] = dv[rows, 128:256].astype(BF16)
        return carry

    lax.fori_loop(0, rows_n // step_rows, some_keys, 0)

    def dilated_copy(j):
        to = (r + j) % rows_n
        return remote(dilated_block(to), dkvr.at[j - 1], bss.at[j - 1], bsr.at[j - 1], (to, c))

    each_row(lambda j: dilated_copy(j).start())

    qf[...] = jnp.zeros(qf.shape, F32)

    def weights_in(i):
        return pltpu.make_async_copy(p_h.at[i], pbuf.at[i % 2], psem.at[i % 2])

    def backward_tile(i):
        h, ib = i // 4, i % 4
        p, half = h // 2, h % 2
        slot = i if keep else i % 2
        if not keep:
            weights_in(i).wait()

            @pl.when(i + 1 < 16)
            def _():
                weights_in(i + 1).start()

        rhs = qtm[h, ib]
        for jb in range(4):
            at = slice(256 * jb, 256 * jb + 256)
            dsb[at, :] = (pbuf[slot, at, :].astype(F32) * nn(vaug[p, at, :], rhs)).astype(BF16)
        keys = jnp.concatenate([kt[h, jb] for jb in range(4)], axis=1)
        dqt[h, ib] = nn(keys, dsb[...])
        at = pl.ds(pl.multiple_of(256 * ib, 256), 256)
        own = (iota((256, 128), 1) >> 6) == half
        d_rows, q_rows = kaug[p, at, :], qrow[p, at, :]
        for jb in range(4):
            js = slice(256 * jb, 256 * jb + 256)
            qf[2 + p, js, :] += jnp.where(own, nn(dsb[js, :], q_rows), 0.0)
            qf[4 + p, js, :] += jnp.where(own, nn(pbuf[slot, js, :], d_rows), 0.0)

    if not keep:
        weights_in(0).start()
    for first, last in ((0, 11), (11, 16)):
        def bwd(t, carry):
            backward_tile(t)
            return carry

        lax.fori_loop(first, last, bwd, 0)
        if first:
            one(UP_LAST).start()
        if first == 0:
            start_two(DOWN)
            one(UP).start()
            one(OUT).start()

    each_row(lambda j: dilated_copy(j).wait_recv())
    spread = lax.fori_loop(
        0, rows_n - 1, lambda j, t: t + dkvr[j].astype(F32), dilated_block(r)[...].astype(F32)
    )
    each_row(lambda j: dilated_copy(j).wait_send())
    back_qkv = [local(h, wup.at[:, pl.ds(768 * i, 768)], 2 + i) for i, h in enumerate((wq_h, wk_h, wv_h))]
    for d in back_qkv:
        d.start()
    source, slot = iota((384, 512), 0), iota((384, 512), 1)
    spread = moved(
        spread,
        onehot(((slot & 63) < 48) & (source == 192 * (slot >> 8) + 48 * ((slot & 255) >> 6) + (slot & 63))),
        2,
    )
    dq_b = [moved(dqb[p], placing(p, 0, True), 2) for p in range(2)]
    for h in range(4):
        p, rows = h // 2, slice(64 * (h % 2), 64 * (h % 2) + 64)
        own = (iota((64, 128), 1) >> 6) == h % 2
        at = pl.ds(LOCAL_HEADS * c + h, 64, stride=STRIDE)
        qf[p, at, :] += jnp.where(own, dq_b[p][rows], 0.0)
        qf[2 + p, at, :] += jnp.where(own, spread[:, 128 * p : 128 * p + 128], 0.0)
        qf[4 + p, at, :] += jnp.where(own, spread[:, 256 + 128 * p : 384 + 128 * p], 0.0)

    def turned(i, b):
        at = pl.ds(pl.multiple_of(256 * b, 256), 256)
        return jnp.concatenate([qf[2 * i, at, :], qf[2 * i + 1, at, :]], axis=1).T

    def compact(b, carry):
        dq = (jnp.concatenate([dqt[h, b] for h in range(4)], axis=0) + turned(0, b)) * SCALE
        for i, m in enumerate((dq, turned(1, b) * SCALE, turned(2, b))):
            for h in range(4):
                a2[b, 48 * h : 48 * h + 48, 256 * i : 256 * i + 256] = m[64 * h : 64 * h + 48].astype(BF16)
        return carry

    lax.fori_loop(0, 4, compact, 0)

    def exchange(j):
        to = (c + j) % COLS
        at = pl.ds(pl.multiple_of(192 * c, 64), 192)
        return remote(a2.at[to, pl.ds(0, 192), :], dqr.at[at, :], ats.at[j - 1], atr.at[j - 1], (r, to))

    for j in range(1, COLS):
        exchange(j).start()
    dqr[pl.ds(pl.multiple_of(192 * c, 64), 192), :] = a2[c, 0:192, :]
    rows576 = [
        jnp.concatenate(
            [a2[b, 0:192, 256 * i : 256 * i + 256] for i in range(3)] + [jnp.zeros((64, 256), BF16)], axis=0
        )
        for b in range(4)
    ]
    lhs = jnp.concatenate(rows576, axis=1)
    def own_grads(n, first):
        for m in range(2):
            lanes = jnp.concatenate([a1[b, :, 384 * m : 384 * m + 384] for b in range(4)], axis=0)
            put(n, nn(lhs[first : first + UNITS[n]], lanes).T, 384 * m)

    own_grads(QK, 0)
    one(QK).start()
    own_grads(VAL, UNITS[QK])
    ones = jnp.ones((16, 1024), BF16)
    vec[7:8, 0:640] = nt(ones, lhs)[0:1]
    start_three(DOWN)
    start_two(UP)
    start_two(OUT)
    start_two(UP_LAST)
    finish(DOWN)
    start_three(UP)
    start_two(QK)
    one(VAL).start()

    for d in back_qkv:
        d.wait()
    for j in range(1, COLS):
        exchange(j).wait_recv()
    da1 = nn(wup[:, 0:768], dqr[:, 0:256])
    for i in range(1, 3):
        da1 = da1 + nn(wup[:, 768 * i : 768 * i + 768], dqr[:, 256 * i : 256 * i + 256])
    da1 = da1.T
    unit, inverse = normalise(tok[c].astype(F32))
    vec[0:1, :] = colsum(da1 * unit)
    vec[1:2, :] = colsum(da1)
    vec_one = remote(vec, vin.at[0], vss.at[0], vsr.at[0], (r + 1 - 2 * bit, c))
    vec_one.start()
    da2[...] = y1[...] + norm_back(da1, unit, inverse, par[0:1, :])
    gt_copy = local(da2, gt_h, 1)
    gt_copy.start()
    start_three(OUT)
    start_three(UP_LAST)
    start_two(VAL)
    start_three(QK)
    vec_one.wait_recv()
    vcol[c] = vec[...] + vin[0]
    vec_two = remote(vcol.at[c], vin.at[1], vss.at[1], vsr.at[1], (r + 2 - 4 * lo, c))
    vec_two.start()
    finish(UP)
    finish(OUT)
    vec_two.wait_recv()
    vrow[hi] = vcol[c] + vin[1]

    def vec_three(j):
        to = (hi + j) % his
        return remote(vrow.at[hi], vrow.at[hi], vss.at[1 + j], vsr.at[1 + j], (4 * to + 2 * lo + bit, c))

    each_hi(lambda j: vec_three(j).start())
    finish(UP_LAST)
    start_three(VAL)
    each_hi(lambda j: vec_three(j).wait_recv())
    vec_two.wait_send()
    vcol[c] = lax.fori_loop(0, his, lambda j, t: t + vrow[j], jnp.zeros((16, 768), F32))

    def vec_col(j):
        return remote(vcol.at[c], vcol.at[c], vcs.at[j - 1], vcr.at[j - 1], (r, (c + j) % COLS))

    for j in range(1, COLS):
        vec_col(j).start()
    finish(QK)
    finish(VAL)
    for j in range(1, COLS):
        vec_col(j).wait_recv()
        for n in range(6):
            col_copy(n, j).wait_recv()
    out_gath = local(gath, gath_h, 2)
    out_vec = local(vcol, vec_h, 3)
    out_gath.start()
    out_vec.start()

    for g in (g_tok, g_cot, g_dr):
        g.drain()
    for a in attended:
        for d in (*a.first, *a.rest, *a.hand):
            d.wait_send()
    each_row(lambda j: sparse_copy(j).wait_send())
    vec_one.wait_send()
    each_hi(lambda j: vec_three(j).wait_send())
    for n in range(6):
        slab_sent(n)
        for j in range(1, COLS):
            col_copy(n, j).wait_send()
    for j in range(1, COLS):
        exchange(j).wait_send()
        own_dilated(j).wait_send()
        vec_col(j).wait_send()
    out_copy.wait()
    gt_copy.wait()
    out_gath.wait()
    out_vec.wait()


def finale(
    rows_n, gath_h, vec_h, out_h, gt_h, out, gt, g1, b1, gq, bq, gk, gv, bv, go, bo, g2, b2, gu, bu, gd, bd,
    gath, vec, sems,
):
    copies = [
        pltpu.make_async_copy(src, dst, sems.at[i])
        for i, (src, dst) in enumerate(((gath_h, gath), (vec_h, vec), (out_h, out), (gt_h, gt)))
    ]
    for d in copies:
        d.start()
    share = 768 // rows_n
    r = lax.axis_index("row")
    copies[0].wait()
    part = [gath[s].astype(F32)[:share] for s in range(COLS)]

    def across(off, width):
        return jnp.concatenate([part[s][:, off : off + width] for s in range(COLS)], axis=1)

    gq[...] = across(1792, 192)
    gk[...] = across(1792 + 192, 192)
    gv[...] = across(1792 + 384, 192)
    go[...] = across(1536, 192)
    gu[...] = jnp.concatenate(
        [part[s][:, 768 + share * t : 768 + share * t + share] for t in range(rows_n) for s in range(COLS)], axis=1
    )
    for s in range(COLS):
        gd[share * s : share * s + share, :] = part[s][:, 0:768]
    copies[1].wait()
    summed = vec[0] + vec[1] + vec[2] + vec[3]
    wide = max(128, -(-share // 128) * 128)
    f, j = iota((768, wide), 0), iota((768, wide), 1)
    pick = onehot((f == share * r + j) & (j < share))
    mine = vec[0]
    total = moved(jnp.concatenate([summed[0:8], mine[0:8]], axis=0), pick)
    hidden = [moved(vec[s][0:8], pick) for s in range(COLS)]
    qv = [None, None]
    for n, off in enumerate((0, 384)):
        for s in range(COLS):
            place = onehot((f + 192 * s - off == share * r + j) & (j < share) & (f >= off) & (f < off + 192))
            term = moved(vec[s][0:8], place)
            qv[n] = term if qv[n] is None else qv[n] + term
    g1[...] = total[0, :share]
    b1[...] = total[1, :share]
    bo[...] = total[8 + 2, :share]
    g2[...] = total[3, :share]
    b2[...] = total[4, :share]
    bd[...] = total[8 + 5, :share]
    bq[...] = qv[0][7, :share]
    bv[...] = qv[1][7, :share]
    bu[...] = jnp.concatenate([hidden[s][6:7, :share] for s in range(COLS)], axis=1)[0]
    copies[2].wait()
    copies[3].wait()


def body(rows_n, tokens, norm1_gain, norm1_bias, w_query, b_query, w_key, w_value, b_value, w_out, b_out,
         norm2_gain, norm2_bias, w_up, b_up, w_down, b_down, slide_padded_units, padding_shortfall, cotangent):
    his, share = rows_n // 4, 768 // rows_n
    padded = -(-share // 16) * 16
    c = lax.axis_index("col")
    down_q = w_down
    if share % 16:
        down_q = lax.dynamic_index_in_dim(w_down.reshape(rows_n, COLS, share, 768), c, 1, False).reshape(768, 768)
    vmem = pltpu.VMEM
    dma = pltpu.SemaphoreType.DMA
    between = max(his - 1, 1)
    keep = rows_n <= 8
    scratch = [
        vmem((768, 3072), BF16), vmem((3072, 768), BF16), vmem((768, 768), BF16), vmem((768, 768), BF16),
        vmem((768, 768), BF16), vmem((4, 256, 768), BF16),
        *[vmem((4, 256, 768), BF16) for _ in range(5)],
        vmem((6, 1040, 128), F32), vmem((2, 1024, 128), BF16), vmem((2, 1024, 128), BF16),
        vmem((2, 1024, 128), BF16), vmem((4, 4, 128, 256), BF16), vmem((4, 4, 64, 256), BF16),
        vmem((4, 4, 64, 256), BF16), vmem((4, 4, 8, 256), F32),
        vmem((16 if keep else 2, 1024, 256), BF16), vmem((1024, 256), F32), vmem((1024, 256), BF16),
        vmem((2, 1040, 128), F32), vmem((4, 2, 4, 256, 128), BF16),
        vmem((256, 768), F32), vmem((256, 768), F32), vmem((256, 768), F32),
        vmem((4, 4, 64, 256), F32), vmem((768, 768), BF16),
        *[vmem((rows_n * padded, w), BF16) for w in UNITS[:QK]],
        *[vmem((2 * his * padded, w), BF16) for w in UNITS],
        *[vmem((his * padded, w), BF16) for w in UNITS],
        *[vmem((between, padded, w), BF16) for w in UNITS],
        vmem((4, padded, WIDTH), BF16),
        vmem((4, 16, 384), BF16), vmem((rows_n, 64, 384), BF16), vmem((2, 128, 256), BF16),
        vmem((2, 128, rows_n * 64), BF16), vmem((2, 128, 256), F32), vmem((rows_n - 1, 64, 384), BF16),
        vmem((16, 768), F32), vmem((16, 768), F32), vmem((2, 16, 768), F32), vmem((his, 16, 768), F32),
        vmem((4, 16, 768), F32), vmem((8, 768), F32), vmem((8, 768), F32),
        dma((24 + rows_n,)), dma((3, 3)), dma((3, 3)), dma((2, 9)), dma((2, 9)), dma((3,)), dma((3,)),
        dma((rows_n - 1,)), dma((rows_n - 1,)), dma((rows_n - 1,)), dma((rows_n - 1,)),
        dma((6,)), dma((6,)), dma((6,)), dma((6,)), dma((6, between)), dma((6, between)), dma((6, 3)), dma((6, 3)),
        dma((3,)), dma((3,)), dma((his + 1,)), dma((his + 1,)), dma((3,)), dma((3,)), dma((2,)),
    ]
    hbm = pl.BlockSpec(memory_space=pl.ANY)
    smem = pl.BlockSpec(memory_space=pltpu.SMEM)
    whole = pl.BlockSpec(memory_space=pltpu.VMEM)
    sds = jax.ShapeDtypeStruct
    out, gt, gath, vec, _ = pl.pallas_call(
        functools.partial(layer, rows_n, slide_padded_units.shape[0], keep),
        out_shape=(
            sds((256, 768), BF16), sds((256, 768), F32), sds((4, padded, WIDTH), BF16), sds((4, 16, 768), F32),
            sds((8, 128) if keep else (16, 1024, 256), BF16),
        ),
        in_specs=[smem, smem] + [whole] * 9 + [hbm] * 9,
        out_specs=(hbm,) * 5,
        scratch_shapes=scratch,
        compiler_params=pltpu.CompilerParams(
            collective_id=0, has_side_effects=True, vmem_limit_bytes=(992 if rows_n <= 8 else 1021) * 64 * 1024
        ),
        name="layer",
    )(slide_padded_units, padding_shortfall, norm1_gain, norm1_bias, b_query, b_value, b_out, norm2_gain, norm2_bias,
      b_down, b_up, tokens, cotangent, w_query, w_key, w_value, w_out, w_up, w_down,
      down_q)
    vec1 = sds((share,), F32)
    mat = sds((share, 768), F32)
    return pl.pallas_call(
        functools.partial(finale, rows_n),
        out_shape=(
            sds((256, 768), BF16), sds((256, 768), F32), vec1, vec1, mat, vec1, mat, mat, vec1, mat, vec1, vec1, vec1,
            sds((share, 3072), F32), sds((4 * share,), F32), sds((4 * share, 768), F32), vec1,
        ),
        in_specs=[pl.BlockSpec(memory_space=pltpu.HBM)] * 4,
        out_specs=(whole,) * 17,
        scratch_shapes=[vmem((4, padded, WIDTH), BF16), vmem((4, 16, 768), F32), dma((4,))],
        compiler_params=pltpu.CompilerParams(vmem_limit_bytes=1016 * 64 * 1024),
        name="finale",
    )(gath, vec, out, gt)


def solution(mesh):
    tiles = P(("row", "col"), None)
    one, two = P("row"), P("row", None)
    return jax.shard_map(
        functools.partial(body, mesh.shape["row"]),
        mesh=mesh,
        in_specs=(tiles,) + (P(),) * 17 + (tiles,),
        out_specs=(tiles, tiles, one, one, two, one, two, two, one, two, one, one, one, two, one, two, one),
        check_vma=False,
    )
```

```python
import functools

import jax
import jax.numpy as jnp
from jax import lax
from jax.experimental import pallas as pl
from jax.experimental.pallas import tpu as pltpu
from jax.sharding import PartitionSpec as P

HEADS = 16
HEAD_DIM = 48
SLOT = 64
STRIDE = 16
PAD = 256
COLS = 4
LOCAL_HEADS = HEADS // COLS
EPS = 1e-05
NEG = -1e30
SCALE = HEAD_DIM**-0.5
SCALE2 = SCALE * 1.4426950408889634
MESH = pl.DeviceIdType.MESH
BF16 = jnp.bfloat16
F32 = jnp.float32
UNITS = (768, 512, 256, 256, 384, 256)
OFFSETS = (0, 768, 1280, 1536, 1792, 2176)
DOWN, UP, UP_LAST, OUT, QK, VAL = range(6)
WIDTH = 2432


def nn(left, right):
    return jnp.dot(left, right, preferred_element_type=F32)


def nt(left, right):
    return lax.dot_general(left, right, (((1,), (1,)), ((), ())), preferred_element_type=F32)


def tn(left, right):
    return lax.dot_general(left, right, (((0,), (0,)), ((), ())), preferred_element_type=F32)


def iota(shape, dim):
    return lax.broadcasted_iota(jnp.int32, shape, dim)


def onehot(test):
    return jnp.where(test, 1.0, 0.0).astype(BF16)


def moved(values, chooser, parts=3):
    total = None
    for i in range(parts):
        low = values.astype(BF16)
        term = nn(low, chooser)
        total = term if total is None else total + term
        if i < parts - 1:
            values = values - low.astype(F32)
    return total


def normalise(x):
    centred = x - jnp.mean(x, axis=-1, keepdims=True)
    inverse = lax.rsqrt(jnp.mean(centred * centred, axis=-1, keepdims=True) + EPS)
    return centred * inverse, inverse


def norm_back(grad, unit, inverse, gain):
    scaled = grad * gain
    mean_one = jnp.mean(scaled, axis=-1, keepdims=True)
    mean_two = jnp.mean(scaled * unit, axis=-1, keepdims=True)
    return inverse * (scaled - mean_one - unit * mean_two)


def gelu_parts(u):
    z = jnp.abs(u) * 0.7071067811865476
    e = jnp.exp(-z * z)
    t = 1.0 / (1.0 + 0.3275911 * z)
    poly = t * (0.254829592 + t * (-0.284496736 + t * (1.421413741 + t * (-1.453152027 + t * 1.061405429))))
    tail = 0.5 * poly * e
    phi = jnp.where(u >= 0, 1.0 - tail, tail)
    return u * phi, phi + u * e * 0.3989422804014327


def colsum(x):
    return jnp.sum(x, axis=0, keepdims=True)


def layer(
    rows_n, slides_n, keep,
    slide_units, shortfall, v0, v1, v2, v3, v4, v5, v6, v7, v8, tok_h, cot_h, wq_h, wk_h, wv_h, wo_h, wup_h, wdn_h, wdq_h,
    out_h, gt_h, gath_h, vec_h, p_h,
    wup, wdn, wqkv, wupq, wdq, wop,
    tok, gb, a1, a2, drb,
    qf, qrow, kaug, vaug, qtm, kt, vta, sdr,
    pbuf, sref, dsb, oa, att,
    y1, acc, da2, dqt, dqr,
    slab0, slab1, slab2, slab3, ra0, ra1, ra2, ra3, ra4, ra5, rb0, rb1, rb2, rb3, rb4, rb5, rc0, rc1, rc2, rc3, rc4, rc5, gath,
    kvo, kvc, qsel, wb, dqb, dkvr,
    par, vec, vin, vrow, vcol, bupq, bqkv,
    lsem, gss, gsr, afs, afr, kos, kor, sps, spr, bss, bsr, u1s, u1r, u2s, u2r, u3s, u3r, ucs, ucr, ats, atr,
    vss, vsr, vcs, vcr, psem,
):
    his = rows_n // 4
    share = 768 // rows_n
    r = lax.axis_index("row")
    c = lax.axis_index("col")
    sib = c + 1 - 2 * (c % 2)
    across = (c + 2) % COLS
    diag = (sib + 2) % COLS
    hi, lo, bit = r // 4, (r // 2) % 2, r % 2
    recv_a, recv_b, recv_c = (ra0, ra1, ra2, ra3, ra4, ra5), (rb0, rb1, rb2, rb3, rb4, rb5), (rc0, rc1, rc2, rc3, rc4, rc5)
    slabs = (
        slab0, slab1, slab2, slab3,
        wdn.at[pl.ds(0, slab0.shape[0]), pl.ds(0, UNITS[QK])],
        wdn.at[pl.ds(0, slab0.shape[0]), pl.ds(UNITS[QK], UNITS[VAL])],
    )
    tall = slab0.shape[0] // rows_n
    key_count = rows_n * 64

    def local(src, dst, i):
        return pltpu.make_async_copy(src, dst, lsem.at[i])

    in_tok = local(tok_h, tok.at[c], 0)
    in_cot = local(cot_h, gb.at[c], 1)
    in_qkv = [local(h, wdn.at[pl.ds(768 * i, 768), :], 2 + i) for i, h in enumerate((wq_h, wk_h, wv_h))]
    in_up = local(wup_h, wup, 5)
    in_dn = local(wdn_h, wdn, 6)
    if share % 16 == 0:
        in_dq = [
            local(wdq_h.at[pl.ds(4 * share * t + share * c, share), :], wdq.at[pl.ds(share * t, share), :], 24 + t)
            for t in range(rows_n)
        ]
    else:
        in_dq = [local(wdq_h, wdq, 24)]
    in_wo = [
        local(wo_h.at[pl.ds(192 * s + 48 * h, 48), :], wop.at[s, pl.ds(64 * h, 48), :], 8 + 4 * s + h)
        for s in range(4)
        for h in range(4)
    ]
    in_tok.start()
    in_cot.start()
    for d in in_qkv:
        d.start()

    bar = pltpu.get_barrier_semaphore()
    for j in range(1, COLS):
        pl.semaphore_signal(bar, inc=1, device_id=(r, (c + j) % COLS), device_id_type=MESH)

    def greet(j, carry):
        pl.semaphore_signal(bar, inc=1, device_id=((r + j) % rows_n, c), device_id_type=MESH)
        return carry

    lax.fori_loop(1, rows_n, greet, 0)
    pl.semaphore_wait(bar, COLS - 1 + rows_n - 1)

    def remote(src, dst, send, recv, dev):
        return pltpu.make_async_remote_copy(
            src_ref=src, dst_ref=dst, send_sem=send, recv_sem=recv, device_id=dev, device_id_type=MESH
        )

    class Gather:
        def __init__(self, n, slot):
            self.near = remote(slot(c), slot(c), gss.at[n, 0], gsr.at[n, 0], (r, sib))
            self.far = remote(slot(c), slot(c), gss.at[n, 1], gsr.at[n, 1], (r, across))
            self.hand = remote(slot(across), slot(across), gss.at[n, 2], gsr.at[n, 2], (r, sib))

        def start(self):
            self.far.start()
            self.near.start()

        def forward(self):
            self.far.wait_recv()
            self.hand.start()

        def drain(self):
            self.near.wait_send()
            self.far.wait_send()
            self.hand.wait_send()

    g_tok = Gather(0, lambda i: tok.at[i])
    g_cot = Gather(1, lambda i: gb.at[i])
    g_dr = Gather(2, lambda i: drb.at[i])

    class Attended:
        def __init__(self, p):
            def copy(n, owner, block, dev):
                ref = att.at[owner, p] if block is None else att.at[owner, p, block]
                return remote(ref, ref, afs.at[p, n], afr.at[p, n], (r, dev))

            self.first = [copy(0, c, None, sib), copy(1, c, across, across), copy(2, c, diag, diag)]
            self.rest = [copy(3, c, diag, across), copy(4, c, c, across), copy(5, c, sib, across)]
            self.hand = [copy(6, across, c, sib), copy(7, across, across, sib), copy(8, across, diag, sib)]

    attended = [Attended(p) for p in range(2)]

    in_tok.wait()
    g_tok.start()
    for i, v in enumerate((v0, v1, v2, v3, v4, v5, v6, v7)):
        par[i : i + 1, :] = v[...].reshape(1, 768)
    for i in range(4):
        par[8 + i : 9 + i, :] = v8[768 * i : 768 * i + 768].reshape(1, 768)

    ends, lims = [], []
    total = jnp.int32(0)
    for s in range(slides_n):
        total = total + slide_units[s] * PAD
        ends.append(total)
        lims.append(total - shortfall[s])

    def label_of(pos):
        lab = jnp.zeros(pos.shape, jnp.int32)
        for s in range(slides_n - 1):
            lab = lab + jnp.where(pos >= ends[s], 1, 0)
        return lab

    def code_of(pos):
        code = label_of(pos)
        for s in range(slides_n):
            code = jnp.where((pos >= lims[s]) & (pos < ends[s]), -1, code)
        return code

    seg_first = r * 1024

    vec[...] = jnp.zeros(vec.shape, F32)
    for s in range(4):
        for h in range(4):
            wop[s, 64 * h + 48 : 64 * h + 64, :] = jnp.zeros((16, 768), BF16)
    sel_f, sel_j = iota((768, 256), 0), iota((768, 256), 1)
    head_sel = onehot((sel_f == 192 * c + 48 * (sel_j >> 6) + (sel_j & 63)) & ((sel_j & 63) < 48))
    for i, d in enumerate(in_qkv):
        d.wait()
        wqkv[:, 256 * i : 256 * i + 256] = nn(wdn[768 * i : 768 * i + 768, :], head_sel).astype(BF16)
    in_up.start()
    for d in in_wo:
        d.start()
    bqkv[...] = jnp.zeros(bqkv.shape, F32)
    biases = moved(par[0:8, :], head_sel)
    bqkv[0:1, 0:256] = biases[2:3]
    bqkv[0:1, 512:768] = biases[3:4]

    def first_norm(b):
        unit, _ = normalise(tok[b].astype(F32))
        a1[b] = (unit * par[0:1, :] + par[1:2, :]).astype(BF16)

    first_norm(c)
    on_head = (iota((256, 768), 0) & (STRIDE - 1)) == ((iota((256, 768), 1) * 1366) >> 16)

    def dilated(values):
        return jnp.sum(jnp.where(on_head, values.astype(BF16).astype(F32), 0.0).reshape(16, 16, 768), axis=1)

    k_sel = dilated(nn(a1[c], wdn[768:1536, :]))
    v_sel = dilated(nn(a1[c], wdn[1536:2304, :]) + par[3:4, :])
    for s in range(COLS):
        kvo[s] = jnp.concatenate(
            [k_sel[:, 192 * s : 192 * s + 192], v_sel[:, 192 * s : 192 * s + 192]], axis=1
        ).astype(BF16)
    own16 = pl.ds(pl.multiple_of(16 * c, 16), 16)

    def own_dilated(j):
        to = (c + j) % COLS
        return remote(kvo.at[to], kvc.at[r, own16, :], kos.at[j - 1], kor.at[j - 1], (r, to))

    for j in range(1, COLS):
        own_dilated(j).start()
    kvc[r, own16, :] = kvo[c]
    in_cot.wait()
    g_cot.start()
    in_dn.start()
    for d in in_dq:
        d.start()

    def qkv_block(b):
        low = a1[b]
        y = (nn(low, wqkv[...]) + bqkv[0:1, :]).astype(BF16).astype(F32)
        at = pl.ds(pl.multiple_of(256 * b, 256), 256)
        for i in range(6):
            qf[i, at, :] = y[:, 128 * i : 128 * i + 128]
        lane = iota((256, 128), 1) & 63
        key_code = code_of(seg_first + 256 * b + iota((256, 128), 0))
        key_mark = jnp.where(key_code == lane - 48, 0.0, NEG)
        marked = (lane >= 48) & (lane < 48 + slides_n)
        for p in range(2):
            qrow[p, at, :] = y[:, 128 * p : 128 * p + 128].astype(BF16)
            kaug[p, at, :] = jnp.where(marked, key_mark, y[:, 256 + 128 * p : 384 + 128 * p]).astype(BF16)
            vaug[p, at, :] = jnp.where(
                (lane == 48) | (lane == 49), 1.0, y[:, 512 + 128 * p : 640 + 128 * p]
            ).astype(BF16)
        qt, ktv, vt = y[:, :256].T, y[:, 256:512].T, y[:, 512:].T
        row = iota((128, 256), 0)
        query_label = label_of(seg_first + 256 * b + iota((128, 256), 1))
        mark = jnp.where(query_label == (row & 63) - 48, 1.0, 0.0)
        for h in range(4):
            p, half = h // 2, h % 2
            own = (row >> 6) == half
            full = jnp.where((row & 63) < 48, qt[128 * p : 128 * p + 128], mark)
            qtm[h, b] = jnp.where(own, full, 0.0).astype(BF16)
            hq, hk, hv = (m[64 * h : 64 * h + 64] for m in (qt, ktv, vt))
            kt[h, b] = hk.astype(BF16)
            vta[h, b] = jnp.where(iota((64, 256), 0) == 48, 1.0, hv).astype(BF16)
            sdr[h, b] = jnp.broadcast_to(colsum(hq * hk) * SCALE2, (8, 256))

    def sparse_copy(j):
        return remote(kvc.at[r], kvc.at[r], sps.at[j - 1], spr.at[j - 1], ((r + j) % rows_n, c))

    def each_row(fn):
        def step(j, carry):
            fn(j)
            return carry

        lax.fori_loop(1, rows_n, step, 0)

    qkv_block(c)
    g_tok.near.wait_recv()
    first_norm(sib)
    qkv_block(sib)
    for j in range(1, COLS):
        own_dilated(j).wait_recv()
    each_row(lambda j: sparse_copy(j).start())

    g_tok.forward()
    first_norm(across)
    qkv_block(across)
    g_tok.hand.wait_recv()
    first_norm(diag)
    qkv_block(diag)

    def picked(i, h):
        return qf[i, pl.ds(LOCAL_HEADS * c + h, 64, stride=STRIDE), :]

    def both_picked(i, p):
        lane = iota((64, 128), 1)
        return jnp.concatenate(
            [jnp.where((lane >> 6) == half, picked(i, 2 * p + half), 0.0) for half in range(2)], axis=0
        ).astype(BF16)

    def placing(p, first, transposed=False):
        shape = (256, 128) if transposed else (128, 256)
        wide, narrow = iota(shape, 0 if transposed else 1), iota(shape, 1 if transposed else 0)
        return onehot(((narrow & 63) < 48) & (wide == first + 48 * (2 * p + (narrow >> 6)) + (narrow & 63)))

    for p in range(2):
        qsel[p] = nn(both_picked(p, p), placing(p, 0)).astype(BF16)

    eye = iota((256, 256), 0) == iota((256, 256), 1)

    def weights_out(i):
        return pltpu.make_async_copy(pbuf.at[i % 2], p_h.at[i], psem.at[i % 2])

    def forward_tile(i):
        h, ib = i // 4, i % 4
        p, half = h // 2, h % 2
        slot = i if keep else i % 2
        rhs = qtm[h, ib]
        top = jnp.full((8, 256), NEG * 10, F32)
        for jb in range(4):
            s = nn(kaug[p, 256 * jb : 256 * jb + 256, :], rhs) * SCALE2
            sref[256 * jb : 256 * jb + 256, :] = s
            top = jnp.maximum(top, jnp.max(s.reshape(32, 8, 256), axis=0))
        own = sdr[h, ib]
        top = jnp.max(jnp.maximum(top, own), axis=0, keepdims=True)
        at = pl.ds(pl.multiple_of(256 * ib, 256), 256)
        sref[at, :] = jnp.where(eye, own[0:1], sref[at, :])

        if not keep:

            @pl.when(i >= 2)
            def _():
                weights_out(i).wait()

        for jb in range(4):
            pbuf[slot, 256 * jb : 256 * jb + 256, :] = jnp.exp2(
                sref[256 * jb : 256 * jb + 256, :] - top
            ).astype(BF16)
        if not keep:
            weights_out(i).start()
        values = jnp.concatenate([vta[h, jb] for jb in range(4)], axis=1)
        o = nn(values, pbuf[slot])
        z = o[48:49]
        inverse = 1.0 / z
        line = iota((64, 256), 0)
        o = o * inverse
        o = jnp.where(line == 48, inverse, jnp.where(line == 49, top, jnp.where(line == 50, z, o)))
        dqt[half, ib] = o

    def branch_b(p):
        lane = iota((64, 128), 1)
        s = nt(qsel[p], kvc[:, :, 0:256].reshape(key_count, 256)) * SCALE2
        masked = []
        for half in range(2):
            first = LOCAL_HEADS * c + 2 * p + half
            qpos = seg_first + STRIDE * iota((64, 128), 0)[:, 0:1] + first
            kpos = STRIDE * iota((8, key_count), 1)[0:1] + first
            allowed = (label_of(qpos) == code_of(kpos)) | (qpos == kpos)
            masked.append(jnp.where(allowed, s[64 * half : 64 * half + 64], NEG))
        s = jnp.concatenate(masked, axis=0)
        tops = jnp.max(s, axis=1, keepdims=True)
        e = jnp.exp2(s - tops)
        sums = jnp.sum(e, axis=1, keepdims=True)
        outs = moved(nn(e.astype(BF16), kvc[:, :, 128:384].reshape(key_count, 256)), placing(p, 64, True))
        factors = []
        for half in range(2):
            rows = slice(64 * half, 64 * half + 64)
            top_b, z_b, o_b = tops[rows], sums[rows], outs[rows]
            at = pl.ds(LOCAL_HEADS * c + 2 * p + half, 64, stride=STRIDE)
            old = oa[p, at, :]
            top_a = old[:, 64 * half + 49 : 64 * half + 50]
            z_a = old[:, 64 * half + 50 : 64 * half + 51]
            top = jnp.maximum(top_a, top_b)
            in_a, in_b = jnp.exp2(top_a - top), jnp.exp2(top_b - top)
            inverse = 1.0 / (in_a * z_a + in_b * z_b)
            o = (in_a * z_a * old + in_b * o_b) * inverse
            own = (lane >> 6) == half
            oa[p, at, :] = jnp.where(
                own & ((lane & 63) < 48), o, jnp.where(lane == 64 * half + 48, in_a * inverse, old)
            )
            factors.append(in_b * inverse)
        wb[p] = (e * jnp.concatenate(factors, axis=0)).astype(BF16)

    lane256 = iota((256, 128), 1)
    for p in range(2):
        def fwd(t, carry, p=p):
            forward_tile(8 * p + t)
            return carry

        lax.fori_loop(0, 8, fwd, 0)
        for ib in range(4):
            oa[p, 256 * ib : 256 * ib + 256, :] = jnp.concatenate([dqt[0, ib], dqt[1, ib]], axis=0).T
        if p == 0:
            each_row(lambda j: sparse_copy(j).wait_recv())
        else:
            g_cot.forward()
        branch_b(p)
        for ib in range(4):
            att[c, p, ib] = jnp.where(
                (lane256 & 63) < 48, oa[p, 256 * ib : 256 * ib + 256, :], 0.0
            ).astype(BF16)
        for d in attended[p].first:
            d.start()
    if not keep:
        weights_out(14).wait()
        weights_out(15).wait()
    for a in attended:
        for d in a.rest:
            d.start()

    in_up.wait()
    for n in range(3):
        start = (4 * share * ((256 * n) // share)) // 128 * 128
        stop = -(-(4 * share * ((256 * n + 255) // share + 1)) // 128) * 128
        o = 256 * n + iota((stop - start, 256), 1)
        group = jnp.zeros_like(o)
        for t in range(1, rows_n):
            group = group + jnp.where(o >= share * t, 1, 0)
        unit_sel = onehot(start + iota((stop - start, 256), 0) == 3 * share * group + share * c + o)
        for m in range(3):
            wupq[256 * m : 256 * m + 256, 256 * n : 256 * n + 256] = nn(
                wup[256 * m : 256 * m + 256, start:stop], unit_sel
            ).astype(BF16)
        pieces = [par[8 + t : 9 + t, :] for t in range(4)]
        line = jnp.concatenate(pieces, axis=1)[:, start:stop]
        bupq[0:8, 256 * n : 256 * n + 256] = moved(jnp.broadcast_to(line, (8, stop - start)), unit_sel)

    g_cot.near.wait_recv()
    g_cot.hand.wait_recv()
    vec[5:6, :] = colsum(gb[...].reshape(1024, 768).astype(F32))
    for d in in_wo:
        d.wait()
    for a in attended:
        for d in a.first:
            d.wait_recv()

    def project(b):
        out = tok[b].astype(F32) + par[4:5, :]
        for s in range(4):
            out = out + nn(jnp.concatenate([att[s, 0, b], att[s, 1, b]], axis=1), wop[s])
        return out

    def second_norm(b, values):
        unit, inverse = normalise(values)
        a2[b] = (unit * par[5:6, :] + par[6:7, :]).astype(BF16)
        return unit, inverse

    y1[...] = project(c)
    second_norm(c, y1[...])

    in_dn.wait()
    acc[...] = y1[...] + par[7:8, :]
    da2[...] = jnp.zeros(da2.shape, F32)

    def mlp(i, carry):
        low = a2[c]
        g = gb[c]
        at = pl.ds(pl.multiple_of(768 * i, 768), 768)
        u = nn(low, wup[:, at]) + par[pl.ds(8 + i, 1), :]
        hidden, slope = gelu_parts(u)
        acc[...] += nn(hidden.astype(BF16), wdn[at, :])
        du = (nt(g, wdn[at, :]) * slope).astype(BF16)
        da2[...] += nt(du, wup[:, at])
        return carry

    lax.fori_loop(0, 4, mlp, 0)
    for a in attended:
        for d in a.rest:
            d.wait_recv()
        for d in a.hand:
            d.start()
    wqkv[0:256, :] = acc[...].astype(BF16)
    out_copy = local(wqkv.at[pl.ds(0, 256), :], out_h, 0)
    out_copy.start()
    unit, inverse = normalise(y1[...])
    vec[3:4, :] = colsum(da2[...] * unit)
    vec[4:5, :] = colsum(da2[...])
    dy1 = gb[c].astype(F32) + norm_back(da2[...], unit, inverse, par[5:6, :])
    y1[...] = dy1
    drb[c] = dy1.astype(BF16)
    g_dr.start()

    for a in attended:
        for d in a.hand:
            d.wait_recv()
    for j in range(1, 4):
        b = (c + j) % 4
        second_norm(b, project(b))
    for d in in_dq:
        d.wait()

    def quarter(b, carry):
        u = nn(a2[b], wupq[...]) + bupq[0:1, :]
        hidden, slope = gelu_parts(u)
        at = pl.ds(pl.multiple_of(256 * b, 256), 256)
        wdn[at, :] = hidden.astype(BF16)
        du = (nt(gb[b], wdq[...]) * slope).astype(BF16)
        wdn[pl.ds(pl.multiple_of(1024 + 256 * b, 256), 256), :] = du
        vec[6:7, :] += colsum(du.astype(F32))
        return carry

    lax.fori_loop(0, 4, quarter, 0)

    def slab_at(b, l, h):
        return ((2 * b + l) * his + h) * tall

    def put(n, block, first):
        buf = slabs[n]
        width = block.shape[1]
        at = first
        while at < first + block.shape[0]:
            which, off = at // share, at % share
            size = min(share - off, first + block.shape[0] - at)
            row = slab_at(which % 2, (which // 2) % 2, which // 4) + off
            buf[row : row + size, 0:width] = block[at - first : at - first + size].astype(BF16)
            at += size

    def one(n):
        half = 2 * his * tall
        at = pl.ds(pl.multiple_of((1 - bit) * half, half), half)
        return remote(slabs[n].at[at, :], recv_a[n], u1s.at[n], u1r.at[n], (r + 1 - 2 * bit, c))

    def two(n):
        at = pl.ds(pl.multiple_of(slab_at(bit, 1 - lo, 0), his * tall), his * tall)
        return remote(slabs[n].at[at, :], recv_b[n], u2s.at[n], u2r.at[n], (r + 2 - 4 * lo, c))

    def slab(l, h):
        return pl.ds(pl.multiple_of(slab_at(bit, l, h), tall), tall)

    def three(n, j):
        to = (hi + j) % his
        return remote(
            slabs[n].at[slab(lo, to), :], recv_c[n].at[j - 1], u3s.at[n, j - 1], u3r.at[n, j - 1],
            (4 * to + 2 * lo + bit, c),
        )

    def each_hi(fn):
        def step(j, carry):
            fn(j)
            return carry

        lax.fori_loop(1, his, step, 0)

    def start_two(n):
        one(n).wait_recv()

        def add(i, carry):
            for l in range(2):
                at = pl.ds(pl.multiple_of((l * his + i) * tall, tall), tall)
                slabs[n][slab(l, i), :] = (slabs[n][slab(l, i), :].astype(F32) + recv_a[n][at, :].astype(F32)).astype(BF16)
            return carry

        lax.fori_loop(0, his, add, 0)
        two(n).start()

    def start_three(n):
        two(n).wait_recv()

        def add(i, carry):
            at = pl.ds(pl.multiple_of(i * tall, tall), tall)
            slabs[n][slab(lo, i), :] = (slabs[n][slab(lo, i), :].astype(F32) + recv_b[n][at, :].astype(F32)).astype(BF16)
            return carry

        lax.fori_loop(0, his, add, 0)
        each_hi(lambda j: three(n, j).start())

    def slab_sent(n):
        one(n).wait_send()
        two(n).wait_send()
        each_hi(lambda j: three(n, j).wait_send())

    def col_copy(n, j):
        at = pl.ds(OFFSETS[n], UNITS[n])
        return remote(gath.at[c, :, at], gath.at[c, :, at], ucs.at[n, j - 1], ucr.at[n, j - 1], (r, (c + j) % COLS))

    def finish(n):
        each_hi(lambda j: three(n, j).wait_recv())
        gath[c, :, OFFSETS[n] : OFFSETS[n] + UNITS[n]] = (
            lax.fori_loop(
                0, his - 1, lambda j, t: t + recv_c[n][j].astype(F32), slabs[n][slab(lo, hi), :].astype(F32)
            )
        ).astype(BF16)
        for j in range(1, COLS):
            col_copy(n, j).start()

    for m in range(2):
        put(DOWN, tn(wdn[0:1024, 384 * m : 384 * m + 384], gb[...].reshape(1024, 768)), 384 * m)
    one(DOWN).start()
    g_dr.forward()
    for m in range(2):
        lanes = jnp.concatenate([a2[b, :, 384 * m : 384 * m + 384] for b in range(4)], axis=0)
        block = tn(lanes, wdn[1024:2048, :])
        put(UP, block[:, 0:512], 384 * m)
        put(UP_LAST, block[:, 512:768], 384 * m)

    g_dr.near.wait_recv()
    g_dr.hand.wait_recv()
    vec[2:3, :] = colsum(drb[...].reshape(1024, 768).astype(F32))
    bones = onehot((iota((256, 256), 0) >> 6) == (iota((256, 256), 1) >> 6))

    def out_grad(b, carry):
        lane = iota((256, 256), 1) & 63
        at = pl.ds(pl.multiple_of(256 * b, 256), 256)
        d_att = nt(drb[b], wop[c]).astype(BF16).astype(F32)
        mine = jnp.concatenate([att[c, 0, b], att[c, 1, b]], axis=1).astype(F32)
        rowsum = moved(d_att * mine, bones, 2)
        factor = moved(
            jnp.where(lane == 48, jnp.concatenate([oa[0, at, :], oa[1, at, :]], axis=1), 0.0), bones
        )
        minus = -rowsum * factor
        high = minus.astype(BF16).astype(F32)
        marked = jnp.where(lane == 48, high, jnp.where(lane == 49, minus - high, d_att * factor))
        flipped = marked.T
        line = iota((128, 256), 0)
        for p in range(2):
            kaug[p, at, :] = marked[:, 128 * p : 128 * p + 128].astype(BF16)
            qf[p, at, :] = d_att[:, 128 * p : 128 * p + 128]
            qf[2 + p, at, :] = rowsum[:, 128 * p : 128 * p + 128]
        for h in range(4):
            p = h // 2
            qtm[h, b] = jnp.where(
                (line >> 6) == h % 2, flipped[128 * p : 128 * p + 128], 0.0
            ).astype(BF16)
        return carry

    lax.fori_loop(0, 4, out_grad, 0)

    own_cols = onehot(
        (iota((256, 768), 1) == 192 * c + iota((256, 768), 0)) & (iota((256, 768), 0) < 192)
    )
    dr_own = jnp.concatenate([nt(own_cols, drb[b]).astype(BF16) for b in range(4)], axis=1)
    for s in range(4):
        both = jnp.concatenate(
            [att[s, 0].reshape(1024, 128), att[s, 1].reshape(1024, 128)], axis=1
        )
        block = nn(dr_own, both).T
        for h in range(4):
            put(OUT, block[64 * h : 64 * h + 48], 192 * s + 48 * h)

    step_rows = min(rows_n, 8)
    step_keys = 64 * step_rows

    def dilated_block(t):
        tall, wide = pl.multiple_of(64 * (t // 8), 64), pl.multiple_of(384 * (t % 8), 384)
        return wup.at[pl.ds(tall, 64), pl.ds(wide, 384)]

    d_sel, sums = [], []
    for p in range(2):
        d_sel.append(nn(both_picked(p, p), placing(p, 64)).astype(BF16))
        sums.append(
            jnp.concatenate([picked(2 + p, 2 * p + i)[:, 64 * i : 64 * i + 1] for i in range(2)], axis=0)
        )
    dqb[...] = jnp.zeros(dqb.shape, F32)

    def some_keys(n, carry):
        some = pl.ds(pl.multiple_of(step_rows * n, step_rows), step_rows)
        k2 = kvc[some, :, 0:256].reshape(step_keys, 256)
        v2 = kvc[some, :, 128:384].reshape(step_keys, 256)
        dk, dv = 0.0, 0.0
        for p in range(2):
            w = wb[p, :, pl.ds(pl.multiple_of(step_keys * n, step_keys), step_keys)]
            ds = (w.astype(F32) * (nt(d_sel[p], v2) - sums[p])).astype(BF16)
            dqb[p] += nn(ds, k2)
            dk = dk + tn(ds, qsel[p])
            dv = dv + tn(w, d_sel[p])
        for t in range(step_rows):
            block = dilated_block(step_rows * n + t)
            rows = slice(64 * t, 64 * t + 64)
            block[:, 0:128] = dk[rows, 0:128].astype(BF16)
            block[:, 128:256] = (dk[rows, 128:256] + dv[rows, 0:128]).astype(BF16)
            block[:, 256:384] = dv[rows, 128:256].astype(BF16)
        return carry

    lax.fori_loop(0, rows_n // step_rows, some_keys, 0)

    def dilated_copy(j):
        to = (r + j) % rows_n
        return remote(dilated_block(to), dkvr.at[j - 1], bss.at[j - 1], bsr.at[j - 1], (to, c))

    each_row(lambda j: dilated_copy(j).start())

    qf[...] = jnp.zeros(qf.shape, F32)

    def weights_in(i):
        return pltpu.make_async_copy(p_h.at[i], pbuf.at[i % 2], psem.at[i % 2])

    def backward_tile(i):
        h, ib = i // 4, i % 4
        p, half = h // 2, h % 2
        slot = i if keep else i % 2
        if not keep:
            weights_in(i).wait()

            @pl.when(i + 1 < 16)
            def _():
                weights_in(i + 1).start()

        rhs = qtm[h, ib]
        for jb in range(4):
            at = slice(256 * jb, 256 * jb + 256)
            dsb[at, :] = (pbuf[slot, at, :].astype(F32) * nn(vaug[p, at, :], rhs)).astype(BF16)
        keys = jnp.concatenate([kt[h, jb] for jb in range(4)], axis=1)
        dqt[h, ib] = nn(keys, dsb[...])
        at = pl.ds(pl.multiple_of(256 * ib, 256), 256)
        own = (iota((256, 128), 1) >> 6) == half
        d_rows, q_rows = kaug[p, at, :], qrow[p, at, :]
        for jb in range(4):
            js = slice(256 * jb, 256 * jb + 256)
            qf[2 + p, js, :] += jnp.where(own, nn(dsb[js, :], q_rows), 0.0)
            qf[4 + p, js, :] += jnp.where(own, nn(pbuf[slot, js, :], d_rows), 0.0)

    if not keep:
        weights_in(0).start()
    for first, last in ((0, 11), (11, 16)):
        def bwd(t, carry):
            backward_tile(t)
            return carry

        lax.fori_loop(first, last, bwd, 0)
        if first:
            start_three(DOWN)
        if first == 0:
            start_two(DOWN)
            one(UP).start()
            one(OUT).start()

    each_row(lambda j: dilated_copy(j).wait_recv())
    spread = lax.fori_loop(
        0, rows_n - 1, lambda j, t: t + dkvr[j].astype(F32), dilated_block(r)[...].astype(F32)
    )
    each_row(lambda j: dilated_copy(j).wait_send())
    back_qkv = [local(h, wup.at[:, pl.ds(768 * i, 768)], 2 + i) for i, h in enumerate((wq_h, wk_h, wv_h))]
    for d in back_qkv:
        d.start()
    source, slot = iota((384, 512), 0), iota((384, 512), 1)
    spread = moved(
        spread,
        onehot(((slot & 63) < 48) & (source == 192 * (slot >> 8) + 48 * ((slot & 255) >> 6) + (slot & 63))),
        2,
    )
    dq_b = [moved(dqb[p], placing(p, 0, True), 2) for p in range(2)]
    for h in range(4):
        p, rows = h // 2, slice(64 * (h % 2), 64 * (h % 2) + 64)
        own = (iota((64, 128), 1) >> 6) == h % 2
        at = pl.ds(LOCAL_HEADS * c + h, 64, stride=STRIDE)
        qf[p, at, :] += jnp.where(own, dq_b[p][rows], 0.0)
        qf[2 + p, at, :] += jnp.where(own, spread[:, 128 * p : 128 * p + 128], 0.0)
        qf[4 + p, at, :] += jnp.where(own, spread[:, 256 + 128 * p : 384 + 128 * p], 0.0)

    def turned(i, b):
        at = pl.ds(pl.multiple_of(256 * b, 256), 256)
        return jnp.concatenate([qf[2 * i, at, :], qf[2 * i + 1, at, :]], axis=1).T

    def compact(b, carry):
        dq = (jnp.concatenate([dqt[h, b] for h in range(4)], axis=0) + turned(0, b)) * SCALE
        for i, m in enumerate((dq, turned(1, b) * SCALE, turned(2, b))):
            for h in range(4):
                a2[b, 48 * h : 48 * h + 48, 256 * i : 256 * i + 256] = m[64 * h : 64 * h + 48].astype(BF16)
        return carry

    lax.fori_loop(0, 4, compact, 0)

    def exchange(j):
        to = (c + j) % COLS
        at = pl.ds(pl.multiple_of(192 * c, 64), 192)
        return remote(a2.at[to, pl.ds(0, 192), :], dqr.at[at, :], ats.at[j - 1], atr.at[j - 1], (r, to))

    for j in range(1, COLS):
        exchange(j).start()
    dqr[pl.ds(pl.multiple_of(192 * c, 64), 192), :] = a2[c, 0:192, :]
    rows576 = [
        jnp.concatenate(
            [a2[b, 0:192, 256 * i : 256 * i + 256] for i in range(3)] + [jnp.zeros((64, 256), BF16)], axis=0
        )
        for b in range(4)
    ]
    lhs = jnp.concatenate(rows576, axis=1)
    def own_grads(n, first):
        for m in range(2):
            lanes = jnp.concatenate([a1[b, :, 384 * m : 384 * m + 384] for b in range(4)], axis=0)
            put(n, nn(lhs[first : first + UNITS[n]], lanes).T, 384 * m)

    own_grads(QK, 0)
    one(QK).start()
    own_grads(VAL, UNITS[QK])
    ones = jnp.ones((16, 1024), BF16)
    vec[7:8, 0:640] = nt(ones, lhs)[0:1]
    start_two(UP)
    start_two(OUT)
    one(UP_LAST).start()
    finish(DOWN)
    start_three(UP)
    start_two(QK)
    one(VAL).start()
    start_two(UP_LAST)

    for d in back_qkv:
        d.wait()
    for j in range(1, COLS):
        exchange(j).wait_recv()
    da1 = nn(wup[:, 0:768], dqr[:, 0:256])
    for i in range(1, 3):
        da1 = da1 + nn(wup[:, 768 * i : 768 * i + 768], dqr[:, 256 * i : 256 * i + 256])
    da1 = da1.T
    unit, inverse = normalise(tok[c].astype(F32))
    vec[0:1, :] = colsum(da1 * unit)
    vec[1:2, :] = colsum(da1)
    vec_one = remote(vec, vin.at[0], vss.at[0], vsr.at[0], (r + 1 - 2 * bit, c))
    vec_one.start()
    da2[...] = y1[...] + norm_back(da1, unit, inverse, par[0:1, :])
    gt_copy = local(da2, gt_h, 1)
    gt_copy.start()
    start_three(OUT)
    start_three(UP_LAST)
    start_two(VAL)
    start_three(QK)
    vec_one.wait_recv()
    vcol[c] = vec[...] + vin[0]
    vec_two = remote(vcol.at[c], vin.at[1], vss.at[1], vsr.at[1], (r + 2 - 4 * lo, c))
    vec_two.start()
    finish(UP)
    finish(OUT)
    vec_two.wait_recv()
    vrow[hi] = vcol[c] + vin[1]

    def vec_three(j):
        to = (hi + j) % his
        return remote(vrow.at[hi], vrow.at[hi], vss.at[1 + j], vsr.at[1 + j], (4 * to + 2 * lo + bit, c))

    each_hi(lambda j: vec_three(j).start())
    finish(UP_LAST)
    start_three(VAL)
    each_hi(lambda j: vec_three(j).wait_recv())
    vec_two.wait_send()
    vcol[c] = lax.fori_loop(0, his, lambda j, t: t + vrow[j], jnp.zeros((16, 768), F32))

    def vec_col(j):
        return remote(vcol.at[c], vcol.at[c], vcs.at[j - 1], vcr.at[j - 1], (r, (c + j) % COLS))

    for j in range(1, COLS):
        vec_col(j).start()
    finish(QK)
    finish(VAL)
    for j in range(1, COLS):
        vec_col(j).wait_recv()
        for n in range(6):
            col_copy(n, j).wait_recv()
    out_gath = local(gath, gath_h, 2)
    out_vec = local(vcol, vec_h, 3)
    out_gath.start()
    out_vec.start()

    for g in (g_tok, g_cot, g_dr):
        g.drain()
    for a in attended:
        for d in (*a.first, *a.rest, *a.hand):
            d.wait_send()
    each_row(lambda j: sparse_copy(j).wait_send())
    vec_one.wait_send()
    each_hi(lambda j: vec_three(j).wait_send())
    for n in range(6):
        slab_sent(n)
        for j in range(1, COLS):
            col_copy(n, j).wait_send()
    for j in range(1, COLS):
        exchange(j).wait_send()
        own_dilated(j).wait_send()
        vec_col(j).wait_send()
    out_copy.wait()
    gt_copy.wait()
    out_gath.wait()
    out_vec.wait()


def finale(
    rows_n, gath_h, vec_h, out_h, gt_h, out, gt, g1, b1, gq, bq, gk, gv, bv, go, bo, g2, b2, gu, bu, gd, bd,
    gath, vec, sems,
):
    copies = [
        pltpu.make_async_copy(src, dst, sems.at[i])
        for i, (src, dst) in enumerate(((gath_h, gath), (vec_h, vec), (out_h, out), (gt_h, gt)))
    ]
    for d in copies:
        d.start()
    share = 768 // rows_n
    r = lax.axis_index("row")
    copies[0].wait()
    part = [gath[s].astype(F32)[:share] for s in range(COLS)]

    def across(off, width):
        return jnp.concatenate([part[s][:, off : off + width] for s in range(COLS)], axis=1)

    gq[...] = across(1792, 192)
    gk[...] = across(1792 + 192, 192)
    gv[...] = across(1792 + 384, 192)
    go[...] = across(1536, 192)
    gu[...] = jnp.concatenate(
        [part[s][:, 768 + share * t : 768 + share * t + share] for t in range(rows_n) for s in range(COLS)], axis=1
    )
    for s in range(COLS):
        gd[share * s : share * s + share, :] = part[s][:, 0:768]
    copies[1].wait()
    summed = vec[0] + vec[1] + vec[2] + vec[3]
    wide = max(128, -(-share // 128) * 128)
    f, j = iota((768, wide), 0), iota((768, wide), 1)
    pick = onehot((f == share * r + j) & (j < share))
    mine = vec[0]
    total = moved(jnp.concatenate([summed[0:8], mine[0:8]], axis=0), pick)
    hidden = [moved(vec[s][0:8], pick) for s in range(COLS)]
    qv = [None, None]
    for n, off in enumerate((0, 384)):
        for s in range(COLS):
            place = onehot((f + 192 * s - off == share * r + j) & (j < share) & (f >= off) & (f < off + 192))
            term = moved(vec[s][0:8], place)
            qv[n] = term if qv[n] is None else qv[n] + term
    g1[...] = total[0, :share]
    b1[...] = total[1, :share]
    bo[...] = total[8 + 2, :share]
    g2[...] = total[3, :share]
    b2[...] = total[4, :share]
    bd[...] = total[8 + 5, :share]
    bq[...] = qv[0][7, :share]
    bv[...] = qv[1][7, :share]
    bu[...] = jnp.concatenate([hidden[s][6:7, :share] for s in range(COLS)], axis=1)[0]
    copies[2].wait()
    copies[3].wait()


def body(rows_n, tokens, norm1_gain, norm1_bias, w_query, b_query, w_key, w_value, b_value, w_out, b_out,
         norm2_gain, norm2_bias, w_up, b_up, w_down, b_down, slide_padded_units, padding_shortfall, cotangent):
    his, share = rows_n // 4, 768 // rows_n
    padded = -(-share // 16) * 16
    c = lax.axis_index("col")
    down_q = w_down
    if share % 16:
        down_q = lax.dynamic_index_in_dim(w_down.reshape(rows_n, COLS, share, 768), c, 1, False).reshape(768, 768)
    vmem = pltpu.VMEM
    dma = pltpu.SemaphoreType.DMA
    between = max(his - 1, 1)
    keep = rows_n <= 8
    scratch = [
        vmem((768, 3072), BF16), vmem((3072, 768), BF16), vmem((768, 768), BF16), vmem((768, 768), BF16),
        vmem((768, 768), BF16), vmem((4, 256, 768), BF16),
        *[vmem((4, 256, 768), BF16) for _ in range(5)],
        vmem((6, 1040, 128), F32), vmem((2, 1024, 128), BF16), vmem((2, 1024, 128), BF16),
        vmem((2, 1024, 128), BF16), vmem((4, 4, 128, 256), BF16), vmem((4, 4, 64, 256), BF16),
        vmem((4, 4, 64, 256), BF16), vmem((4, 4, 8, 256), F32),
        vmem((16 if keep else 2, 1024, 256), BF16), vmem((1024, 256), F32), vmem((1024, 256), BF16),
        vmem((2, 1040, 128), F32), vmem((4, 2, 4, 256, 128), BF16),
        vmem((256, 768), F32), vmem((256, 768), F32), vmem((256, 768), F32),
        vmem((4, 4, 64, 256), F32), vmem((768, 768), BF16),
        *[vmem((rows_n * padded, w), BF16) for w in UNITS[:QK]],
        *[vmem((2 * his * padded, w), BF16) for w in UNITS],
        *[vmem((his * padded, w), BF16) for w in UNITS],
        *[vmem((between, padded, w), BF16) for w in UNITS],
        vmem((4, padded, WIDTH), BF16),
        vmem((4, 16, 384), BF16), vmem((rows_n, 64, 384), BF16), vmem((2, 128, 256), BF16),
        vmem((2, 128, rows_n * 64), BF16), vmem((2, 128, 256), F32), vmem((rows_n - 1, 64, 384), BF16),
        vmem((16, 768), F32), vmem((16, 768), F32), vmem((2, 16, 768), F32), vmem((his, 16, 768), F32),
        vmem((4, 16, 768), F32), vmem((8, 768), F32), vmem((8, 768), F32),
        dma((24 + rows_n,)), dma((3, 3)), dma((3, 3)), dma((2, 9)), dma((2, 9)), dma((3,)), dma((3,)),
        dma((rows_n - 1,)), dma((rows_n - 1,)), dma((rows_n - 1,)), dma((rows_n - 1,)),
        dma((6,)), dma((6,)), dma((6,)), dma((6,)), dma((6, between)), dma((6, between)), dma((6, 3)), dma((6, 3)),
        dma((3,)), dma((3,)), dma((his + 1,)), dma((his + 1,)), dma((3,)), dma((3,)), dma((2,)),
    ]
    hbm = pl.BlockSpec(memory_space=pl.ANY)
    smem = pl.BlockSpec(memory_space=pltpu.SMEM)
    whole = pl.BlockSpec(memory_space=pltpu.VMEM)
    sds = jax.ShapeDtypeStruct
    out, gt, gath, vec, _ = pl.pallas_call(
        functools.partial(layer, rows_n, slide_padded_units.shape[0], keep),
        out_shape=(
            sds((256, 768), BF16), sds((256, 768), F32), sds((4, padded, WIDTH), BF16), sds((4, 16, 768), F32),
            sds((8, 128) if keep else (16, 1024, 256), BF16),
        ),
        in_specs=[smem, smem] + [whole] * 9 + [hbm] * 9,
        out_specs=(hbm,) * 5,
        scratch_shapes=scratch,
        compiler_params=pltpu.CompilerParams(
            collective_id=0, has_side_effects=True, vmem_limit_bytes=(992 if rows_n <= 8 else 1021) * 64 * 1024
        ),
        name="layer",
    )(slide_padded_units, padding_shortfall, norm1_gain, norm1_bias, b_query, b_value, b_out, norm2_gain, norm2_bias,
      b_down, b_up, tokens, cotangent, w_query, w_key, w_value, w_out, w_up, w_down,
      down_q)
    vec1 = sds((share,), F32)
    mat = sds((share, 768), F32)
    return pl.pallas_call(
        functools.partial(finale, rows_n),
        out_shape=(
            sds((256, 768), BF16), sds((256, 768), F32), vec1, vec1, mat, vec1, mat, mat, vec1, mat, vec1, vec1, vec1,
            sds((share, 3072), F32), sds((4 * share,), F32), sds((4 * share, 768), F32), vec1,
        ),
        in_specs=[pl.BlockSpec(memory_space=pltpu.HBM)] * 4,
        out_specs=(whole,) * 17,
        scratch_shapes=[vmem((4, padded, WIDTH), BF16), vmem((4, 16, 768), F32), dma((4,))],
        compiler_params=pltpu.CompilerParams(vmem_limit_bytes=1016 * 64 * 1024),
        name="finale",
    )(gath, vec, out, gt)


def solution(mesh):
    tiles = P(("row", "col"), None)
    one, two = P("row"), P("row", None)
    return jax.shard_map(
        functools.partial(body, mesh.shape["row"]),
        mesh=mesh,
        in_specs=(tiles,) + (P(),) * 17 + (tiles,),
        out_specs=(tiles, tiles, one, one, two, one, two, two, one, two, one, one, one, two, one, two, one),
        check_vma=False,
    )
```
